32 devices in a mesh: section: 8 (over z, x), tensor: 4 (over y, core).
Axes of the slice: x: 2, y: 2, z: 4, core: 2. Of those that a mesh axis runs over, the one named last changes fastest.
Arguments:
- trainer_tiles: bfloat16 [49152, 6144], P(('section', 'tensor')), may hold values from -0.09375 to 0.09375
- tile_lengths: int32 [32], replicated, may hold values from 1 to 24, 512 in all
- wo_rollout: bfloat16 [8, 4096, 4096], P('section', 'tensor'), may hold values from -0.1875 to 0.1875
- cache_keys: bfloat16 [8, 32, 64, 1024], P('section', None, None, 'tensor')
- cache_values: bfloat16 [8, 32, 64, 1024], P('section', None, None, 'tensor'), may hold values from -6 to 6
- cache_lengths: int32 [32], replicated, may hold values from 1 to 64, as said below
- norm_gain: float32 [8, 4096], P('section'), may hold values from 0.1 to 1.9
- step_inputs: bfloat16 [3, 32, 4096], replicated, may hold values from -3 to 3
Outputs:
- hidden: float32 [8, 3, 32, 4096], P('section', None, None, 'tensor')
The draws below stay inside these ranges and needn't reach their ends.
Inputs may be any that keep to these rules, and one draw needn't show every extreme that they name: `tile_lengths`: the lengths of all tiles sum to 512; some tile holds exactly 24 blocks. `cache_lengths`: some sequence uses all 64 positions.
All inputs are finite; a program needn't handle non-finite values.
Results may differ from the reference program's by a relative error of at most 0.03.
Values may be sent and summed in bfloat16 or wider, within the bound.
No kernel may reach another device: no remote copies, remote signals or barrier semaphores. Data moves between devices by JAX's collectives and lax.ppermute only.
A program may use at most 192 MiB of HBM per device.

```python
import math
import jax
import jax.numpy as jnp
import numpy as np
from jax import lax

D = 4096
HEADS = 32
KV_HEADS = 8
HDIM = 128
FB = 8
STEPS = 3
ROWS = 32
CACHE = 64
CAP = 24
QKVC = 6144
N_SECTION = 8
N_TENSOR = 4
DEVICES = 32


def draw_cache_keys(key, part):
    key = jax.random.fold_in(key, 7)
    shape = (N_SECTION, ROWS, CACHE, KV_HEADS * HDIM)
    return jnp.clip(jax.random.normal(key, shape, jnp.float32), -6.0, 6.0).astype(jnp.bfloat16)


def draw_cache_lengths(key, part):
    key = jax.random.fold_in(key, 11)
    spans = jax.random.randint(key, (ROWS,), 1, CACHE + 1)
    chosen = jax.random.randint(jax.random.fold_in(key, 1), (), 0, ROWS)
    return jnp.where(jnp.arange(ROWS) == chosen, CACHE, spans).astype(jnp.int32)


def block_scale(rng, extent, pieces, smallest, largest):
    loudness = 1.0
    for axis_at, parts in pieces:
        heights = jax.random.uniform(jax.random.fold_in(jax.random.fold_in(rng, 6), axis_at), (parts,), jnp.float32, smallest / len(pieces), largest / len(pieces))
        loudness = loudness * jnp.repeat(jnp.exp(heights), extent[axis_at] // parts).reshape((-1,) + (1,) * (len(extent) - 1 - axis_at))
    return loudness


def split_up(count, total, most, skew):
    loads = [(1 << 20) // math.isqrt(grade ** skew) + 1 for grade in range(2, count + 1)]
    rest, counts = total - most - (count - 1), [1] * (count - 1)
    while rest > 0:
        candidates = [i for i in range(count - 1) if counts[i] < most]
        mass, remaining = sum([loads[i] for i in candidates]), rest
        for i in candidates:
            extra = min(most - counts[i], max(1, remaining * loads[i] // mass), rest)
            counts[i] = counts[i] + extra
            rest = rest - extra
    return np.array([most] + counts)


def uneven_parts(key, amount, total, limit, skew):
    if amount == 2:
        one = jax.random.randint(key, (), max(1, total - limit), min(limit, total - 1) + 1)
        return jnp.stack([one, total - one])
    tallies = jnp.asarray(split_up(amount, total, limit, skew), jnp.int32)
    pairs = (amount - 1) // 2
    donor, taker = tallies[1:1 + 2 * pairs:2], tallies[2:2 + 2 * pairs:2]
    slack = jnp.minimum(donor - 1, limit - taker)
    shifted = jax.random.randint(jax.random.fold_in(key, 1), (pairs,), 0, 1 << 20) % (slack + 1)
    tallies = tallies.at[1:1 + 2 * pairs:2].set(donor - shifted).at[2:2 + 2 * pairs:2].set(taker + shifted)
    return tallies[jax.random.permutation(jax.random.fold_in(key, 2), amount)]


def bell_draw(own_key, shape, width, limit, cuts=(), kind=jnp.bfloat16):
    drawn = width * jax.random.normal(own_key, shape, jnp.float32)
    if cuts:
        drawn = drawn * block_scale(own_key, shape, cuts, -0.22, 0.18)
    return jnp.clip(drawn, -limit, limit).astype(kind)


def setup_inputs(seed: int = 0) -> dict:
    streams_of = jax.random.split(jax.random.key(seed), 9)
    return {
        "trainer_tiles": bell_draw(streams_of[0], (DEVICES * CAP * FB * N_SECTION, QKVC), D ** -0.5, 0.09375, ((0, 32),)),
        "tile_lengths": uneven_parts(streams_of[1], DEVICES, D // FB, CAP, 1).astype(jnp.int32),
        "wo_rollout": bell_draw(streams_of[2], (N_SECTION, HEADS * HDIM, D), (HEADS * HDIM // 4) ** -0.5, 0.1875, ((0, 8), (1, 4))),
        "cache_keys": draw_cache_keys(jax.random.fold_in(streams_of[8], 71), 0),
        "cache_values": bell_draw(streams_of[4], (N_SECTION, ROWS, CACHE, KV_HEADS * HDIM), 1.0, 6.0, ((0, 8), (3, 4))),
        "cache_lengths": draw_cache_lengths(jax.random.fold_in(streams_of[8], 71), 0),
        "norm_gain": jnp.clip(1.0 + 0.18 * jax.random.normal(streams_of[6], (N_SECTION, D), jnp.float32), 0.1, 1.9),
        "step_inputs": bell_draw(streams_of[7], (STEPS, ROWS, D), 0.5, 3.0),
    }


def block_owner(tile_lengths):
    ends = jnp.cumsum(tile_lengths).astype(jnp.int32)
    starts = ends - tile_lengths
    blocks = jnp.arange(D // FB, dtype=jnp.int32)
    owner = lax.optimization_barrier(jnp.sum((ends[None, :] <= blocks[:, None]).astype(jnp.int32), axis=1)).astype(jnp.int32)
    inner = (blocks - starts[owner]).astype(jnp.int32)
    return (owner, inner)

def reference(trainer_tiles, tile_lengths, wo_rollout, cache_keys, cache_values, cache_lengths, norm_gain, step_inputs):
    owner, inner = block_owner(tile_lengths)
    feats = jnp.arange(D, dtype=jnp.int32)
    picks = ((owner[feats // FB] * CAP + inner[feats // FB]) * FB + feats % FB).astype(jnp.int32)
    tiles = trainer_tiles.reshape(DEVICES * CAP * FB, N_SECTION, QKVC)
    hpd = HEADS // N_TENSOR
    kpd = KV_HEADS // N_TENSOR
    cdev = QKVC // N_TENSOR
    groups = HEADS // KV_HEADS
    scale = 1.0 / HDIM ** 0.5
    cmask = (jnp.arange(CACHE)[None, :] < cache_lengths[:, None])[None, :, None, None, :]
    nmask = (jnp.arange(STEPS)[None, :] <= jnp.arange(STEPS)[:, None])[:, None, None, None, :]

    def layer(state, xs):
        index, wo, keys, values, gain = xs
        weights = lax.dynamic_index_in_dim(tiles, index, 1, keepdims=False)[picks]
        states = state.astype(jnp.float32)
        normed = (states * lax.rsqrt(lax.optimization_barrier(jnp.mean(states * states, axis=-1, keepdims=True)) + 1e-06) * gain).astype(jnp.bfloat16)
        qkv = jnp.dot(normed.reshape(STEPS * ROWS, D), weights, preferred_element_type=jnp.float32).astype(jnp.bfloat16)
        qkv = qkv.reshape(STEPS, ROWS, N_TENSOR, cdev)
        query = qkv[..., :hpd * HDIM].reshape(STEPS, ROWS, KV_HEADS, groups, HDIM).astype(jnp.float32)
        knew = qkv[..., hpd * HDIM:(hpd + kpd) * HDIM].reshape(STEPS, ROWS, KV_HEADS, HDIM).astype(jnp.float32)
        vnew = qkv[..., (hpd + kpd) * HDIM:].reshape(STEPS, ROWS, KV_HEADS, HDIM).astype(jnp.float32)
        ckeys = keys.reshape(ROWS, CACHE, KV_HEADS, HDIM).astype(jnp.float32)
        cvals = values.reshape(ROWS, CACHE, KV_HEADS, HDIM).astype(jnp.float32)
        scache = jnp.einsum('srkgd,rlkd->srkgl', query, ckeys) * scale
        snew = jnp.einsum('srkgd,trkd->srkgt', query, knew) * scale
        scache = jnp.where(cmask, scache, -1e+30)
        snew = jnp.where(nmask, snew, -1e+30)
        top = jnp.maximum(lax.optimization_barrier(jnp.max(scache, axis=-1)), lax.optimization_barrier(jnp.max(snew, axis=-1)))[..., None]
        ecache = jnp.where(cmask, jnp.exp(scache - top), 0.0)
        enew = jnp.where(nmask, jnp.exp(snew - top), 0.0)
        total = (lax.optimization_barrier(jnp.sum(ecache, axis=-1)) + lax.optimization_barrier(jnp.sum(enew, axis=-1)))[..., None]
        wcache = lax.optimization_barrier((ecache / total).astype(jnp.bfloat16)).astype(jnp.float32)
        wnew = lax.optimization_barrier((enew / total).astype(jnp.bfloat16)).astype(jnp.float32)
        mixed = jnp.einsum('srkgl,rlkd->srkgd', wcache, cvals) + jnp.einsum('srkgt,trkd->srkgd', wnew, vnew)
        attn = lax.optimization_barrier(mixed.astype(jnp.bfloat16)).reshape(STEPS, ROWS, N_TENSOR, hpd * HDIM).astype(jnp.float32)
        wgroups = wo.reshape(N_TENSOR, hpd * HDIM, D).astype(jnp.float32)
        partial_value = jnp.einsum('srtc,tcd->srtd', attn, wgroups).astype(jnp.bfloat16)
        partial_value = lax.optimization_barrier(partial_value).astype(jnp.float32)
        wide = states + lax.optimization_barrier(jnp.sum(partial_value, axis=2))
        after = wide.astype(jnp.bfloat16)
        return (after, wide)
    layers = jnp.arange(N_SECTION, dtype=jnp.int32)
    final, hidden = lax.scan(layer, step_inputs, (layers, wo_rollout, cache_keys, cache_values, norm_gain))
    return hidden
```

```python
import jax
import jax.numpy as jnp
from jax import lax
from jax.sharding import PartitionSpec as P

HDIM = 128
FB = 8


def from_behind(value, axis, steps):
    count = lax.axis_size(axis)
    leading, last = (max(0, -steps), min(count, count - steps))
    return lax.ppermute(value, axis, [(source, source + steps) for source in range(leading, last)])


def per_device(
    trainer_tiles,
    tile_lengths,
    wo_rollout,
    cache_keys,
    cache_values,
    cache_lengths,
    norm_gain,
    step_inputs,
):
    n_section = lax.axis_size("section")
    n_tensor = lax.axis_size("tensor")
    devices = n_section * n_tensor
    cdev = trainer_tiles.shape[1] // n_tensor
    slab = trainer_tiles.shape[0] // n_section
    slots = slab // FB
    width = wo_rollout.shape[2]
    qdim = wo_rollout.shape[1]
    kvdim = cache_keys.shape[3]
    kvlocal = kvdim // HDIM
    groups = qdim // HDIM // kvlocal
    ends = jnp.cumsum(tile_lengths)
    starts = ends - tile_lengths
    blocks = jnp.arange(width // FB, dtype=jnp.int32)
    owner = jnp.sum((ends[None, :] <= blocks[:, None]).astype(jnp.int32), axis=1)
    inner = blocks - starts[owner]
    feats = jnp.arange(width, dtype=jnp.int32)
    owner_f = owner[feats // FB]
    inner_f = inner[feats // FB]
    outgoing = trainer_tiles.reshape(slab, devices, cdev)
    arrived = lax.all_to_all(
        outgoing, ("section", "tensor"), split_axis=1, concat_axis=0, tiled=True
    )
    picks = (owner_f * slots + inner_f) * FB + feats % FB
    weights = arrived.reshape(-1, cdev)[picks]
    section = lax.axis_index("section")
    tpos = lax.axis_index("tensor")
    steps = step_inputs.shape[0]
    seqs = cache_keys.shape[1]
    length = cache_keys.shape[2]
    nblock = 4
    brow = seqs // nblock
    rows = steps * brow
    ticks = nblock + n_section - 1
    shard = width // n_tensor
    scale = 1.0 / HDIM**0.5
    wo_local = wo_rollout[0]
    keys_local = cache_keys[0]
    values_local = cache_values[0]
    gain = norm_gain[0]
    nmask = (jnp.arange(steps)[None, :] <= jnp.arange(steps)[:, None])[:, None, None, None, :]
    along_core = [(t, t ^ 1) for t in range(n_tensor)]
    record = jnp.zeros((steps, seqs, shard), jnp.float32)
    current = jnp.zeros((rows, shard), jnp.bfloat16)

    for tick in range(ticks):
        item = tick - section
        valid = (item >= 0) & (item < nblock)
        first = jnp.clip(item, 0, nblock - 1) * brow
        fresh = lax.dynamic_slice(step_inputs, (0, first, 0), (steps, brow, width)).reshape(rows, width)
        if tick:
            halves = jnp.stack([current, lax.ppermute(current, "tensor", along_core)])
            even = jnp.where(tpos % 2 == 0, halves[0], halves[1])
            odd = jnp.where(tpos % 2 == 0, halves[1], halves[0])
            pair = jnp.concatenate([even, odd], axis=1)
            chips = n_tensor // 2
            gathered = [None] * chips
            parts = [pair]
            for hop in range(1, chips):
                moved = lax.ppermute(
                    pair, "tensor", [(t, (t + 2 * hop) % n_tensor) for t in range(n_tensor)]
                )
                parts.append(moved)
            stacked = jnp.stack(parts)
            order = (tpos // 2 - jnp.arange(chips)) % chips
            placed = jnp.concatenate([stacked[order[c]] for c in range(chips)], axis=1)
            resid = jnp.where(section == 0, fresh, placed)
        else:
            resid = fresh
        states = resid.astype(jnp.float32)
        normed = (
            states * lax.rsqrt(jnp.mean(states * states, axis=-1, keepdims=True) + 1e-06) * gain
        ).astype(jnp.bfloat16)
        qkv = jnp.dot(normed, weights, preferred_element_type=jnp.float32).astype(jnp.bfloat16)
        query = qkv[:, :qdim].reshape(steps, brow, kvlocal, groups, HDIM)
        block_k = qkv[:, qdim : qdim + kvdim].reshape(steps, brow, kvlocal, HDIM)
        block_v = qkv[:, qdim + kvdim :].reshape(steps, brow, kvlocal, HDIM)
        ckeys = lax.dynamic_slice_in_dim(keys_local, first, brow, 0).reshape(
            brow, length, kvlocal, HDIM
        )
        cvals = lax.dynamic_slice_in_dim(values_local, first, brow, 0).reshape(
            brow, length, kvlocal, HDIM
        )
        spans = lax.dynamic_slice_in_dim(cache_lengths, first, brow)
        cmask = (jnp.arange(length)[None, :] < spans[:, None])[None, :, None, None, :]
        scache = (
            jnp.einsum("sbkgd,blkd->sbkgl", query, ckeys, preferred_element_type=jnp.float32)
            * scale
        )
        snew = (
            jnp.einsum("sbkgd,tbkd->sbkgt", query, block_k, preferred_element_type=jnp.float32)
            * scale
        )
        scache = jnp.where(cmask, scache, -1e30)
        snew = jnp.where(nmask, snew, -1e30)
        top = jnp.maximum(jnp.max(scache, axis=-1), jnp.max(snew, axis=-1))[..., None]
        ecache = jnp.where(cmask, jnp.exp(scache - top), 0.0)
        enew = jnp.where(nmask, jnp.exp(snew - top), 0.0)
        total = (jnp.sum(ecache, axis=-1) + jnp.sum(enew, axis=-1))[..., None]
        wcache = (ecache / total).astype(jnp.bfloat16)
        wnew = (enew / total).astype(jnp.bfloat16)
        mixed = jnp.einsum("sbkgl,blkd->sbkgd", wcache, cvals, preferred_element_type=jnp.float32)
        mixed = mixed + jnp.einsum(
            "sbkgt,tbkd->sbkgd", wnew, block_v, preferred_element_type=jnp.float32
        )
        attn = mixed.astype(jnp.bfloat16).reshape(rows, qdim)
        partial_value = jnp.dot(attn, wo_local, preferred_element_type=jnp.float32).astype(
            jnp.bfloat16
        )
        pieces = partial_value.reshape(rows, n_tensor, shard).swapaxes(0, 1)
        swapped = lax.all_to_all(pieces, "tensor", split_axis=0, concat_axis=0, tiled=True)
        summed = jnp.sum(swapped.astype(jnp.float32), axis=0)
        wide = lax.dynamic_slice_in_dim(states, tpos * shard, shard, 1) + summed
        record = jnp.where(
            valid,
            lax.dynamic_update_slice(record, wide.reshape(steps, brow, shard), (0, first, 0)),
            record,
        )
        if tick < ticks - 1:
            current = from_behind(wide.astype(jnp.bfloat16), "section", 1)
    return record[None]


def solution(mesh):
    placed = (
        P(("section", "tensor"), None),
        P(),
        P("section", "tensor", None),
        P("section", None, None, "tensor"),
        P("section", None, None, "tensor"),
        P(),
        P("section", None),
        P(),
    )
    return jax.shard_map(
        per_device,
        mesh=mesh,
        in_specs=placed,
        out_specs=P("section", None, None, "tensor"),
        check_vma=False,
    )
```

```python
import functools

import jax
import jax.numpy as jnp
import numpy as np
from jax import lax
from jax.experimental import pallas as pl
from jax.experimental.pallas import tpu as pltpu
from jax.sharding import Mesh, PartitionSpec as P

HDIM = 128
FB = 8
STREAMS = 2
ITEMS = 2
ROWBLOCK = 256
CHUNK = 384
WINDOW = 512
VMEM = 48 * 1024 * 1024


def sort_kernel(first, layers, kept, slab, out):
    feats = ROWBLOCK // layers
    row = lax.broadcasted_iota(jnp.int32, (kept * feats, ROWBLOCK), 0)
    col = lax.broadcasted_iota(jnp.int32, (kept * feats, ROWBLOCK), 1)
    source = row % feats * layers + first + row // feats
    order = jnp.where(col == source, 1.0, 0.0).astype(jnp.bfloat16)
    moved = jnp.dot(order, slab[...], preferred_element_type=jnp.float32).astype(jnp.bfloat16)
    for layer in range(kept):
        out[layer, 0] = moved[layer * feats : (layer + 1) * feats]


def sort_slab(slab, phase, layers, n_tensor):
    rows, columns = slab.shape
    kept = layers // 2
    cdev = columns // n_tensor
    feats = ROWBLOCK // layers
    return pl.pallas_call(
        functools.partial(sort_kernel, phase * kept, layers, kept),
        grid=(n_tensor, rows // ROWBLOCK),
        in_specs=[pl.BlockSpec((ROWBLOCK, cdev), lambda t, i: (i, t))],
        out_specs=pl.BlockSpec((kept, 1, feats, cdev), lambda t, i: (0, t, i, 0)),
        out_shape=jax.ShapeDtypeStruct((kept, n_tensor, rows // layers, cdev), jnp.bfloat16),
        compiler_params=pltpu.CompilerParams(vmem_limit_bytes=VMEM),
        cost_estimate=pl.CostEstimate(
            flops=rows * columns * ROWBLOCK, bytes_accessed=3 * rows * columns, transcendentals=0
        ),
    )(slab)


def project_kernel(tick, tiles, tilew, n_y, use, scalars, mine, other, gains, *rest):
    weights, (out, normed, acc) = rest[: len(use)], rest[len(use) :]
    j = pl.program_id(0)
    rows, half = mine.shape
    width = 2 * half
    shard = half // n_y
    core, phase = scalars[0], scalars[1 + tick]

    @pl.when(j == 0)
    def _():
        here = mine[...].astype(jnp.float32)
        there = other[...].astype(jnp.float32)
        total = jnp.sum(here * here, axis=1, keepdims=True)
        total = total + jnp.sum(there * there, axis=1, keepdims=True)
        inverse = lax.rsqrt(total / width + 1e-06)
        gain = jnp.where(phase == 0, gains[0:1], gains[1:2])
        low = jnp.where(core == 0, here, there) * inverse
        high = jnp.where(core == 0, there, here) * inverse
        for y in range(n_y):
            at = 2 * y * shard
            piece = slice(y * shard, (y + 1) * shard)
            normed[:, at : at + shard] = low[:, piece] * gain[:, at : at + shard]
            at = at + shard
            normed[:, at : at + shard] = high[:, piece] * gain[:, at : at + shard]
        normed[:, width:] = jnp.zeros((rows, WINDOW), jnp.float32)
        acc[...] = jnp.zeros_like(acc)

    per = CHUNK // tilew
    base = scalars.shape[0] - 2 * tiles
    lane = lax.broadcasted_iota(jnp.int32, (rows, CHUNK), 1)
    spread = jnp.zeros((rows, CHUNK), jnp.float32)
    for a in range(per):
        start = scalars[base + j * per + a] * FB
        count = scalars[base + tiles + j * per + a] * FB
        aligned = start // 128 * 128
        window = normed[:, pl.ds(pl.multiple_of(aligned, 128), WINDOW)]
        put = a * tilew
        shift = (put - (start - aligned) + WINDOW) % WINDOW
        rolled = pltpu.roll(window, shift, 1)[:, :CHUNK]
        spread = jnp.where((lane >= put) & (lane < put + count), rolled, spread)
    spread = spread.astype(jnp.bfloat16)
    if len(use) == 1:
        acc[...] += jnp.dot(spread, weights[0][...], preferred_element_type=jnp.float32)
    else:

        @pl.when(phase == 0)
        def _():
            acc[...] += jnp.dot(spread, weights[0][...], preferred_element_type=jnp.float32)

        @pl.when(phase == 1)
        def _():
            acc[...] += jnp.dot(spread, weights[1][...], preferred_element_type=jnp.float32)

    @pl.when(j == pl.num_programs(0) - 1)
    def _():
        out[...] = acc[...].astype(jnp.bfloat16)


def project(tick, use, tiles, tilew, n_y, scalars, mine, other, gains, weights):
    rows, half = mine.shape
    depth, cdev = weights[0].shape
    if len(use) == 1:
        maps = [lambda j, s: (j, 0)]
    else:
        maps = [
            lambda j, s: (jnp.where(s[1 + tick] == 0, j, 0), 0),
            lambda j, s: (jnp.where(s[1 + tick] == 1, j, 0), 0),
        ]
    whole = lambda j, s: (0, 0)
    return pl.pallas_call(
        functools.partial(project_kernel, tick, tiles, tilew, n_y, use),
        grid_spec=pltpu.PrefetchScalarGridSpec(
            num_scalar_prefetch=1,
            grid=(depth // CHUNK,),
            in_specs=[
                pl.BlockSpec((rows, half), whole),
                pl.BlockSpec((rows, half), whole),
                pl.BlockSpec(gains.shape, whole),
            ]
            + [pl.BlockSpec((CHUNK, cdev), m) for m in maps],
            out_specs=pl.BlockSpec((rows, cdev), whole),
            scratch_shapes=[
                pltpu.VMEM((rows, 2 * half + WINDOW), jnp.float32),
                pltpu.VMEM((rows, cdev), jnp.float32),
            ],
        ),
        out_shape=jax.ShapeDtypeStruct((rows, cdev), jnp.bfloat16),
        compiler_params=pltpu.CompilerParams(vmem_limit_bytes=VMEM),
        cost_estimate=pl.CostEstimate(
            flops=2 * rows * depth * cdev, bytes_accessed=2 * depth * cdev, transcendentals=0
        ),
    )(scalars, mine, other, gains, *weights)


def attend_kernel(steps, brow, kvlocal, groups, n_y, scalars, own, sent, span, ckeys, cvals, wo, theirs, ours, attn):
    k = pl.program_id(0)
    rows = steps * brow
    length = ckeys.shape[1]
    scale = 1.0 / HDIM**0.5
    qdim = kvlocal * groups * HDIM
    kvdim = kvlocal * HDIM

    @pl.when(k == 0)
    def _():
        qkv = (own[...].astype(jnp.float32) + sent[...].astype(jnp.float32)).astype(jnp.bfloat16)
        qkv = qkv.astype(jnp.float32)
        keys = ckeys[...].reshape(brow * length, kvdim)
        values = cvals[...].reshape(brow * length, kvdim)
        tall = groups * rows
        at = lax.broadcasted_iota(jnp.int32, (tall, brow * length), 0)
        col = lax.broadcasted_iota(jnp.int32, (tall, brow * length), 1)
        cmask = (at % brow == col // length) & (col % length < span[0])
        at = lax.broadcasted_iota(jnp.int32, (tall, rows), 0)
        col = lax.broadcasted_iota(jnp.int32, (tall, rows), 1)
        nmask = (at % brow == col % brow) & (col // brow <= at % rows // brow)
        contract = (((1,), (1,)), ((), ()))
        for head in range(kvlocal):
            lanes = slice(head * HDIM, (head + 1) * HDIM)
            first = head * groups * HDIM
            query = jnp.concatenate(
                [qkv[:, first + g * HDIM : first + (g + 1) * HDIM] for g in range(groups)], axis=0
            ).astype(jnp.bfloat16)
            at = qdim + head * HDIM
            knew = qkv[:, at : at + HDIM].astype(jnp.bfloat16)
            at = at + kvdim
            vnew = qkv[:, at : at + HDIM].astype(jnp.bfloat16)
            scache = scale * lax.dot_general(
                query, keys[:, lanes], contract, preferred_element_type=jnp.float32
            )
            snew = scale * lax.dot_general(
                query, knew, contract, preferred_element_type=jnp.float32
            )
            scache = jnp.where(cmask, scache, -1e30)
            snew = jnp.where(nmask, snew, -1e30)
            top = jnp.maximum(
                jnp.max(scache, axis=1, keepdims=True), jnp.max(snew, axis=1, keepdims=True)
            )
            ecache = jnp.where(cmask, jnp.exp(scache - top), 0.0)
            enew = jnp.where(nmask, jnp.exp(snew - top), 0.0)
            total = jnp.sum(ecache, axis=1, keepdims=True) + jnp.sum(enew, axis=1, keepdims=True)
            inverse = 1.0 / total
            wcache = (ecache * inverse).astype(jnp.bfloat16)
            wnew = (enew * inverse).astype(jnp.bfloat16)
            mixed = jnp.dot(wcache, values[:, lanes], preferred_element_type=jnp.float32)
            mixed = mixed + jnp.dot(wnew, vnew, preferred_element_type=jnp.float32)
            for g in range(groups):
                attn[:, first + g * HDIM : first + (g + 1) * HDIM] = mixed[
                    g * rows : (g + 1) * rows
                ].astype(jnp.bfloat16)

    product = jnp.dot(attn[...], wo[0], preferred_element_type=jnp.float32).astype(jnp.bfloat16)

    @pl.when(k < n_y)
    def _():
        theirs[...] = product

    @pl.when(k >= n_y)
    def _():
        ours[...] = product


def attend(item_at, steps, brow, n_y, scalars, own, sent, spans, keys, values, wo):
    rows, cdev = own.shape
    _, qdim, width = wo.shape
    length, kvdim = keys.shape[1:]
    kvlocal = kvdim // HDIM
    groups = qdim // kvdim
    shard = width // (2 * n_y)
    whole = lambda k, s: (0, 0)
    return pl.pallas_call(
        functools.partial(attend_kernel, steps, brow, kvlocal, groups, n_y),
        grid_spec=pltpu.PrefetchScalarGridSpec(
            num_scalar_prefetch=1,
            grid=(2 * n_y,),
            in_specs=[
                pl.BlockSpec((rows, cdev), whole),
                pl.BlockSpec((rows, cdev), whole),
                pl.BlockSpec((1, 1, brow * length), lambda k, s: (s[item_at], 0, 0)),
                pl.BlockSpec((brow, length, kvdim), lambda k, s: (s[item_at], 0, 0)),
                pl.BlockSpec((brow, length, kvdim), lambda k, s: (s[item_at], 0, 0)),
                pl.BlockSpec(
                    (1, qdim, shard),
                    lambda k, s: (0, 0, k % n_y * 2 + jnp.where(k < n_y, 1 - s[0], s[0])),
                ),
            ],
            out_specs=[
                pl.BlockSpec((rows, shard), lambda k, s: (0, jnp.minimum(k, n_y - 1))),
                pl.BlockSpec((rows, shard), lambda k, s: (0, jnp.maximum(k - n_y, 0))),
            ],
            scratch_shapes=[pltpu.VMEM((rows, qdim), jnp.bfloat16)],
        ),
        out_shape=[jax.ShapeDtypeStruct((rows, shard * n_y), jnp.bfloat16)] * 2,
        compiler_params=pltpu.CompilerParams(vmem_limit_bytes=VMEM),
        cost_estimate=pl.CostEstimate(
            flops=2 * rows * qdim * width, bytes_accessed=2 * qdim * width, transcendentals=0
        ),
    )(scalars, own, sent, spans, keys, values, wo)


def per_device(
    trainer_tiles,
    tile_lengths,
    wo_rollout,
    cache_keys,
    cache_values,
    cache_lengths,
    norm_gain,
    step_inputs,
):
    n_zone = lax.axis_size("zone")
    n_spot = lax.axis_size("spot")
    n_tensor = lax.axis_size("tensor")
    layers = n_zone * n_spot
    tiles = n_spot * n_tensor
    n_y = n_tensor // 2
    slab, columns = trainer_tiles.shape
    cdev = columns // n_tensor
    tilew = slab // layers
    width = wo_rollout.shape[2]
    shard = width // n_tensor
    half = n_y * shard
    steps = step_inputs.shape[0]
    seqs, length = cache_keys.shape[1:3]
    n_item = STREAMS * ITEMS
    brow = seqs // n_item
    rows = steps * brow
    ticks = layers + ITEMS - 1
    zone = lax.axis_index("zone")
    spot = lax.axis_index("spot")
    tpos = lax.axis_index("tensor")
    core = tpos % 2
    layer = zone * n_spot + spot

    weights = []
    for phase in range(2):
        ordered = sort_slab(trainer_tiles, phase, layers, n_tensor)
        arrived = lax.all_to_all(
            ordered.reshape(tiles, tilew, cdev),
            ("spot", "tensor"),
            split_axis=0,
            concat_axis=0,
            tiled=True,
        )
        weights.append(arrived.reshape(tiles * tilew, cdev))

    ends = jnp.cumsum(tile_lengths)
    starts = lax.dynamic_slice_in_dim(ends - tile_lengths, zone * tiles, tiles)
    counts = lax.dynamic_slice_in_dim(tile_lengths, zone * tiles, tiles)
    tick_ids = jnp.arange(ticks, dtype=jnp.int32)
    phases = (tick_ids >= spot + n_spot).astype(jnp.int32)
    turns = jnp.clip(tick_ids - layer, 0, ITEMS - 1)
    turns = jnp.concatenate([turns + stream * ITEMS for stream in range(STREAMS)])
    scalars = jnp.concatenate([core[None], phases, turns, starts, counts]).astype(jnp.int32)
    flip = [(z, 1 - z) for z in range(2)]
    swapped = lax.ppermute(norm_gain, "zone", flip)
    gains = jnp.concatenate(
        [jnp.where(zone == 0, norm_gain, swapped), jnp.where(zone == 0, swapped, norm_gain)]
    )
    spans = jnp.repeat(cache_lengths, length).reshape(n_item, 1, brow * length)
    axes = ("zone", "spot", "tensor")

    def device(z, s, t):
        return (z * n_spot + s) * n_tensor + t

    def split(pairs, value):
        return lax.ppermute(value, axes, pairs)

    def active(tick):
        return [l for l in range(layers) if 0 <= tick - l < ITEMS]

    across = [(t, t ^ 1) for t in range(n_tensor)]
    shown = step_inputs.reshape(steps, n_item, brow, n_y, 2, shard)
    records = []
    for stream in range(STREAMS):
        arrived, record = None, []
        for tick in range(ticks):
            busy = active(tick)
            if tick < ITEMS:
                item = stream * ITEMS + tick
                fresh = shown[:, item].reshape(rows, n_y, 2, shard)
                mine = lax.dynamic_index_in_dim(fresh, core, 2, False).reshape(rows, half)
                mine = jnp.where(spot == 0, mine, 0)
                if tick:
                    mine = mine + arrived
            else:
                mine = arrived
            if tick:
                other = lax.ppermute(mine, "tensor", across)
            else:
                other = lax.dynamic_index_in_dim(fresh, 1 - core, 2, False).reshape(rows, half)
            use = sorted({l // n_spot for l in busy})
            own = project(
                tick, use, tiles, tilew, n_y, scalars, mine, other, gains, [weights[p] for p in use]
            )
            pairs = [
                (device(1 - l // n_spot, l % n_spot, t), device(l // n_spot, l % n_spot, t))
                for l in busy
                for t in range(n_tensor)
            ]
            sent = split(pairs, own)
            item_at = 1 + ticks + stream * ticks + tick
            theirs, ours = attend(
                item_at, steps, brow, n_y, scalars, own, sent, spans, cache_keys[0], cache_values[0], wo_rollout
            )
            part = ours.astype(jnp.float32) + lax.ppermute(theirs, "tensor", across).astype(
                jnp.float32
            )
            bit = 2
            while bit < n_tensor:
                part = part.astype(jnp.bfloat16)
                moved = lax.ppermute(part, "tensor", [(t, t ^ bit) for t in range(n_tensor)])
                part = part.astype(jnp.float32) + moved.astype(jnp.float32)
                bit = bit * 2
            wide = mine.astype(jnp.float32) + part
            record.append(lax.dynamic_slice_in_dim(wide, tpos // 2 * shard, shard, 1))
            after = wide.astype(jnp.bfloat16)
            going = [l for l in busy if l + 1 < layers]
            if tick + 1 < ticks:
                arrived = 0
                for turn in range(2):
                    pairs = []
                    for l in going:
                        home = l // n_spot
                        for t in range(n_tensor):
                            source = device(home, l % n_spot, t)
                            pairs.append((source, device(home ^ turn, (l + 1) % n_spot, t)))
                    arrived = arrived + split(pairs, after)
        record = jnp.stack(record)
        record = lax.dynamic_slice_in_dim(record, layer, ITEMS, 0)
        record = record.reshape(ITEMS, steps, brow, shard).swapaxes(0, 1)
        records.append(record.reshape(steps, ITEMS * brow, shard))
    return jnp.concatenate(records, axis=1)[None]


def solution(mesh):
    n_section, n_tensor = mesh.devices.shape
    fine = Mesh(mesh.devices.reshape(2, n_section // 2, n_tensor), ("zone", "spot", "tensor"))
    section = ("zone", "spot")
    placed = (
        P(("zone", "spot", "tensor"), None),
        P(),
        P(section, "tensor", None),
        P(section, None, None, "tensor"),
        P(section, None, None, "tensor"),
        P(),
        P(section, None),
        P(),
    )
    return jax.shard_map(
        per_device,
        mesh=fine,
        in_specs=placed,
        out_specs=P(section, None, None, "tensor"),
        check_vma=False,
    )
```

```python
import functools

import jax
import jax.numpy as jnp
import numpy as np
from jax import lax
from jax.experimental import pallas as pl
from jax.experimental.pallas import tpu as pltpu
from jax.sharding import Mesh, PartitionSpec as P

HDIM = 128
FB = 8
STREAMS = 2
ITEMS = 2
ROWBLOCK = 256
CHUNK = 384
WINDOW = 512
VMEM = 48 * 1024 * 1024


def sort_kernel(first, layers, kept, slab, out):
    feats = ROWBLOCK // layers
    row = lax.broadcasted_iota(jnp.int32, (kept * feats, ROWBLOCK), 0)
    col = lax.broadcasted_iota(jnp.int32, (kept * feats, ROWBLOCK), 1)
    source = row % feats * layers + first + row // feats
    order = jnp.where(col == source, 1.0, 0.0).astype(jnp.bfloat16)
    moved = jnp.dot(order, slab[...], preferred_element_type=jnp.float32).astype(jnp.bfloat16)
    for layer in range(kept):
        out[layer, 0] = moved[layer * feats : (layer + 1) * feats]


def sort_slab(slab, phase, layers, n_tensor):
    rows, columns = slab.shape
    kept = layers // 2
    cdev = columns // n_tensor
    feats = ROWBLOCK // layers
    return pl.pallas_call(
        functools.partial(sort_kernel, phase * kept, layers, kept),
        grid=(n_tensor, rows // ROWBLOCK),
        in_specs=[pl.BlockSpec((ROWBLOCK, cdev), lambda t, i: (i, t))],
        out_specs=pl.BlockSpec((kept, 1, feats, cdev), lambda t, i: (0, t, i, 0)),
        out_shape=jax.ShapeDtypeStruct((kept, n_tensor, rows // layers, cdev), jnp.bfloat16),
        compiler_params=pltpu.CompilerParams(vmem_limit_bytes=VMEM),
        cost_estimate=pl.CostEstimate(
            flops=rows * columns * ROWBLOCK, bytes_accessed=3 * rows * columns, transcendentals=0
        ),
    )(slab)


def project_kernel(tick, tiles, tilew, n_y, use, scalars, mine, other, gains, *rest):
    weights, (out, normed, held, sems) = rest[: len(use)], rest[len(use) :]
    rows, half = mine.shape
    width = 2 * half
    shard = half // n_y
    chunks, size, cdev = held.shape
    core, phase = scalars[0], scalars[1 + tick]

    def fetch(source, j):
        return pltpu.make_async_copy(source.at[pl.ds(j * size, size)], held.at[j], sems.at[j])

    if len(use) == 1:
        for j in range(chunks):
            fetch(weights[0], j).start()
    else:
        for p in range(2):

            @pl.when(phase == p)
            def _():
                for j in range(chunks):
                    fetch(weights[p], j).start()

    here = mine[...].astype(jnp.float32)
    there = other[...].astype(jnp.float32)
    total = jnp.sum(here * here, axis=1, keepdims=True)
    total = total + jnp.sum(there * there, axis=1, keepdims=True)
    inverse = lax.rsqrt(total / width + 1e-06)
    gain = jnp.where(phase == 0, gains[0:1], gains[1:2])
    low = jnp.where(core == 0, here, there) * inverse
    high = jnp.where(core == 0, there, here) * inverse
    for y in range(n_y):
        at = 2 * y * shard
        piece = slice(y * shard, (y + 1) * shard)
        normed[:, at : at + shard] = low[:, piece] * gain[:, at : at + shard]
        at = at + shard
        normed[:, at : at + shard] = high[:, piece] * gain[:, at : at + shard]
    normed[:, width:] = jnp.zeros((rows, WINDOW), jnp.float32)

    per = CHUNK // tilew
    base = scalars.shape[0] - 2 * tiles
    lane = lax.broadcasted_iota(jnp.int32, (rows, CHUNK), 1)

    def spread(j):
        value = jnp.zeros((rows, CHUNK), jnp.float32)
        for a in range(per):
            start = scalars[base + j * per + a] * FB
            count = scalars[base + tiles + j * per + a] * FB
            aligned = start // 128 * 128
            window = normed[:, pl.ds(pl.multiple_of(aligned, 128), WINDOW)]
            put = a * tilew
            shift = (put - (start - aligned) + WINDOW) % WINDOW
            rolled = pltpu.roll(window, shift, 1)[:, :CHUNK]
            value = jnp.where((lane >= put) & (lane < put + count), rolled, value)
        return value.astype(jnp.bfloat16)

    acc = jnp.zeros((rows, cdev), jnp.float32)
    for j in range(chunks):
        parts = [spread(j * (size // CHUNK) + i) for i in range(size // CHUNK)]
        fetch(weights[0], j).wait()
        acc = acc + jnp.dot(
            jnp.concatenate(parts, axis=1), held[j], preferred_element_type=jnp.float32
        )
    out[...] = acc.astype(jnp.bfloat16)


def project(tick, use, tiles, tilew, n_y, scalars, mine, other, gains, weights):
    rows, half = mine.shape
    depth, cdev = weights[0].shape
    size = 2 * CHUNK
    vmem = pl.BlockSpec(memory_space=pltpu.VMEM)
    return pl.pallas_call(
        functools.partial(project_kernel, tick, tiles, tilew, n_y, use),
        in_specs=[pl.BlockSpec(memory_space=pltpu.SMEM)]
        + [vmem] * 3
        + [pl.BlockSpec(memory_space=pl.ANY)] * len(use),
        out_specs=vmem,
        scratch_shapes=[
            pltpu.VMEM((rows, 2 * half + WINDOW), jnp.float32),
            pltpu.VMEM((depth // size, size, cdev), jnp.bfloat16),
            pltpu.SemaphoreType.DMA((depth // size,)),
        ],
        out_shape=jax.ShapeDtypeStruct((rows, cdev), jnp.bfloat16),
        compiler_params=pltpu.CompilerParams(vmem_limit_bytes=VMEM),
        cost_estimate=pl.CostEstimate(
            flops=2 * rows * depth * cdev, bytes_accessed=2 * depth * cdev, transcendentals=0
        ),
    )(scalars, mine, other, gains, *weights)


def attend_kernel(steps, brow, kvlocal, groups, n_y, item_at, scalars, own, sent, spans, ckeys, cvals, wo, theirs, ours, attn, kheld, vheld, held, sems):
    rows = steps * brow
    length = ckeys.shape[1]
    scale = 1.0 / HDIM**0.5
    qdim = kvlocal * groups * HDIM
    kvdim = kvlocal * HDIM
    shard = held.shape[2]
    core = scalars[0]
    item = scalars[item_at]
    first = pl.multiple_of(item * brow, brow)
    gets = [
        pltpu.make_async_copy(ckeys.at[pl.ds(first, brow)], kheld, sems.at[2 * n_y]),
        pltpu.make_async_copy(cvals.at[pl.ds(first, brow)], vheld, sems.at[2 * n_y + 1]),
    ]
    for k in range(2 * n_y):
        side = 1 - core if k < n_y else core
        at = pl.multiple_of((k % n_y * 2 + side) * shard, shard)
        gets.append(
            pltpu.make_async_copy(wo.at[0, :, pl.ds(at, shard)], held.at[k], sems.at[k])
        )
    for get in gets:
        get.start()
    gets[0].wait()
    gets[1].wait()
    span = spans[item]

    qkv = (own[...].astype(jnp.float32) + sent[...].astype(jnp.float32)).astype(jnp.bfloat16)
    qkv = qkv.astype(jnp.float32)
    keys = kheld[...].reshape(brow * length, kvdim)
    values = vheld[...].reshape(brow * length, kvdim)
    tall = groups * rows
    at = lax.broadcasted_iota(jnp.int32, (tall, brow * length), 0)
    col = lax.broadcasted_iota(jnp.int32, (tall, brow * length), 1)
    cmask = (at % brow == col // length) & (col % length < span)
    at = lax.broadcasted_iota(jnp.int32, (tall, rows), 0)
    col = lax.broadcasted_iota(jnp.int32, (tall, rows), 1)
    nmask = (at % brow == col % brow) & (col // brow <= at % rows // brow)
    contract = (((1,), (1,)), ((), ()))
    for head in range(kvlocal):
        lanes = slice(head * HDIM, (head + 1) * HDIM)
        first = head * groups * HDIM
        query = jnp.concatenate(
            [qkv[:, first + g * HDIM : first + (g + 1) * HDIM] for g in range(groups)], axis=0
        ).astype(jnp.bfloat16)
        at = qdim + head * HDIM
        knew = qkv[:, at : at + HDIM].astype(jnp.bfloat16)
        at = at + kvdim
        vnew = qkv[:, at : at + HDIM].astype(jnp.bfloat16)
        scache = scale * lax.dot_general(
            query, keys[:, lanes], contract, preferred_element_type=jnp.float32
        )
        snew = scale * lax.dot_general(
            query, knew, contract, preferred_element_type=jnp.float32
        )
        scache = jnp.where(cmask, scache, -1e30)
        snew = jnp.where(nmask, snew, -1e30)
        top = jnp.maximum(
            jnp.max(scache, axis=1, keepdims=True), jnp.max(snew, axis=1, keepdims=True)
        )
        ecache = jnp.where(cmask, jnp.exp(scache - top), 0.0)
        enew = jnp.where(nmask, jnp.exp(snew - top), 0.0)
        total = jnp.sum(ecache, axis=1, keepdims=True) + jnp.sum(enew, axis=1, keepdims=True)
        inverse = 1.0 / total
        wcache = (ecache * inverse).astype(jnp.bfloat16)
        wnew = (enew * inverse).astype(jnp.bfloat16)
        mixed = jnp.dot(wcache, values[:, lanes], preferred_element_type=jnp.float32)
        mixed = mixed + jnp.dot(wnew, vnew, preferred_element_type=jnp.float32)
        for g in range(groups):
            attn[:, first + g * HDIM : first + (g + 1) * HDIM] = mixed[
                g * rows : (g + 1) * rows
            ].astype(jnp.bfloat16)

    for k in range(2 * n_y):
        gets[2 + k].wait()
        product = jnp.dot(attn[...], held[k], preferred_element_type=jnp.float32)
        target = theirs if k < n_y else ours
        at = k % n_y * shard
        target[:, at : at + shard] = product.astype(jnp.bfloat16)


def attend(item_at, steps, brow, n_y, scalars, own, sent, spans, keys, values, wo):
    rows, cdev = own.shape
    _, qdim, width = wo.shape
    length, kvdim = keys.shape[1:]
    kvlocal = kvdim // HDIM
    groups = qdim // kvdim
    shard = width // (2 * n_y)
    vmem = pl.BlockSpec(memory_space=pltpu.VMEM)
    return pl.pallas_call(
        functools.partial(attend_kernel, steps, brow, kvlocal, groups, n_y, item_at),
        in_specs=[pl.BlockSpec(memory_space=pltpu.SMEM)]
        + [vmem] * 3
        + [pl.BlockSpec(memory_space=pl.ANY)] * 3,
        out_specs=[vmem] * 2,
        scratch_shapes=[
            pltpu.VMEM((rows, qdim), jnp.bfloat16),
            pltpu.VMEM((brow, length, kvdim), jnp.bfloat16),
            pltpu.VMEM((brow, length, kvdim), jnp.bfloat16),
            pltpu.VMEM((2 * n_y, qdim, shard), jnp.bfloat16),
            pltpu.SemaphoreType.DMA((2 * n_y + 2,)),
        ],
        out_shape=[jax.ShapeDtypeStruct((rows, shard * n_y), jnp.bfloat16)] * 2,
        compiler_params=pltpu.CompilerParams(vmem_limit_bytes=VMEM),
        cost_estimate=pl.CostEstimate(
            flops=2 * rows * qdim * width, bytes_accessed=2 * qdim * width, transcendentals=0
        ),
    )(scalars, own, sent, spans, keys, values, wo)


def per_device(
    trainer_tiles,
    tile_lengths,
    wo_rollout,
    cache_keys,
    cache_values,
    cache_lengths,
    norm_gain,
    step_inputs,
):
    n_zone = lax.axis_size("zone")
    n_spot = lax.axis_size("spot")
    n_tensor = lax.axis_size("tensor")
    layers = n_zone * n_spot
    tiles = n_spot * n_tensor
    n_y = n_tensor // 2
    slab, columns = trainer_tiles.shape
    cdev = columns // n_tensor
    tilew = slab // layers
    width = wo_rollout.shape[2]
    shard = width // n_tensor
    half = n_y * shard
    steps = step_inputs.shape[0]
    seqs, length = cache_keys.shape[1:3]
    n_item = STREAMS * ITEMS
    brow = seqs // n_item
    rows = steps * brow
    ticks = layers + ITEMS - 1
    zone = lax.axis_index("zone")
    spot = lax.axis_index("spot")
    tpos = lax.axis_index("tensor")
    core = tpos % 2
    layer = zone * n_spot + spot

    weights = []
    for phase in range(2):
        ordered = sort_slab(trainer_tiles, phase, layers, n_tensor)
        arrived = lax.all_to_all(
            ordered.reshape(tiles, tilew, cdev),
            ("spot", "tensor"),
            split_axis=0,
            concat_axis=0,
            tiled=True,
        )
        weights.append(arrived.reshape(tiles * tilew, cdev))

    ends = jnp.cumsum(tile_lengths)
    starts = lax.dynamic_slice_in_dim(ends - tile_lengths, zone * tiles, tiles)
    counts = lax.dynamic_slice_in_dim(tile_lengths, zone * tiles, tiles)
    tick_ids = jnp.arange(ticks, dtype=jnp.int32)
    phases = (tick_ids >= spot + n_spot).astype(jnp.int32)
    turns = jnp.clip(tick_ids - layer, 0, ITEMS - 1)
    turns = jnp.concatenate([turns + stream * ITEMS for stream in range(STREAMS)])
    scalars = jnp.concatenate([core[None], phases, turns, starts, counts]).astype(jnp.int32)
    flip = [(z, 1 - z) for z in range(2)]
    swapped = lax.ppermute(norm_gain, "zone", flip)
    gains = jnp.concatenate(
        [jnp.where(zone == 0, norm_gain, swapped), jnp.where(zone == 0, swapped, norm_gain)]
    )
    spans = jnp.repeat(cache_lengths, length).reshape(n_item, 1, brow * length)
    axes = ("zone", "spot", "tensor")

    flat = [(z, s) for z in range(n_zone) for s in range(n_spot)]

    def shifted(turn):
        pairs = []
        for z, s in flat:
            nearby = (s + 1) % n_spot
            ahead = z if s + 1 < n_spot else 1 - z
            pairs.append((z * n_spot + s, (ahead ^ turn) * n_spot + nearby))
        return pairs

    hops = [shifted(turn) for turn in range(2)]

    def active(tick):
        return [l for l in range(layers) if 0 <= tick - l < ITEMS]

    across = [(t, t ^ 1) for t in range(n_tensor)]
    shown = step_inputs.reshape(steps, n_item, brow, n_y, 2, shard)
    records = []
    for stream in range(STREAMS):
        arrived, record = None, []
        for tick in range(ticks):
            busy = active(tick)
            if tick < ITEMS:
                item = stream * ITEMS + tick
                fresh = shown[:, item].reshape(rows, n_y, 2, shard)
                mine = lax.dynamic_index_in_dim(fresh, core, 2, False).reshape(rows, half)
                mine = jnp.where(spot == 0, mine, arrived if tick else 0)
            else:
                mine = arrived
            if tick:
                other = lax.ppermute(mine, "tensor", across)
            else:
                other = lax.dynamic_index_in_dim(fresh, 1 - core, 2, False).reshape(rows, half)
            use = sorted({l // n_spot for l in busy})
            own = project(
                tick, use, tiles, tilew, n_y, scalars, mine, other, gains, [weights[p] for p in use]
            )
            sent = lax.ppermute(own, "zone", flip)
            item_at = 1 + ticks + stream * ticks + tick
            theirs, ours = attend(
                item_at, steps, brow, n_y, scalars, own, sent, spans, cache_keys[0], cache_values[0], wo_rollout
            )
            part = ours.astype(jnp.float32) + lax.ppermute(theirs, "tensor", across).astype(
                jnp.float32
            )
            bit = 2
            while bit < n_tensor:
                part = part.astype(jnp.bfloat16)
                moved = lax.ppermute(part, "tensor", [(t, t ^ bit) for t in range(n_tensor)])
                part = part.astype(jnp.float32) + moved.astype(jnp.float32)
                bit = bit * 2
            wide = mine.astype(jnp.float32) + part
            record.append(lax.dynamic_slice_in_dim(wide, tpos // 2 * shard, shard, 1))
            after = wide.astype(jnp.bfloat16)
            if tick + 1 < ticks:
                at_home = phases[tick + 1] == zone
                near = lax.ppermute(after, ("zone", "spot"), hops[0])
                far = lax.ppermute(after, ("zone", "spot"), hops[1])
                arrived = jnp.where(at_home, near, far)
        record = jnp.stack(record)
        record = lax.dynamic_slice_in_dim(record, layer, ITEMS, 0)
        record = record.reshape(ITEMS, steps, brow, shard).swapaxes(0, 1)
        records.append(record.reshape(steps, ITEMS * brow, shard))
    return jnp.concatenate(records, axis=1)[None]


def solution(mesh):
    n_section, n_tensor = mesh.devices.shape
    fine = Mesh(mesh.devices.reshape(2, n_section // 2, n_tensor), ("zone", "spot", "tensor"))
    section = ("zone", "spot")
    placed = (
        P(("zone", "spot", "tensor"), None),
        P(),
        P(section, "tensor", None),
        P(section, None, None, "tensor"),
        P(section, None, None, "tensor"),
        P(),
        P(section, None),
        P(),
    )
    return jax.shard_map(
        per_device,
        mesh=fine,
        in_specs=placed,
        out_specs=P(section, None, None, "tensor"),
        check_vma=False,
    )
```

```python
import functools

import jax
import jax.numpy as jnp
import numpy as np
from jax import lax
from jax.experimental import pallas as pl
from jax.experimental.pallas import tpu as pltpu
from jax.sharding import Mesh, PartitionSpec as P

HDIM = 128
FB = 8
STREAMS = 1
ITEMS = 2
ROWBLOCK = 256
CHUNK = 384
WINDOW = 512
VMEM = 48 * 1024 * 1024


def sort_kernel(first, layers, kept, slab, out):
    feats = ROWBLOCK // layers
    row = lax.broadcasted_iota(jnp.int32, (kept * feats, ROWBLOCK), 0)
    col = lax.broadcasted_iota(jnp.int32, (kept * feats, ROWBLOCK), 1)
    source = row % feats * layers + first + row // feats
    order = jnp.where(col == source, 1.0, 0.0).astype(jnp.bfloat16)
    moved = jnp.dot(order, slab[...], preferred_element_type=jnp.float32).astype(jnp.bfloat16)
    for layer in range(kept):
        out[layer, 0] = moved[layer * feats : (layer + 1) * feats]


def sort_slab(slab, phase, layers, n_tensor):
    rows, columns = slab.shape
    kept = layers // 2
    cdev = columns // n_tensor
    feats = ROWBLOCK // layers
    return pl.pallas_call(
        functools.partial(sort_kernel, phase * kept, layers, kept),
        grid=(n_tensor, rows // ROWBLOCK),
        in_specs=[pl.BlockSpec((ROWBLOCK, cdev), lambda t, i: (i, t))],
        out_specs=pl.BlockSpec((kept, 1, feats, cdev), lambda t, i: (0, t, i, 0)),
        out_shape=jax.ShapeDtypeStruct((kept, n_tensor, rows // layers, cdev), jnp.bfloat16),
        compiler_params=pltpu.CompilerParams(vmem_limit_bytes=VMEM),
        cost_estimate=pl.CostEstimate(
            flops=rows * columns * ROWBLOCK, bytes_accessed=3 * rows * columns, transcendentals=0
        ),
    )(slab)


def project_kernel(tick, tiles, tilew, n_y, use, scalars, mine, other, gains, *rest):
    weights, (out, normed, held, sems) = rest[: len(use)], rest[len(use) :]
    rows, half = mine.shape
    width = 2 * half
    shard = half // n_y
    chunks, size, cdev = held.shape
    core, phase = scalars[0], scalars[1 + tick]

    def fetch(source, j):
        return pltpu.make_async_copy(source.at[pl.ds(j * size, size)], held.at[j], sems.at[j])

    if len(use) == 1:
        for j in range(chunks):
            fetch(weights[0], j).start()
    else:
        for p in range(2):

            @pl.when(phase == p)
            def _():
                for j in range(chunks):
                    fetch(weights[p], j).start()

    here = mine[...].astype(jnp.float32)
    there = other[...].astype(jnp.float32)
    total = jnp.sum(here * here, axis=1, keepdims=True)
    total = total + jnp.sum(there * there, axis=1, keepdims=True)
    inverse = lax.rsqrt(total / width + 1e-06)
    gain = jnp.where(phase == 0, gains[0:1], gains[1:2])
    low = jnp.where(core == 0, here, there) * inverse
    high = jnp.where(core == 0, there, here) * inverse
    for y in range(n_y):
        at = 2 * y * shard
        piece = slice(y * shard, (y + 1) * shard)
        normed[:, at : at + shard] = low[:, piece] * gain[:, at : at + shard]
        at = at + shard
        normed[:, at : at + shard] = high[:, piece] * gain[:, at : at + shard]
    normed[:, width:] = jnp.zeros((rows, WINDOW), jnp.float32)

    per = CHUNK // tilew
    base = scalars.shape[0] - 2 * tiles
    lane = lax.broadcasted_iota(jnp.int32, (rows, CHUNK), 1)

    def spread(j):
        value = jnp.zeros((rows, CHUNK), jnp.float32)
        for a in range(per):
            start = scalars[base + j * per + a] * FB
            count = scalars[base + tiles + j * per + a] * FB
            aligned = start // 128 * 128
            window = normed[:, pl.ds(pl.multiple_of(aligned, 128), WINDOW)]
            put = a * tilew
            shift = (put - (start - aligned) + WINDOW) % WINDOW
            rolled = pltpu.roll(window, shift, 1)[:, :CHUNK]
            value = jnp.where((lane >= put) & (lane < put + count), rolled, value)
        return value.astype(jnp.bfloat16)

    acc = jnp.zeros((rows, cdev), jnp.float32)
    for j in range(chunks):
        parts = [spread(j * (size // CHUNK) + i) for i in range(size // CHUNK)]
        fetch(weights[0], j).wait()
        acc = acc + jnp.dot(
            jnp.concatenate(parts, axis=1), held[j], preferred_element_type=jnp.float32
        )
    out[...] = acc.astype(jnp.bfloat16)


def project(tick, use, tiles, tilew, n_y, scalars, mine, other, gains, weights):
    rows, half = mine.shape
    depth, cdev = weights[0].shape
    size = 2 * CHUNK
    vmem = pl.BlockSpec(memory_space=pltpu.VMEM)
    return pl.pallas_call(
        functools.partial(project_kernel, tick, tiles, tilew, n_y, use),
        in_specs=[pl.BlockSpec(memory_space=pltpu.SMEM)]
        + [vmem] * 3
        + [pl.BlockSpec(memory_space=pl.ANY)] * len(use),
        out_specs=vmem,
        scratch_shapes=[
            pltpu.VMEM((rows, 2 * half + WINDOW), jnp.float32),
            pltpu.VMEM((depth // size, size, cdev), jnp.bfloat16),
            pltpu.SemaphoreType.DMA((depth // size,)),
        ],
        out_shape=jax.ShapeDtypeStruct((rows, cdev), jnp.bfloat16),
        compiler_params=pltpu.CompilerParams(vmem_limit_bytes=VMEM),
        cost_estimate=pl.CostEstimate(
            flops=2 * rows * depth * cdev, bytes_accessed=2 * depth * cdev, transcendentals=0
        ),
    )(scalars, mine, other, gains, *weights)


def attend_kernel(steps, brow, kvlocal, groups, n_y, item_at, scalars, own, sent, spans, ckeys, cvals, wo, theirs, ours, attn, kheld, vheld, held, sems):
    rows = steps * brow
    length = ckeys.shape[1]
    scale = 1.0 / HDIM**0.5
    qdim = kvlocal * groups * HDIM
    kvdim = kvlocal * HDIM
    shard = held.shape[2]
    core = scalars[0]
    item = scalars[item_at]
    first = pl.multiple_of(item * brow, brow)
    gets = [
        pltpu.make_async_copy(ckeys.at[pl.ds(first, brow)], kheld, sems.at[2 * n_y]),
        pltpu.make_async_copy(cvals.at[pl.ds(first, brow)], vheld, sems.at[2 * n_y + 1]),
    ]
    for k in range(2 * n_y):
        side = 1 - core if k < n_y else core
        at = pl.multiple_of((k % n_y * 2 + side) * shard, shard)
        gets.append(
            pltpu.make_async_copy(wo.at[0, :, pl.ds(at, shard)], held.at[k], sems.at[k])
        )
    for get in gets:
        get.start()
    gets[0].wait()
    gets[1].wait()
    span = spans[item]

    qkv = (own[...].astype(jnp.float32) + sent[...].astype(jnp.float32)).astype(jnp.bfloat16)
    qkv = qkv.astype(jnp.float32)
    keys = kheld[...].reshape(brow * length, kvdim)
    values = vheld[...].reshape(brow * length, kvdim)
    tall = groups * rows
    at = lax.broadcasted_iota(jnp.int32, (tall, brow * length), 0)
    col = lax.broadcasted_iota(jnp.int32, (tall, brow * length), 1)
    cmask = (at % brow == col // length) & (col % length < span)
    at = lax.broadcasted_iota(jnp.int32, (tall, rows), 0)
    col = lax.broadcasted_iota(jnp.int32, (tall, rows), 1)
    nmask = (at % brow == col % brow) & (col // brow <= at % rows // brow)
    contract = (((1,), (1,)), ((), ()))
    for head in range(kvlocal):
        lanes = slice(head * HDIM, (head + 1) * HDIM)
        first = head * groups * HDIM
        query = jnp.concatenate(
            [qkv[:, first + g * HDIM : first + (g + 1) * HDIM] for g in range(groups)], axis=0
        ).astype(jnp.bfloat16)
        at = qdim + head * HDIM
        knew = qkv[:, at : at + HDIM].astype(jnp.bfloat16)
        at = at + kvdim
        vnew = qkv[:, at : at + HDIM].astype(jnp.bfloat16)
        scache = scale * lax.dot_general(
            query, keys[:, lanes], contract, preferred_element_type=jnp.float32
        )
        snew = scale * lax.dot_general(
            query, knew, contract, preferred_element_type=jnp.float32
        )
        scache = jnp.where(cmask, scache, -1e30)
        snew = jnp.where(nmask, snew, -1e30)
        top = jnp.maximum(
            jnp.max(scache, axis=1, keepdims=True), jnp.max(snew, axis=1, keepdims=True)
        )
        ecache = jnp.where(cmask, jnp.exp(scache - top), 0.0)
        enew = jnp.where(nmask, jnp.exp(snew - top), 0.0)
        total = jnp.sum(ecache, axis=1, keepdims=True) + jnp.sum(enew, axis=1, keepdims=True)
        inverse = 1.0 / total
        wcache = (ecache * inverse).astype(jnp.bfloat16)
        wnew = (enew * inverse).astype(jnp.bfloat16)
        mixed = jnp.dot(wcache, values[:, lanes], preferred_element_type=jnp.float32)
        mixed = mixed + jnp.dot(wnew, vnew, preferred_element_type=jnp.float32)
        for g in range(groups):
            attn[:, first + g * HDIM : first + (g + 1) * HDIM] = mixed[
                g * rows : (g + 1) * rows
            ].astype(jnp.bfloat16)

    for k in range(2 * n_y):
        gets[2 + k].wait()
        product = jnp.dot(attn[...], held[k], preferred_element_type=jnp.float32)
        target = theirs if k < n_y else ours
        at = k % n_y * shard
        target[:, at : at + shard] = product.astype(jnp.bfloat16)


def attend(item_at, steps, brow, n_y, scalars, own, sent, spans, keys, values, wo):
    rows, cdev = own.shape
    _, qdim, width = wo.shape
    length, kvdim = keys.shape[1:]
    kvlocal = kvdim // HDIM
    groups = qdim // kvdim
    shard = width // (2 * n_y)
    vmem = pl.BlockSpec(memory_space=pltpu.VMEM)
    return pl.pallas_call(
        functools.partial(attend_kernel, steps, brow, kvlocal, groups, n_y, item_at),
        in_specs=[pl.BlockSpec(memory_space=pltpu.SMEM)]
        + [vmem] * 3
        + [pl.BlockSpec(memory_space=pl.ANY)] * 3,
        out_specs=[vmem] * 2,
        scratch_shapes=[
            pltpu.VMEM((rows, qdim), jnp.bfloat16),
            pltpu.VMEM((brow, length, kvdim), jnp.bfloat16),
            pltpu.VMEM((brow, length, kvdim), jnp.bfloat16),
            pltpu.VMEM((2 * n_y, qdim, shard), jnp.bfloat16),
            pltpu.SemaphoreType.DMA((2 * n_y + 2,)),
        ],
        out_shape=[jax.ShapeDtypeStruct((rows, shard * n_y), jnp.bfloat16)] * 2,
        compiler_params=pltpu.CompilerParams(vmem_limit_bytes=VMEM),
        cost_estimate=pl.CostEstimate(
            flops=2 * rows * qdim * width, bytes_accessed=2 * qdim * width, transcendentals=0
        ),
    )(scalars, own, sent, spans, keys, values, wo)


def per_device(
    trainer_tiles,
    tile_lengths,
    wo_rollout,
    cache_keys,
    cache_values,
    cache_lengths,
    norm_gain,
    step_inputs,
):
    n_zone = lax.axis_size("zone")
    n_spot = lax.axis_size("spot")
    n_tensor = lax.axis_size("tensor")
    layers = n_zone * n_spot
    tiles = n_spot * n_tensor
    n_y = n_tensor // 2
    slab, columns = trainer_tiles.shape
    cdev = columns // n_tensor
    tilew = slab // layers
    width = wo_rollout.shape[2]
    shard = width // n_tensor
    half = n_y * shard
    steps = step_inputs.shape[0]
    seqs, length = cache_keys.shape[1:3]
    n_item = STREAMS * ITEMS
    brow = seqs // n_item
    rows = steps * brow
    ticks = layers + ITEMS - 1
    zone = lax.axis_index("zone")
    spot = lax.axis_index("spot")
    tpos = lax.axis_index("tensor")
    core = tpos % 2
    layer = zone * n_spot + spot

    weights = []
    for phase in range(2):
        ordered = sort_slab(trainer_tiles, phase, layers, n_tensor)
        arrived = lax.all_to_all(
            ordered.reshape(tiles, tilew, cdev),
            ("spot", "tensor"),
            split_axis=0,
            concat_axis=0,
            tiled=True,
        )
        weights.append(arrived.reshape(tiles * tilew, cdev))

    ends = jnp.cumsum(tile_lengths)
    starts = lax.dynamic_slice_in_dim(ends - tile_lengths, zone * tiles, tiles)
    counts = lax.dynamic_slice_in_dim(tile_lengths, zone * tiles, tiles)
    tick_ids = jnp.arange(ticks, dtype=jnp.int32)
    phases = (tick_ids >= spot + n_spot).astype(jnp.int32)
    turns = jnp.clip(tick_ids - layer, 0, ITEMS - 1)
    turns = jnp.concatenate([turns + stream * ITEMS for stream in range(STREAMS)])
    scalars = jnp.concatenate([core[None], phases, turns, starts, counts]).astype(jnp.int32)
    flip = [(z, 1 - z) for z in range(2)]
    swapped = lax.ppermute(norm_gain, "zone", flip)
    gains = jnp.concatenate(
        [jnp.where(zone == 0, norm_gain, swapped), jnp.where(zone == 0, swapped, norm_gain)]
    )
    spans = jnp.repeat(cache_lengths, length).reshape(n_item, 1, brow * length)
    axes = ("zone", "spot", "tensor")

    flat = [(z, s) for z in range(n_zone) for s in range(n_spot)]

    def shifted(turn):
        pairs = []
        for z, s in flat:
            nearby = (s + 1) % n_spot
            ahead = z if s + 1 < n_spot else 1 - z
            pairs.append((z * n_spot + s, (ahead ^ turn) * n_spot + nearby))
        return pairs

    hops = [shifted(turn) for turn in range(2)]

    def active(tick):
        return [l for l in range(layers) if 0 <= tick - l < ITEMS]

    across = [(t, t ^ 1) for t in range(n_tensor)]
    shown = step_inputs.reshape(steps, n_item, brow, n_y, 2, shard)
    records = []
    for stream in range(STREAMS):
        arrived, record = None, [jnp.zeros((rows, half), jnp.float32)] * ITEMS
        for tick in range(ticks):
            busy = active(tick)
            if tick < ITEMS:
                item = stream * ITEMS + tick
                fresh = shown[:, item].reshape(rows, n_y, 2, shard)
                mine = lax.dynamic_index_in_dim(fresh, core, 2, False).reshape(rows, half)
                mine = jnp.where(spot == 0, mine, arrived if tick else 0)
            else:
                mine = arrived
            if tick:
                other = lax.ppermute(mine, "tensor", across)
            else:
                other = lax.dynamic_index_in_dim(fresh, 1 - core, 2, False).reshape(rows, half)
            use = sorted({l // n_spot for l in busy})
            own = project(
                tick, use, tiles, tilew, n_y, scalars, mine, other, gains, [weights[p] for p in use]
            )
            sent = lax.ppermute(own, "zone", flip)
            item_at = 1 + ticks + stream * ticks + tick
            theirs, ours = attend(
                item_at, steps, brow, n_y, scalars, own, sent, spans, cache_keys[0], cache_values[0], wo_rollout
            )
            part = ours.astype(jnp.float32) + lax.ppermute(theirs, "tensor", across).astype(
                jnp.float32
            )
            bit = 2
            while bit < n_tensor:
                part = part.astype(jnp.bfloat16)
                moved = lax.ppermute(part, "tensor", [(t, t ^ bit) for t in range(n_tensor)])
                part = part.astype(jnp.float32) + moved.astype(jnp.float32)
                bit = bit * 2
            wide = mine.astype(jnp.float32) + part
            for item in range(ITEMS):
                record[item] = jnp.where(layer == tick - item, wide, record[item])
            after = wide.astype(jnp.bfloat16)
            if tick + 1 < ticks:
                at_home = phases[tick + 1] == zone
                near = lax.ppermute(after, ("zone", "spot"), hops[0])
                far = lax.ppermute(after, ("zone", "spot"), hops[1])
                arrived = jnp.where(at_home, near, far)
        for value in record:
            value = lax.dynamic_slice_in_dim(value, tpos // 2 * shard, shard, 1)
            records.append(value.reshape(steps, brow, shard))
    return jnp.concatenate(records, axis=1)[None]


def solution(mesh):
    n_section, n_tensor = mesh.devices.shape
    fine = Mesh(mesh.devices.reshape(2, n_section // 2, n_tensor), ("zone", "spot", "tensor"))
    section = ("zone", "spot")
    placed = (
        P(("zone", "spot", "tensor"), None),
        P(),
        P(section, "tensor", None),
        P(section, None, None, "tensor"),
        P(section, None, None, "tensor"),
        P(),
        P(section, None),
        P(),
    )
    return jax.shard_map(
        per_device,
        mesh=fine,
        in_specs=placed,
        out_specs=P(section, None, None, "tensor"),
        check_vma=False,
    )
```

```python
import functools

import jax
import jax.numpy as jnp
import numpy as np
from jax import lax
from jax.experimental import pallas as pl
from jax.experimental.pallas import tpu as pltpu
from jax.sharding import Mesh, PartitionSpec as P

HDIM = 128
FB = 8
STREAMS = 1
ITEMS = 2
ROWBLOCK = 256
CHUNK = 384
WINDOW = 512
VMEM = 48 * 1024 * 1024


def sort_kernel(first, layers, place, slab, *outs):
    feats = ROWBLOCK // layers
    shape = (len(outs) * feats, ROWBLOCK)
    row = lax.broadcasted_iota(jnp.int32, shape, 0)
    col = lax.broadcasted_iota(jnp.int32, shape, 1)
    source = row % feats * layers + first + ((row // feats) ^ place[0])
    order = jnp.where(col == source, 1.0, 0.0).astype(jnp.bfloat16)
    moved = jnp.dot(order, slab[...], preferred_element_type=jnp.float32).astype(jnp.bfloat16)
    for n, out in enumerate(outs):
        out[...] = moved[n * feats : (n + 1) * feats]


def sort_slab(slab, phase, layers, n_tensor, turn, place):
    rows, columns = slab.shape
    kept = layers // 2
    cdev = columns // n_tensor
    feats = ROWBLOCK // layers
    return pl.pallas_call(
        functools.partial(sort_kernel, phase * kept, layers),
        grid_spec=pltpu.PrefetchScalarGridSpec(
            num_scalar_prefetch=1,
            grid=(rows // ROWBLOCK,),
            in_specs=[pl.BlockSpec((ROWBLOCK, cdev), lambda i, s: (i, s[1] ^ turn))],
            out_specs=[pl.BlockSpec((feats, cdev), lambda i, s: (i, 0))] * kept,
        ),
        out_shape=[jax.ShapeDtypeStruct((rows // layers, cdev), jnp.bfloat16)] * kept,
        compiler_params=pltpu.CompilerParams(vmem_limit_bytes=VMEM),
        cost_estimate=pl.CostEstimate(
            flops=rows * cdev * ROWBLOCK, bytes_accessed=3 * rows * cdev, transcendentals=0
        ),
    )(place, slab)


def project_kernel(tick, tiles, tilew, n_y, use, scalars, mine, other, gains, *rest):
    weights, (out, normed, held, sems) = rest[:-4], rest[-4:]
    rows, half = mine.shape
    width = 2 * half
    shard = half // n_y
    chunks, size, cdev = held.shape
    per = size // tilew
    core, phase = scalars[0], scalars[1 + tick]

    def fetch(p, n):
        target = held.at[n // per, pl.ds(n % per * tilew, tilew)]
        return pltpu.make_async_copy(weights[p * tiles + n], target, sems.at[n])

    if len(use) == 1:
        for n in range(tiles):
            fetch(0, n).start()
    else:
        for p in range(2):

            @pl.when(phase == p)
            def _():
                for n in range(tiles):
                    fetch(p, n).start()

    here = mine[...].astype(jnp.float32)
    there = other[...].astype(jnp.float32)
    total = jnp.sum(here * here, axis=1, keepdims=True)
    total = total + jnp.sum(there * there, axis=1, keepdims=True)
    inverse = lax.rsqrt(total / width + 1e-06)
    gain = jnp.where(phase == 0, gains[0:1], gains[1:2])
    low = jnp.where(core == 0, here, there) * inverse
    high = jnp.where(core == 0, there, here) * inverse
    for y in range(n_y):
        at = 2 * y * shard
        piece = slice(y * shard, (y + 1) * shard)
        normed[:, at : at + shard] = low[:, piece] * gain[:, at : at + shard]
        at = at + shard
        normed[:, at : at + shard] = high[:, piece] * gain[:, at : at + shard]
    normed[:, width:] = jnp.zeros((rows, WINDOW), jnp.float32)

    along = CHUNK // tilew
    base = scalars.shape[0] - 2 * tiles
    lane = lax.broadcasted_iota(jnp.int32, (rows, CHUNK), 1)

    def spread(j):
        value = jnp.zeros((rows, CHUNK), jnp.float32)
        for a in range(along):
            start = scalars[base + j * along + a] * FB
            count = scalars[base + tiles + j * along + a] * FB
            aligned = start // 128 * 128
            window = normed[:, pl.ds(pl.multiple_of(aligned, 128), WINDOW)]
            put = a * tilew
            shift = (put - (start - aligned) + WINDOW) % WINDOW
            rolled = pltpu.roll(window, shift, 1)[:, :CHUNK]
            value = jnp.where((lane >= put) & (lane < put + count), rolled, value)
        return value.astype(jnp.bfloat16)

    acc = jnp.zeros((rows, cdev), jnp.float32)
    for j in range(chunks):
        parts = [spread(j * (size // CHUNK) + i) for i in range(size // CHUNK)]
        for n in range(j * per, (j + 1) * per):
            fetch(0, n).wait()
        acc = acc + jnp.dot(
            jnp.concatenate(parts, axis=1), held[j], preferred_element_type=jnp.float32
        )
    out[...] = acc.astype(jnp.bfloat16)


def project(tick, use, tiles, tilew, n_y, scalars, mine, other, gains, weights):
    rows, half = mine.shape
    cdev = weights[0].shape[1]
    depth = tiles * tilew
    size = 2 * CHUNK
    vmem = pl.BlockSpec(memory_space=pltpu.VMEM)
    return pl.pallas_call(
        functools.partial(project_kernel, tick, tiles, tilew, n_y, use),
        in_specs=[pl.BlockSpec(memory_space=pltpu.SMEM)]
        + [vmem] * 3
        + [pl.BlockSpec(memory_space=pl.ANY)] * len(weights),
        out_specs=vmem,
        scratch_shapes=[
            pltpu.VMEM((rows, 2 * half + WINDOW), jnp.float32),
            pltpu.VMEM((depth // size, size, cdev), jnp.bfloat16),
            pltpu.SemaphoreType.DMA((tiles,)),
        ],
        out_shape=jax.ShapeDtypeStruct((rows, cdev), jnp.bfloat16),
        compiler_params=pltpu.CompilerParams(vmem_limit_bytes=VMEM),
        cost_estimate=pl.CostEstimate(
            flops=2 * rows * depth * cdev, bytes_accessed=2 * depth * cdev, transcendentals=0
        ),
    )(scalars, mine, other, gains, *weights)


def attend_kernel(steps, brow, kvlocal, groups, n_y, item_at, scalars, own, sent, spans, ckeys, cvals, wo, theirs, ours, attn, kheld, vheld, held, sems):
    rows = steps * brow
    length = ckeys.shape[1]
    scale = 1.0 / HDIM**0.5
    qdim = kvlocal * groups * HDIM
    kvdim = kvlocal * HDIM
    shard = held.shape[2]
    core = scalars[0]
    item = scalars[item_at]
    first = pl.multiple_of(item * brow, brow)
    gets = [
        pltpu.make_async_copy(ckeys.at[pl.ds(first, brow)], kheld, sems.at[2 * n_y]),
        pltpu.make_async_copy(cvals.at[pl.ds(first, brow)], vheld, sems.at[2 * n_y + 1]),
    ]
    for k in range(2 * n_y):
        side = 1 - core if k < n_y else core
        at = pl.multiple_of((k % n_y * 2 + side) * shard, shard)
        gets.append(
            pltpu.make_async_copy(wo.at[0, :, pl.ds(at, shard)], held.at[k], sems.at[k])
        )
    for get in gets:
        get.start()
    gets[0].wait()
    gets[1].wait()
    span = spans[item]

    qkv = (own[...].astype(jnp.float32) + sent[...].astype(jnp.float32)).astype(jnp.bfloat16)
    qkv = qkv.astype(jnp.float32)
    keys = kheld[...].reshape(brow * length, kvdim)
    values = vheld[...].reshape(brow * length, kvdim)
    tall = groups * rows
    at = lax.broadcasted_iota(jnp.int32, (tall, brow * length), 0)
    col = lax.broadcasted_iota(jnp.int32, (tall, brow * length), 1)
    cmask = (at % brow == col // length) & (col % length < span)
    at = lax.broadcasted_iota(jnp.int32, (tall, rows), 0)
    col = lax.broadcasted_iota(jnp.int32, (tall, rows), 1)
    nmask = (at % brow == col % brow) & (col // brow <= at % rows // brow)
    contract = (((1,), (1,)), ((), ()))
    for head in range(kvlocal):
        lanes = slice(head * HDIM, (head + 1) * HDIM)
        first = head * groups * HDIM
        query = jnp.concatenate(
            [qkv[:, first + g * HDIM : first + (g + 1) * HDIM] for g in range(groups)], axis=0
        ).astype(jnp.bfloat16)
        at = qdim + head * HDIM
        knew = qkv[:, at : at + HDIM].astype(jnp.bfloat16)
        at = at + kvdim
        vnew = qkv[:, at : at + HDIM].astype(jnp.bfloat16)
        scache = scale * lax.dot_general(
            query, keys[:, lanes], contract, preferred_element_type=jnp.float32
        )
        snew = scale * lax.dot_general(
            query, knew, contract, preferred_element_type=jnp.float32
        )
        scache = jnp.where(cmask, scache, -1e30)
        snew = jnp.where(nmask, snew, -1e30)
        top = jnp.maximum(
            jnp.max(scache, axis=1, keepdims=True), jnp.max(snew, axis=1, keepdims=True)
        )
        ecache = jnp.where(cmask, jnp.exp(scache - top), 0.0)
        enew = jnp.where(nmask, jnp.exp(snew - top), 0.0)
        total = jnp.sum(ecache, axis=1, keepdims=True) + jnp.sum(enew, axis=1, keepdims=True)
        inverse = 1.0 / total
        wcache = (ecache * inverse).astype(jnp.bfloat16)
        wnew = (enew * inverse).astype(jnp.bfloat16)
        mixed = jnp.dot(wcache, values[:, lanes], preferred_element_type=jnp.float32)
        mixed = mixed + jnp.dot(wnew, vnew, preferred_element_type=jnp.float32)
        for g in range(groups):
            attn[:, first + g * HDIM : first + (g + 1) * HDIM] = mixed[
                g * rows : (g + 1) * rows
            ].astype(jnp.bfloat16)

    for k in range(2 * n_y):
        gets[2 + k].wait()
        product = jnp.dot(attn[...], held[k], preferred_element_type=jnp.float32)
        target = theirs if k < n_y else ours
        at = k % n_y * shard
        target[:, at : at + shard] = product.astype(jnp.bfloat16)


def attend(item_at, steps, brow, n_y, scalars, own, sent, spans, keys, values, wo):
    rows, cdev = own.shape
    _, qdim, width = wo.shape
    length, kvdim = keys.shape[1:]
    kvlocal = kvdim // HDIM
    groups = qdim // kvdim
    shard = width // (2 * n_y)
    vmem = pl.BlockSpec(memory_space=pltpu.VMEM)
    return pl.pallas_call(
        functools.partial(attend_kernel, steps, brow, kvlocal, groups, n_y, item_at),
        in_specs=[pl.BlockSpec(memory_space=pltpu.SMEM)]
        + [vmem] * 3
        + [pl.BlockSpec(memory_space=pl.ANY)] * 3,
        out_specs=[vmem] * 2,
        scratch_shapes=[
            pltpu.VMEM((rows, qdim), jnp.bfloat16),
            pltpu.VMEM((brow, length, kvdim), jnp.bfloat16),
            pltpu.VMEM((brow, length, kvdim), jnp.bfloat16),
            pltpu.VMEM((2 * n_y, qdim, shard), jnp.bfloat16),
            pltpu.SemaphoreType.DMA((2 * n_y + 2,)),
        ],
        out_shape=[jax.ShapeDtypeStruct((rows, shard * n_y), jnp.bfloat16)] * 2,
        compiler_params=pltpu.CompilerParams(vmem_limit_bytes=VMEM),
        cost_estimate=pl.CostEstimate(
            flops=2 * rows * qdim * width, bytes_accessed=2 * qdim * width, transcendentals=0
        ),
    )(scalars, own, sent, spans, keys, values, wo)


def per_device(
    trainer_tiles,
    tile_lengths,
    wo_rollout,
    cache_keys,
    cache_values,
    cache_lengths,
    norm_gain,
    step_inputs,
):
    n_zone = lax.axis_size("zone")
    n_spot = lax.axis_size("spot")
    n_tensor = lax.axis_size("tensor")
    layers = n_zone * n_spot
    tiles = n_spot * n_tensor
    n_y = n_tensor // 2
    slab, columns = trainer_tiles.shape
    cdev = columns // n_tensor
    tilew = slab // layers
    width = wo_rollout.shape[2]
    shard = width // n_tensor
    half = n_y * shard
    steps = step_inputs.shape[0]
    seqs, length = cache_keys.shape[1:3]
    n_item = STREAMS * ITEMS
    brow = seqs // n_item
    rows = steps * brow
    ticks = layers + ITEMS - 1
    zone = lax.axis_index("zone")
    spot = lax.axis_index("spot")
    tpos = lax.axis_index("tensor")
    core = tpos % 2
    layer = zone * n_spot + spot

    turns = sorted(range(n_tensor), key=lambda kt: (kt < 2, kt))
    offsets = [(ks, kt) for kt in turns for ks in range(n_spot)]
    place = jnp.stack([spot, tpos]).astype(jnp.int32)
    weights = []
    for phase in range(2):
        pieces = []
        for kt in turns:
            sorted_pieces = sort_slab(trainer_tiles, phase, layers, n_tensor, kt, place)
            for ks, piece in enumerate(sorted_pieces):
                pairs = [
                    (s * n_tensor + t, (s ^ ks) * n_tensor + (t ^ kt))
                    for s in range(n_spot)
                    for t in range(n_tensor)
                ]
                if ks or kt:
                    piece = lax.ppermute(piece, ("spot", "tensor"), pairs)
                pieces.append(piece)
        weights.append(pieces)

    ends = jnp.cumsum(tile_lengths)
    offset = np.array(offsets, np.int32)
    sources = (offset[:, 0] ^ spot) * n_tensor + (offset[:, 1] ^ tpos) + zone * tiles
    starts = (ends - tile_lengths)[sources]
    counts = tile_lengths[sources]
    tick_ids = jnp.arange(ticks, dtype=jnp.int32)
    phases = (tick_ids >= spot + n_spot).astype(jnp.int32)
    turns = jnp.clip(tick_ids - layer, 0, ITEMS - 1)
    turns = jnp.concatenate([turns + stream * ITEMS for stream in range(STREAMS)])
    scalars = jnp.concatenate([core[None], phases, turns, starts, counts]).astype(jnp.int32)
    flip = [(z, 1 - z) for z in range(2)]
    swapped = lax.ppermute(norm_gain, "zone", flip)
    gains = jnp.concatenate(
        [jnp.where(zone == 0, norm_gain, swapped), jnp.where(zone == 0, swapped, norm_gain)]
    )
    spans = jnp.repeat(cache_lengths, length).reshape(n_item, 1, brow * length)
    axes = ("zone", "spot", "tensor")

    def spots(tick):
        return sorted({(tick - i) % n_spot for i in range(ITEMS)})

    def hop(tick, turn):
        pairs = []
        for s in spots(tick):
            for z in range(n_zone):
                ahead = z if s + 1 < n_spot else 1 - z
                pairs.append((z * n_spot + s, (ahead ^ turn) * n_spot + (s + 1) % n_spot))
        return sorted(pairs)

    def mirror(tick):
        return sorted(
            (z * n_spot + s, (1 - z) * n_spot + s) for s in spots(tick) for z in range(n_zone)
        )

    def active(tick):
        return [l for l in range(layers) if 0 <= tick - l < ITEMS]

    across = [(t, t ^ 1) for t in range(n_tensor)]
    shown = step_inputs.reshape(steps, n_item, brow, n_y, 2, shard)
    records = []
    for stream in range(STREAMS):
        arrived, record = None, [jnp.zeros((rows, half), jnp.float32)] * ITEMS
        for tick in range(ticks):
            busy = active(tick)
            if tick < ITEMS:
                item = stream * ITEMS + tick
                fresh = shown[:, item].reshape(rows, n_y, 2, shard)
                mine = lax.dynamic_index_in_dim(fresh, core, 2, False).reshape(rows, half)
                mine = jnp.where(spot == 0, mine, arrived if tick else 0)
            else:
                mine = arrived
            if tick:
                other = lax.ppermute(mine, "tensor", across)
            else:
                other = lax.dynamic_index_in_dim(fresh, 1 - core, 2, False).reshape(rows, half)
            use = sorted({l // n_spot for l in busy})
            own = project(
                tick, use, tiles, tilew, n_y, scalars, mine, other, gains, sum([weights[p] for p in use], [])
            )
            sent = lax.ppermute(own, ("zone", "spot"), mirror(tick))
            item_at = 1 + ticks + stream * ticks + tick
            theirs, ours = attend(
                item_at, steps, brow, n_y, scalars, own, sent, spans, cache_keys[0], cache_values[0], wo_rollout
            )
            part = ours.astype(jnp.float32) + lax.ppermute(theirs, "tensor", across).astype(
                jnp.float32
            )
            bit = 2
            while bit < n_tensor:
                part = part.astype(jnp.bfloat16)
                moved = lax.ppermute(part, "tensor", [(t, t ^ bit) for t in range(n_tensor)])
                part = part.astype(jnp.float32) + moved.astype(jnp.float32)
                bit = bit * 2
            wide = mine.astype(jnp.float32) + part
            for item in range(ITEMS):
                record[item] = jnp.where(layer == tick - item, wide, record[item])
            after = wide.astype(jnp.bfloat16)
            if tick + 1 < ticks:
                at_home = phases[tick + 1] == zone
                near = lax.ppermute(after, ("zone", "spot"), hop(tick, 0))
                far = lax.ppermute(after, ("zone", "spot"), hop(tick, 1))
                arrived = jnp.where(at_home, near, far)
        for value in record:
            value = lax.dynamic_slice_in_dim(value, tpos // 2 * shard, shard, 1)
            records.append(value.reshape(steps, brow, shard))
    return jnp.concatenate(records, axis=1)[None]


def solution(mesh):
    n_section, n_tensor = mesh.devices.shape
    fine = Mesh(mesh.devices.reshape(2, n_section // 2, n_tensor), ("zone", "spot", "tensor"))
    section = ("zone", "spot")
    placed = (
        P(("zone", "spot", "tensor"), None),
        P(),
        P(section, "tensor", None),
        P(section, None, None, "tensor"),
        P(section, None, None, "tensor"),
        P(),
        P(section, None),
        P(),
    )
    return jax.shard_map(
        per_device,
        mesh=fine,
        in_specs=placed,
        out_specs=P(section, None, None, "tensor"),
        check_vma=False,
    )
```

```python
import functools

import jax
import jax.numpy as jnp
import numpy as np
from jax import lax
from jax.experimental import pallas as pl
from jax.experimental.pallas import tpu as pltpu
from jax.sharding import Mesh, PartitionSpec as P

HDIM = 128
FB = 8
STREAMS = 1
ITEMS = 2
ROWBLOCK = 256
CHUNK = 384
WINDOW = 512
VMEM = 48 * 1024 * 1024


def sort_kernel(first, layers, place, slab, *outs):
    feats = ROWBLOCK // layers
    shape = (len(outs) * feats, ROWBLOCK)
    row = lax.broadcasted_iota(jnp.int32, shape, 0)
    col = lax.broadcasted_iota(jnp.int32, shape, 1)
    source = row % feats * layers + first + ((row // feats) ^ place[0])
    order = jnp.where(col == source, 1.0, 0.0).astype(jnp.bfloat16)
    moved = jnp.dot(order, slab[...], preferred_element_type=jnp.float32).astype(jnp.bfloat16)
    for n, out in enumerate(outs):
        out[...] = moved[n * feats : (n + 1) * feats]


def sort_slab(slab, phase, layers, n_tensor, turn, place):
    rows, columns = slab.shape
    kept = layers // 2
    cdev = columns // n_tensor
    feats = ROWBLOCK // layers
    return pl.pallas_call(
        functools.partial(sort_kernel, phase * kept, layers),
        grid_spec=pltpu.PrefetchScalarGridSpec(
            num_scalar_prefetch=1,
            grid=(rows // ROWBLOCK,),
            in_specs=[pl.BlockSpec((ROWBLOCK, cdev), lambda i, s: (i, s[1] ^ turn))],
            out_specs=[pl.BlockSpec((feats, cdev), lambda i, s: (i, 0))] * kept,
        ),
        out_shape=[jax.ShapeDtypeStruct((rows // layers, cdev), jnp.bfloat16)] * kept,
        compiler_params=pltpu.CompilerParams(vmem_limit_bytes=VMEM),
        cost_estimate=pl.CostEstimate(
            flops=rows * cdev * ROWBLOCK, bytes_accessed=3 * rows * cdev, transcendentals=0
        ),
    )(place, slab)


def project_kernel(tick, tiles, tilew, n_y, use, scalars, mine, other, gains, *rest):
    weights, (out, normed, held, sems) = rest[:-4], rest[-4:]
    rows, half = mine.shape
    width = 2 * half
    shard = half // n_y
    chunks, size, cdev = held.shape
    per = size // tilew
    core, phase = scalars[0], scalars[1 + tick]

    def fetch(p, n):
        target = held.at[n // per, pl.ds(n % per * tilew, tilew)]
        return pltpu.make_async_copy(weights[p * tiles + n], target, sems.at[n])

    if len(use) == 1:
        for n in range(tiles):
            fetch(0, n).start()
    else:
        for p in range(2):

            @pl.when(phase == p)
            def _():
                for n in range(tiles):
                    fetch(p, n).start()

    here = mine[...].astype(jnp.float32)
    there = other[...].astype(jnp.float32)
    total = jnp.sum(here * here, axis=1, keepdims=True)
    total = total + jnp.sum(there * there, axis=1, keepdims=True)
    inverse = lax.rsqrt(total / width + 1e-06)
    gain = jnp.where(phase == 0, gains[0:1], gains[1:2])
    low = jnp.where(core == 0, here, there) * inverse
    high = jnp.where(core == 0, there, here) * inverse
    for y in range(n_y):
        at = 2 * y * shard
        piece = slice(y * shard, (y + 1) * shard)
        normed[:, at : at + shard] = low[:, piece] * gain[:, at : at + shard]
        at = at + shard
        normed[:, at : at + shard] = high[:, piece] * gain[:, at : at + shard]
    normed[:, width:] = jnp.zeros((rows, WINDOW), jnp.float32)

    along = CHUNK // tilew
    base = scalars.shape[0] - 2 * tiles
    lane = lax.broadcasted_iota(jnp.int32, (rows, CHUNK), 1)

    def spread(j):
        value = jnp.zeros((rows, CHUNK), jnp.float32)
        for a in range(along):
            start = scalars[base + j * along + a] * FB
            count = scalars[base + tiles + j * along + a] * FB
            aligned = start // 128 * 128
            window = normed[:, pl.ds(pl.multiple_of(aligned, 128), WINDOW)]
            put = a * tilew
            shift = (put - (start - aligned) + WINDOW) % WINDOW
            rolled = pltpu.roll(window, shift, 1)[:, :CHUNK]
            value = jnp.where((lane >= put) & (lane < put + count), rolled, value)
        return value.astype(jnp.bfloat16)

    acc = jnp.zeros((rows, cdev), jnp.float32)
    for j in range(chunks):
        parts = [spread(j * (size // CHUNK) + i) for i in range(size // CHUNK)]
        for n in range(j * per, (j + 1) * per):
            fetch(0, n).wait()
        acc = acc + jnp.dot(
            jnp.concatenate(parts, axis=1), held[j], preferred_element_type=jnp.float32
        )
    out[...] = acc.astype(jnp.bfloat16)


def project(tick, use, tiles, tilew, n_y, scalars, mine, other, gains, weights):
    rows, half = mine.shape
    cdev = weights[0].shape[1]
    depth = tiles * tilew
    size = 2 * CHUNK
    vmem = pl.BlockSpec(memory_space=pltpu.VMEM)
    return pl.pallas_call(
        functools.partial(project_kernel, tick, tiles, tilew, n_y, use),
        in_specs=[pl.BlockSpec(memory_space=pltpu.SMEM)]
        + [vmem] * 3
        + [pl.BlockSpec(memory_space=pl.ANY)] * len(weights),
        out_specs=vmem,
        scratch_shapes=[
            pltpu.VMEM((rows, 2 * half + WINDOW), jnp.float32),
            pltpu.VMEM((depth // size, size, cdev), jnp.bfloat16),
            pltpu.SemaphoreType.DMA((tiles,)),
        ],
        out_shape=jax.ShapeDtypeStruct((rows, cdev), jnp.bfloat16),
        compiler_params=pltpu.CompilerParams(vmem_limit_bytes=VMEM),
        cost_estimate=pl.CostEstimate(
            flops=2 * rows * depth * cdev, bytes_accessed=2 * depth * cdev, transcendentals=0
        ),
    )(scalars, mine, other, gains, *weights)


def attend_kernel(steps, brow, kvlocal, groups, n_y, item_at, scalars, own, sent, spans, ckeys, cvals, wo, theirs, ours, attn, kheld, vheld, held, sems):
    rows = steps * brow
    length = ckeys.shape[1]
    scale = 1.0 / HDIM**0.5
    qdim = kvlocal * groups * HDIM
    kvdim = kvlocal * HDIM
    shard = held.shape[2]
    core = scalars[0]
    item = scalars[item_at]
    first = pl.multiple_of(item * brow, brow)
    gets = [
        pltpu.make_async_copy(ckeys.at[pl.ds(first, brow)], kheld, sems.at[2 * n_y]),
        pltpu.make_async_copy(cvals.at[pl.ds(first, brow)], vheld, sems.at[2 * n_y + 1]),
    ]
    for k in range(2 * n_y):
        side = 1 - core if k < n_y else core
        at = pl.multiple_of((k % n_y * 2 + side) * shard, shard)
        gets.append(
            pltpu.make_async_copy(wo.at[0, :, pl.ds(at, shard)], held.at[k], sems.at[k])
        )
    for get in gets:
        get.start()
    gets[0].wait()
    gets[1].wait()
    span = spans[item]

    qkv = (own[...].astype(jnp.float32) + sent[...].astype(jnp.float32)).astype(jnp.bfloat16)
    qkv = qkv.astype(jnp.float32)
    keys = kheld[...].reshape(brow * length, kvdim)
    values = vheld[...].reshape(brow * length, kvdim)
    tall = groups * rows
    at = lax.broadcasted_iota(jnp.int32, (tall, brow * length), 0)
    col = lax.broadcasted_iota(jnp.int32, (tall, brow * length), 1)
    cmask = (at % brow == col // length) & (col % length < span)
    at = lax.broadcasted_iota(jnp.int32, (tall, rows), 0)
    col = lax.broadcasted_iota(jnp.int32, (tall, rows), 1)
    nmask = (at % brow == col % brow) & (col // brow <= at % rows // brow)
    contract = (((1,), (1,)), ((), ()))
    for head in range(kvlocal):
        lanes = slice(head * HDIM, (head + 1) * HDIM)
        first = head * groups * HDIM
        query = jnp.concatenate(
            [qkv[:, first + g * HDIM : first + (g + 1) * HDIM] for g in range(groups)], axis=0
        ).astype(jnp.bfloat16)
        at = qdim + head * HDIM
        knew = qkv[:, at : at + HDIM].astype(jnp.bfloat16)
        at = at + kvdim
        vnew = qkv[:, at : at + HDIM].astype(jnp.bfloat16)
        scache = scale * lax.dot_general(
            query, keys[:, lanes], contract, preferred_element_type=jnp.float32
        )
        snew = scale * lax.dot_general(
            query, knew, contract, preferred_element_type=jnp.float32
        )
        scache = jnp.where(cmask, scache, -1e30)
        snew = jnp.where(nmask, snew, -1e30)
        top = jnp.maximum(
            jnp.max(scache, axis=1, keepdims=True), jnp.max(snew, axis=1, keepdims=True)
        )
        ecache = jnp.where(cmask, jnp.exp(scache - top), 0.0)
        enew = jnp.where(nmask, jnp.exp(snew - top), 0.0)
        total = jnp.sum(ecache, axis=1, keepdims=True) + jnp.sum(enew, axis=1, keepdims=True)
        inverse = 1.0 / total
        wcache = (ecache * inverse).astype(jnp.bfloat16)
        wnew = (enew * inverse).astype(jnp.bfloat16)
        mixed = jnp.dot(wcache, values[:, lanes], preferred_element_type=jnp.float32)
        mixed = mixed + jnp.dot(wnew, vnew, preferred_element_type=jnp.float32)
        for g in range(groups):
            attn[:, first + g * HDIM : first + (g + 1) * HDIM] = mixed[
                g * rows : (g + 1) * rows
            ].astype(jnp.bfloat16)

    for k in range(2 * n_y):
        gets[2 + k].wait()
        product = jnp.dot(attn[...], held[k], preferred_element_type=jnp.float32)
        target = theirs if k < n_y else ours
        at = k % n_y * shard
        target[:, at : at + shard] = product.astype(jnp.bfloat16)


def attend(item_at, steps, brow, n_y, scalars, own, sent, spans, keys, values, wo):
    rows, cdev = own.shape
    _, qdim, width = wo.shape
    length, kvdim = keys.shape[1:]
    kvlocal = kvdim // HDIM
    groups = qdim // kvdim
    shard = width // (2 * n_y)
    vmem = pl.BlockSpec(memory_space=pltpu.VMEM)
    return pl.pallas_call(
        functools.partial(attend_kernel, steps, brow, kvlocal, groups, n_y, item_at),
        in_specs=[pl.BlockSpec(memory_space=pltpu.SMEM)]
        + [vmem] * 3
        + [pl.BlockSpec(memory_space=pl.ANY)] * 3,
        out_specs=[vmem] * 2,
        scratch_shapes=[
            pltpu.VMEM((rows, qdim), jnp.bfloat16),
            pltpu.VMEM((brow, length, kvdim), jnp.bfloat16),
            pltpu.VMEM((brow, length, kvdim), jnp.bfloat16),
            pltpu.VMEM((2 * n_y, qdim, shard), jnp.bfloat16),
            pltpu.SemaphoreType.DMA((2 * n_y + 2,)),
        ],
        out_shape=[jax.ShapeDtypeStruct((rows, shard * n_y), jnp.bfloat16)] * 2,
        compiler_params=pltpu.CompilerParams(vmem_limit_bytes=VMEM),
        cost_estimate=pl.CostEstimate(
            flops=2 * rows * qdim * width, bytes_accessed=2 * qdim * width, transcendentals=0
        ),
    )(scalars, own, sent, spans, keys, values, wo)


def per_device(
    trainer_tiles,
    tile_lengths,
    wo_rollout,
    cache_keys,
    cache_values,
    cache_lengths,
    norm_gain,
    step_inputs,
):
    n_zone = lax.axis_size("zone")
    n_spot = lax.axis_size("spot")
    n_tensor = lax.axis_size("tensor")
    layers = n_zone * n_spot
    tiles = n_spot * n_tensor
    n_y = n_tensor // 2
    slab, columns = trainer_tiles.shape
    cdev = columns // n_tensor
    tilew = slab // layers
    width = wo_rollout.shape[2]
    shard = width // n_tensor
    half = n_y * shard
    steps = step_inputs.shape[0]
    seqs, length = cache_keys.shape[1:3]
    n_item = STREAMS * ITEMS
    brow = seqs // n_item
    rows = steps * brow
    ticks = layers + ITEMS - 1
    zone = lax.axis_index("zone")
    spot = lax.axis_index("spot")
    tpos = lax.axis_index("tensor")
    core = tpos % 2
    layer = zone * n_spot + spot

    all_s, all_t = n_spot - 1, n_tensor - 2
    turns = sorted(range(n_tensor), key=lambda kt: (kt % 2, kt))
    offsets = [(ks, kt) for kt in turns for ks in range(n_spot)]
    place = jnp.stack([spot ^ core * all_s, tpos ^ core * all_t]).astype(jnp.int32)

    def exchange(offset, piece):
        pairs = []
        for s in range(n_spot):
            for t in range(n_tensor):
                bits = 1 if offset == (all_s, all_t) else t % 2
                ks, kt = (0, 0) if offset == (all_s, all_t) else offset
                target = (s ^ ks ^ bits * all_s) * n_tensor + (t ^ kt ^ bits * all_t)
                pairs.append((s * n_tensor + t, target))
        return lax.ppermute(piece, ("spot", "tensor"), pairs)

    ordered, weights = [], []
    for phase in range(2):
        pieces = {}
        for kt in turns:
            for ks, piece in enumerate(
                sort_slab(trainer_tiles, phase, layers, n_tensor, kt, place)
            ):
                pieces[ks, kt] = piece
        first, last = pieces[0, 0], pieces[all_s, all_t]
        pieces[0, 0] = jnp.where(core == 0, first, last)
        pieces[all_s, all_t] = jnp.where(core == 0, last, first)
        ordered.append(pieces)
    moving = [offset for offset in offsets if offset != (0, 0)]
    early = len(moving) - 2 * min(n_spot, 4)
    got = [{(0, 0): ordered[p][0, 0]} for p in range(2)]
    for phase in range(2):
        for n, offset in enumerate(moving):
            if phase == 0 or n < early:
                got[phase][offset] = exchange(offset, ordered[phase][offset])
    late = moving[early:]

    ends = jnp.cumsum(tile_lengths)
    offset = np.array(offsets, np.int32)
    sender = (offset[:, 1] % 2) ^ core
    fixed = (offset == [0, 0]).all(axis=1) | (offset == [all_s, all_t]).all(axis=1)
    sender = jnp.where(fixed, 0, sender)
    sources = (offset[:, 0] ^ spot ^ sender * all_s) * n_tensor
    sources = sources + (offset[:, 1] ^ tpos ^ sender * all_t) + zone * tiles
    starts = (ends - tile_lengths)[sources]
    counts = tile_lengths[sources]
    tick_ids = jnp.arange(ticks, dtype=jnp.int32)
    phases = (tick_ids >= spot + n_spot).astype(jnp.int32)
    turns = jnp.clip(tick_ids - layer, 0, ITEMS - 1)
    turns = jnp.concatenate([turns + stream * ITEMS for stream in range(STREAMS)])
    scalars = jnp.concatenate([core[None], phases, turns, starts, counts]).astype(jnp.int32)
    flip = [(z, 1 - z) for z in range(2)]
    swapped = lax.ppermute(norm_gain, "zone", flip)
    gains = jnp.concatenate(
        [jnp.where(zone == 0, norm_gain, swapped), jnp.where(zone == 0, swapped, norm_gain)]
    )
    spans = jnp.repeat(cache_lengths, length).reshape(n_item, 1, brow * length)
    axes = ("zone", "spot", "tensor")

    def spots(tick):
        return sorted({(tick - i) % n_spot for i in range(ITEMS)})

    def hop(tick, turn):
        pairs = []
        for s in spots(tick):
            for z in range(n_zone):
                ahead = z if s + 1 < n_spot else 1 - z
                pairs.append((z * n_spot + s, (ahead ^ turn) * n_spot + (s + 1) % n_spot))
        return sorted(pairs)

    def mirror(tick):
        return sorted(
            (z * n_spot + s, (1 - z) * n_spot + s) for s in spots(tick) for z in range(n_zone)
        )

    def active(tick):
        return [l for l in range(layers) if 0 <= tick - l < ITEMS]

    across = [(t, t ^ 1) for t in range(n_tensor)]
    shown = step_inputs.reshape(steps, n_item, brow, n_y, 2, shard)
    records = []
    for stream in range(STREAMS):
        arrived, record = None, [jnp.zeros((rows, half), jnp.float32)] * ITEMS
        for tick in range(ticks):
            busy = active(tick)
            if tick < ITEMS:
                item = stream * ITEMS + tick
                fresh = shown[:, item].reshape(rows, n_y, 2, shard)
                mine = lax.dynamic_index_in_dim(fresh, core, 2, False).reshape(rows, half)
                mine = jnp.where(spot == 0, mine, arrived if tick else 0)
            else:
                mine = arrived
            if tick:
                other = lax.ppermute(mine, "tensor", across)
            else:
                other = lax.dynamic_index_in_dim(fresh, 1 - core, 2, False).reshape(rows, half)
            use = sorted({l // n_spot for l in busy})
            extra = []
            if late:
                offset = late.pop(0)
                if tick == 0:
                    held = [got[1][k] for k in moving[:early]]
                    mine, _ = lax.optimization_barrier((mine, held))
                piece, _ = lax.optimization_barrier((ordered[1][offset], other))
                got[1][offset] = exchange(offset, piece)
                extra.append(got[1][offset])
            weights = [[got[p].get(k) for k in offsets] for p in range(2)]
            own = project(
                tick, use, tiles, tilew, n_y, scalars, mine, other, gains, sum([weights[p] for p in use], [])
            )
            sent = lax.ppermute(own, ("zone", "spot"), mirror(tick))
            if extra:
                sent, _ = lax.optimization_barrier((sent, extra))
            beside = []
            if late:
                offset = late.pop(0)
                piece, _ = lax.optimization_barrier((ordered[1][offset], sent))
                got[1][offset] = exchange(offset, piece)
                beside.append(got[1][offset])
            item_at = 1 + ticks + stream * ticks + tick
            theirs, ours = attend(
                item_at, steps, brow, n_y, scalars, own, sent, spans, cache_keys[0], cache_values[0], wo_rollout
            )
            part = ours.astype(jnp.float32) + lax.ppermute(theirs, "tensor", across).astype(
                jnp.float32
            )
            bit = 2
            while bit < n_tensor:
                part = part.astype(jnp.bfloat16)
                moved = lax.ppermute(part, "tensor", [(t, t ^ bit) for t in range(n_tensor)])
                part = part.astype(jnp.float32) + moved.astype(jnp.float32)
                bit = bit * 2
            wide = mine.astype(jnp.float32) + part
            for item in range(ITEMS):
                record[item] = jnp.where(layer == tick - item, wide, record[item])
            after = wide.astype(jnp.bfloat16)
            if tick + 1 < ticks:
                at_home = phases[tick + 1] == zone
                near = lax.ppermute(after, ("zone", "spot"), hop(tick, 0))
                far = lax.ppermute(after, ("zone", "spot"), hop(tick, 1))
                arrived = jnp.where(at_home, near, far)
                if beside:
                    arrived, _ = lax.optimization_barrier((arrived, beside))
        for value in record:
            value = lax.dynamic_slice_in_dim(value, tpos // 2 * shard, shard, 1)
            records.append(value.reshape(steps, brow, shard))
    return jnp.concatenate(records, axis=1)[None]


def solution(mesh):
    n_section, n_tensor = mesh.devices.shape
    fine = Mesh(mesh.devices.reshape(2, n_section // 2, n_tensor), ("zone", "spot", "tensor"))
    section = ("zone", "spot")
    placed = (
        P(("zone", "spot", "tensor"), None),
        P(),
        P(section, "tensor", None),
        P(section, None, None, "tensor"),
        P(section, None, None, "tensor"),
        P(),
        P(section, None),
        P(),
    )
    return jax.shard_map(
        per_device,
        mesh=fine,
        in_specs=placed,
        out_specs=P(section, None, None, "tensor"),
        check_vma=False,
    )
```

```python
import functools

import jax
import jax.numpy as jnp
import numpy as np
from jax import lax
from jax.experimental import pallas as pl
from jax.experimental.pallas import tpu as pltpu
from jax.sharding import Mesh, PartitionSpec as P

HDIM = 128
FB = 8
STREAMS = 1
ITEMS = 4
ROWBLOCK = 256
CHUNK = 384
WINDOW = 512
VMEM = 48 * 1024 * 1024


def sort_kernel(first, layers, place, slab, *outs):
    feats = ROWBLOCK // layers
    shape = (len(outs) * feats, ROWBLOCK)
    row = lax.broadcasted_iota(jnp.int32, shape, 0)
    col = lax.broadcasted_iota(jnp.int32, shape, 1)
    source = row % feats * layers + first + ((row // feats) ^ place[0])
    order = jnp.where(col == source, 1.0, 0.0).astype(jnp.bfloat16)
    moved = jnp.dot(order, slab[...], preferred_element_type=jnp.float32).astype(jnp.bfloat16)
    for n, out in enumerate(outs):
        out[...] = moved[n * feats : (n + 1) * feats]


def sort_slab(slab, phase, layers, n_tensor, turn, place):
    rows, columns = slab.shape
    kept = layers // 2
    cdev = columns // n_tensor
    feats = ROWBLOCK // layers
    return pl.pallas_call(
        functools.partial(sort_kernel, phase * kept, layers),
        grid_spec=pltpu.PrefetchScalarGridSpec(
            num_scalar_prefetch=1,
            grid=(rows // ROWBLOCK,),
            in_specs=[pl.BlockSpec((ROWBLOCK, cdev), lambda i, s: (i, s[1] ^ turn))],
            out_specs=[pl.BlockSpec((feats, cdev), lambda i, s: (i, 0))] * kept,
        ),
        out_shape=[jax.ShapeDtypeStruct((rows // layers, cdev), jnp.bfloat16)] * kept,
        compiler_params=pltpu.CompilerParams(vmem_limit_bytes=VMEM),
        cost_estimate=pl.CostEstimate(
            flops=rows * cdev * ROWBLOCK, bytes_accessed=3 * rows * cdev, transcendentals=0
        ),
    )(place, slab)


def project_kernel(tick, tiles, tilew, n_y, use, scalars, mine, other, gains, *rest):
    weights, (out, normed, held, sems) = rest[:-4], rest[-4:]
    rows, half = mine.shape
    width = 2 * half
    shard = half // n_y
    chunks, size, cdev = held.shape
    per = size // tilew
    core, phase = scalars[0], scalars[1 + tick]

    def fetch(p, n):
        target = held.at[n // per, pl.ds(n % per * tilew, tilew)]
        return pltpu.make_async_copy(weights[p * tiles + n], target, sems.at[n])

    if len(use) == 1:
        for n in range(tiles):
            fetch(0, n).start()
    else:
        for p in range(2):

            @pl.when(phase == p)
            def _():
                for n in range(tiles):
                    fetch(p, n).start()

    here = mine[...].astype(jnp.float32)
    there = other[...].astype(jnp.float32)
    total = jnp.sum(here * here, axis=1, keepdims=True)
    total = total + jnp.sum(there * there, axis=1, keepdims=True)
    inverse = lax.rsqrt(total / width + 1e-06)
    gain = jnp.where(phase == 0, gains[0:1], gains[1:2])
    low = jnp.where(core == 0, here, there) * inverse
    high = jnp.where(core == 0, there, here) * inverse
    for y in range(n_y):
        at = 2 * y * shard
        piece = slice(y * shard, (y + 1) * shard)
        normed[:, at : at + shard] = low[:, piece] * gain[:, at : at + shard]
        at = at + shard
        normed[:, at : at + shard] = high[:, piece] * gain[:, at : at + shard]
    normed[:, width:] = jnp.zeros((rows, WINDOW), jnp.float32)

    along = CHUNK // tilew
    base = scalars.shape[0] - 2 * tiles
    lane = lax.broadcasted_iota(jnp.int32, (rows, CHUNK), 1)

    def spread(j):
        value = jnp.zeros((rows, CHUNK), jnp.float32)
        for a in range(along):
            start = scalars[base + j * along + a] * FB
            count = scalars[base + tiles + j * along + a] * FB
            aligned = start // 128 * 128
            window = normed[:, pl.ds(pl.multiple_of(aligned, 128), WINDOW)]
            put = a * tilew
            shift = (put - (start - aligned) + WINDOW) % WINDOW
            rolled = pltpu.roll(window, shift, 1)[:, :CHUNK]
            value = jnp.where((lane >= put) & (lane < put + count), rolled, value)
        return value.astype(jnp.bfloat16)

    acc = jnp.zeros((rows, cdev), jnp.float32)
    for j in range(chunks):
        parts = [spread(j * (size // CHUNK) + i) for i in range(size // CHUNK)]
        for n in range(j * per, (j + 1) * per):
            fetch(0, n).wait()
        acc = acc + jnp.dot(
            jnp.concatenate(parts, axis=1), held[j], preferred_element_type=jnp.float32
        )
    out[...] = acc.astype(jnp.bfloat16)


def project(tick, use, tiles, tilew, n_y, scalars, mine, other, gains, weights):
    rows, half = mine.shape
    cdev = weights[0].shape[1]
    depth = tiles * tilew
    size = 2 * CHUNK
    vmem = pl.BlockSpec(memory_space=pltpu.VMEM)
    return pl.pallas_call(
        functools.partial(project_kernel, tick, tiles, tilew, n_y, use),
        in_specs=[pl.BlockSpec(memory_space=pltpu.SMEM)]
        + [vmem] * 3
        + [pl.BlockSpec(memory_space=pltpu.HBM)] * len(weights),
        out_specs=vmem,
        scratch_shapes=[
            pltpu.VMEM((rows, 2 * half + WINDOW), jnp.float32),
            pltpu.VMEM((depth // size, size, cdev), jnp.bfloat16),
            pltpu.SemaphoreType.DMA((tiles,)),
        ],
        out_shape=jax.ShapeDtypeStruct((rows, cdev), jnp.bfloat16),
        compiler_params=pltpu.CompilerParams(vmem_limit_bytes=VMEM),
        cost_estimate=pl.CostEstimate(
            flops=2 * rows * depth * cdev, bytes_accessed=2 * depth * cdev, transcendentals=0
        ),
    )(scalars, mine, other, gains, *weights)


def attend_kernel(steps, brow, kvlocal, groups, n_y, item_at, scalars, own, sent, spans, ckeys, cvals, wo, theirs, attn, kheld, vheld, held, sems):
    rows = steps * brow
    length = ckeys.shape[1]
    scale = 1.0 / HDIM**0.5
    qdim = kvlocal * groups * HDIM
    kvdim = kvlocal * HDIM
    shard = held.shape[2]
    core = scalars[0]
    item = scalars[item_at]
    first = pl.multiple_of(item * brow, brow)
    gets = [
        pltpu.make_async_copy(ckeys.at[pl.ds(first, brow)], kheld, sems.at[n_y]),
        pltpu.make_async_copy(cvals.at[pl.ds(first, brow)], vheld, sems.at[n_y + 1]),
    ]
    gets = gets + wo_copies(1 - core, wo, held, sems)
    for get in gets:
        get.start()
    gets[0].wait()
    gets[1].wait()
    span = spans[item]

    qkv = (own[...].astype(jnp.float32) + sent[...].astype(jnp.float32)).astype(jnp.bfloat16)
    qkv = qkv.astype(jnp.float32)
    keys = kheld[...].reshape(brow * length, kvdim)
    values = vheld[...].reshape(brow * length, kvdim)
    tall = groups * rows
    at = lax.broadcasted_iota(jnp.int32, (tall, brow * length), 0)
    col = lax.broadcasted_iota(jnp.int32, (tall, brow * length), 1)
    cmask = (at % brow == col // length) & (col % length < span)
    at = lax.broadcasted_iota(jnp.int32, (tall, rows), 0)
    col = lax.broadcasted_iota(jnp.int32, (tall, rows), 1)
    nmask = (at % brow == col % brow) & (col // brow <= at % rows // brow)
    contract = (((1,), (1,)), ((), ()))
    for head in range(kvlocal):
        lanes = slice(head * HDIM, (head + 1) * HDIM)
        first = head * groups * HDIM
        query = jnp.concatenate(
            [qkv[:, first + g * HDIM : first + (g + 1) * HDIM] for g in range(groups)], axis=0
        ).astype(jnp.bfloat16)
        at = qdim + head * HDIM
        knew = qkv[:, at : at + HDIM].astype(jnp.bfloat16)
        at = at + kvdim
        vnew = qkv[:, at : at + HDIM].astype(jnp.bfloat16)
        scache = scale * lax.dot_general(
            query, keys[:, lanes], contract, preferred_element_type=jnp.float32
        )
        snew = scale * lax.dot_general(
            query, knew, contract, preferred_element_type=jnp.float32
        )
        scache = jnp.where(cmask, scache, -1e30)
        snew = jnp.where(nmask, snew, -1e30)
        top = jnp.maximum(
            jnp.max(scache, axis=1, keepdims=True), jnp.max(snew, axis=1, keepdims=True)
        )
        ecache = jnp.where(cmask, jnp.exp(scache - top), 0.0)
        enew = jnp.where(nmask, jnp.exp(snew - top), 0.0)
        total = jnp.sum(ecache, axis=1, keepdims=True) + jnp.sum(enew, axis=1, keepdims=True)
        inverse = 1.0 / total
        wcache = (ecache * inverse).astype(jnp.bfloat16)
        wnew = (enew * inverse).astype(jnp.bfloat16)
        mixed = jnp.dot(wcache, values[:, lanes], preferred_element_type=jnp.float32)
        mixed = mixed + jnp.dot(wnew, vnew, preferred_element_type=jnp.float32)
        for g in range(groups):
            attn[:, first + g * HDIM : first + (g + 1) * HDIM] = mixed[
                g * rows : (g + 1) * rows
            ].astype(jnp.bfloat16)

    multiply(attn, gets[2:], held, theirs)


def wo_copies(side, wo, held, sems):
    n_y, _, shard = held.shape
    copies = []
    for y in range(n_y):
        at = pl.multiple_of((2 * y + side) * shard, shard)
        copies.append(
            pltpu.make_async_copy(wo.at[0, :, pl.ds(at, shard)], held.at[y], sems.at[y])
        )
    return copies


def multiply(attn, copies, held, out):
    shard = held.shape[2]
    for y, copy in enumerate(copies):
        copy.wait()
        product = jnp.dot(attn[...], held[y], preferred_element_type=jnp.float32)
        out[:, y * shard : (y + 1) * shard] = product.astype(jnp.bfloat16)


def finish_kernel(scalars, attn, wo, ours, held, sems):
    copies = wo_copies(scalars[0], wo, held, sems)
    for copy in copies:
        copy.start()
    multiply(attn, copies, held, ours)


def finish(n_y, scalars, attn, wo):
    rows, qdim = attn.shape
    width = wo.shape[2]
    shard = width // (2 * n_y)
    vmem = pl.BlockSpec(memory_space=pltpu.VMEM)
    return pl.pallas_call(
        finish_kernel,
        in_specs=[
            pl.BlockSpec(memory_space=pltpu.SMEM),
            vmem,
            pl.BlockSpec(memory_space=pltpu.HBM),
        ],
        out_specs=vmem,
        scratch_shapes=[
            pltpu.VMEM((n_y, qdim, shard), jnp.bfloat16),
            pltpu.SemaphoreType.DMA((n_y,)),
        ],
        out_shape=jax.ShapeDtypeStruct((rows, shard * n_y), jnp.bfloat16),
        compiler_params=pltpu.CompilerParams(vmem_limit_bytes=VMEM),
        cost_estimate=pl.CostEstimate(
            flops=rows * qdim * width, bytes_accessed=qdim * width, transcendentals=0
        ),
    )(scalars, attn, wo)


def attend(item_at, steps, brow, n_y, scalars, own, sent, spans, keys, values, wo):
    rows, cdev = own.shape
    _, qdim, width = wo.shape
    length, kvdim = keys.shape[1:]
    kvlocal = kvdim // HDIM
    groups = qdim // kvdim
    shard = width // (2 * n_y)
    vmem = pl.BlockSpec(memory_space=pltpu.VMEM)
    return pl.pallas_call(
        functools.partial(attend_kernel, steps, brow, kvlocal, groups, n_y, item_at),
        in_specs=[pl.BlockSpec(memory_space=pltpu.SMEM)]
        + [vmem] * 3
        + [pl.BlockSpec(memory_space=pltpu.HBM)] * 3,
        out_specs=[vmem] * 2,
        scratch_shapes=[
            pltpu.VMEM((brow, length, kvdim), jnp.bfloat16),
            pltpu.VMEM((brow, length, kvdim), jnp.bfloat16),
            pltpu.VMEM((n_y, qdim, shard), jnp.bfloat16),
            pltpu.SemaphoreType.DMA((n_y + 2,)),
        ],
        out_shape=[
            jax.ShapeDtypeStruct((rows, shard * n_y), jnp.bfloat16),
            jax.ShapeDtypeStruct((rows, qdim), jnp.bfloat16),
        ],
        compiler_params=pltpu.CompilerParams(vmem_limit_bytes=VMEM),
        cost_estimate=pl.CostEstimate(
            flops=rows * qdim * width, bytes_accessed=qdim * width, transcendentals=0
        ),
    )(scalars, own, sent, spans, keys, values, wo)


def per_device(
    trainer_tiles,
    tile_lengths,
    wo_rollout,
    cache_keys,
    cache_values,
    cache_lengths,
    norm_gain,
    step_inputs,
):
    n_zone = lax.axis_size("zone")
    n_spot = lax.axis_size("spot")
    n_tensor = lax.axis_size("tensor")
    layers = n_zone * n_spot
    tiles = n_spot * n_tensor
    n_y = n_tensor // 2
    slab, columns = trainer_tiles.shape
    cdev = columns // n_tensor
    tilew = slab // layers
    width = wo_rollout.shape[2]
    shard = width // n_tensor
    half = n_y * shard
    steps = step_inputs.shape[0]
    seqs, length = cache_keys.shape[1:3]
    n_item = STREAMS * ITEMS
    brow = seqs // n_item
    rows = steps * brow
    ticks = layers + ITEMS - 1
    zone = lax.axis_index("zone")
    spot = lax.axis_index("spot")
    tpos = lax.axis_index("tensor")
    core = tpos % 2
    layer = zone * n_spot + spot

    all_s, all_t = n_spot - 1, n_tensor - 2
    turns = sorted(range(n_tensor), key=lambda kt: (kt % 2, kt))
    offsets = [(ks, kt) for kt in turns for ks in range(n_spot)]
    place = jnp.stack([spot ^ core * all_s, tpos ^ core * all_t]).astype(jnp.int32)

    def exchange(offset, piece):
        pairs = []
        for s in range(n_spot):
            for t in range(n_tensor):
                bits = 1 if offset == (all_s, all_t) else t % 2
                ks, kt = (0, 0) if offset == (all_s, all_t) else offset
                target = (s ^ ks ^ bits * all_s) * n_tensor + (t ^ kt ^ bits * all_t)
                pairs.append((s * n_tensor + t, target))
        return lax.ppermute(piece, ("spot", "tensor"), pairs)

    ordered, weights = [], []
    for phase in range(2):
        pieces = {}
        for kt in turns:
            for ks, piece in enumerate(
                sort_slab(trainer_tiles, phase, layers, n_tensor, kt, place)
            ):
                pieces[ks, kt] = piece
        first, last = pieces[0, 0], pieces[all_s, all_t]
        pieces[0, 0] = jnp.where(core == 0, first, last)
        pieces[all_s, all_t] = jnp.where(core == 0, last, first)
        ordered.append(pieces)
    moving = [offset for offset in offsets if offset != (0, 0)]
    early = len(moving) - 2 * min(n_spot, 4)
    got = [{(0, 0): ordered[p][0, 0]} for p in range(2)]
    for phase in range(2):
        for n, offset in enumerate(moving):
            if phase == 0 or n < early:
                got[phase][offset] = exchange(offset, ordered[phase][offset])
    late = moving[early:]

    ends = jnp.cumsum(tile_lengths)
    offset = np.array(offsets, np.int32)
    sender = (offset[:, 1] % 2) ^ core
    fixed = (offset == [0, 0]).all(axis=1) | (offset == [all_s, all_t]).all(axis=1)
    sender = jnp.where(fixed, 0, sender)
    sources = (offset[:, 0] ^ spot ^ sender * all_s) * n_tensor
    sources = sources + (offset[:, 1] ^ tpos ^ sender * all_t) + zone * tiles
    starts = (ends - tile_lengths)[sources]
    counts = tile_lengths[sources]
    tick_ids = jnp.arange(ticks, dtype=jnp.int32)
    phases = (tick_ids >= spot + n_spot).astype(jnp.int32)
    turns = jnp.clip(tick_ids - layer, 0, ITEMS - 1)
    turns = jnp.concatenate([turns + stream * ITEMS for stream in range(STREAMS)])
    scalars = jnp.concatenate([core[None], phases, turns, starts, counts]).astype(jnp.int32)
    flip = [(z, 1 - z) for z in range(2)]
    swapped = lax.ppermute(norm_gain, "zone", flip)
    gains = jnp.concatenate(
        [jnp.where(zone == 0, norm_gain, swapped), jnp.where(zone == 0, swapped, norm_gain)]
    )
    spans = jnp.repeat(cache_lengths, length).reshape(n_item, 1, brow * length)
    axes = ("zone", "spot", "tensor")

    def spots(tick):
        return sorted({(tick - i) % n_spot for i in range(ITEMS)})

    def hop(tick, turn):
        pairs = []
        for s in spots(tick):
            for z in range(n_zone):
                ahead = z if s + 1 < n_spot else 1 - z
                pairs.append((z * n_spot + s, (ahead ^ turn) * n_spot + (s + 1) % n_spot))
        return sorted(pairs)

    def mirror(tick):
        return sorted(
            (z * n_spot + s, (1 - z) * n_spot + s) for s in spots(tick) for z in range(n_zone)
        )

    def active(tick):
        return [l for l in range(layers) if 0 <= tick - l < ITEMS]

    across = [(t, t ^ 1) for t in range(n_tensor)]
    shown = step_inputs.reshape(steps, n_item, brow, n_y, 2, shard)
    records = []
    for stream in range(STREAMS):
        arrived, record = None, [jnp.zeros((rows, half), jnp.float32)] * ITEMS
        for tick in range(ticks):
            busy = active(tick)
            if tick < ITEMS:
                item = stream * ITEMS + tick
                fresh = shown[:, item].reshape(rows, n_y, 2, shard)
                mine = lax.dynamic_index_in_dim(fresh, core, 2, False).reshape(rows, half)
                mine = jnp.where(spot == 0, mine, arrived if tick else 0)
            else:
                mine = arrived
            if tick:
                other = lax.ppermute(mine, "tensor", across)
            else:
                other = lax.dynamic_index_in_dim(fresh, 1 - core, 2, False).reshape(rows, half)
            use = sorted({l // n_spot for l in busy})
            extra = []
            if late:
                offset = late.pop(0)
                if tick == 0:
                    held = [got[1][k] for k in moving[:early]]
                    mine, _ = lax.optimization_barrier((mine, held))
                piece, _ = lax.optimization_barrier((ordered[1][offset], other))
                got[1][offset] = exchange(offset, piece)
                extra.append(got[1][offset])
            weights = [[got[p].get(k) for k in offsets] for p in range(2)]
            own = project(
                tick, use, tiles, tilew, n_y, scalars, mine, other, gains, sum([weights[p] for p in use], [])
            )
            sent = lax.ppermute(own, ("zone", "spot"), mirror(tick))
            if extra:
                sent, _ = lax.optimization_barrier((sent, extra))
            beside = []
            if late:
                offset = late.pop(0)
                piece, _ = lax.optimization_barrier((ordered[1][offset], sent))
                got[1][offset] = exchange(offset, piece)
                beside.append(got[1][offset])
            item_at = 1 + ticks + stream * ticks + tick
            theirs, attn = attend(
                item_at, steps, brow, n_y, scalars, own, sent, spans, cache_keys[0], cache_values[0], wo_rollout
            )
            moved = lax.ppermute(theirs, "tensor", across)
            ours = finish(n_y, scalars, attn, wo_rollout)
            part = ours.astype(jnp.float32) + moved.astype(jnp.float32)
            bit = 2
            while bit < n_tensor:
                part = part.astype(jnp.bfloat16)
                moved = lax.ppermute(part, "tensor", [(t, t ^ bit) for t in range(n_tensor)])
                part = part.astype(jnp.float32) + moved.astype(jnp.float32)
                bit = bit * 2
            wide = mine.astype(jnp.float32) + part
            for item in range(ITEMS):
                record[item] = jnp.where(layer == tick - item, wide, record[item])
            after = wide.astype(jnp.bfloat16)
            if tick + 1 < ticks:
                at_home = phases[tick + 1] == zone
                near = lax.ppermute(after, ("zone", "spot"), hop(tick, 0))
                far = lax.ppermute(after, ("zone", "spot"), hop(tick, 1))
                arrived = jnp.where(at_home, near, far)
                if beside:
                    arrived, _ = lax.optimization_barrier((arrived, beside))
        for value in record:
            value = lax.dynamic_slice_in_dim(value, tpos // 2 * shard, shard, 1)
            records.append(value.reshape(steps, brow, shard))
    return jnp.concatenate(records, axis=1)[None]


def solution(mesh):
    n_section, n_tensor = mesh.devices.shape
    fine = Mesh(mesh.devices.reshape(2, n_section // 2, n_tensor), ("zone", "spot", "tensor"))
    section = ("zone", "spot")
    placed = (
        P(("zone", "spot", "tensor"), None),
        P(),
        P(section, "tensor", None),
        P(section, None, None, "tensor"),
        P(section, None, None, "tensor"),
        P(),
        P(section, None),
        P(),
    )
    return jax.shard_map(
        per_device,
        mesh=fine,
        in_specs=placed,
        out_specs=P(section, None, None, "tensor"),
        check_vma=False,
    )
```

```python
import functools

import jax
import jax.numpy as jnp
import numpy as np
from jax import lax
from jax.experimental import pallas as pl
from jax.experimental.pallas import tpu as pltpu
from jax.sharding import Mesh, PartitionSpec as P

HDIM = 128
FB = 8
STREAMS = 1
ITEMS = 2
ROWBLOCK = 256
CHUNK = 384
WINDOW = 512
VMEM = 48 * 1024 * 1024


def sort_kernel(layers, place, slab, *outs):
    feats = ROWBLOCK // layers
    kept = len(outs)
    row = lax.broadcasted_iota(jnp.int32, (ROWBLOCK, ROWBLOCK), 0)
    col = lax.broadcasted_iota(jnp.int32, (ROWBLOCK, ROWBLOCK), 1)
    layer = row // feats % 2 * kept + ((row // (2 * feats)) ^ place[0])
    order = jnp.where(col == row % feats * layers + layer, 1.0, 0.0).astype(jnp.bfloat16)
    moved = jnp.dot(order, slab[...], preferred_element_type=jnp.float32).astype(jnp.bfloat16)
    for n, out in enumerate(outs):
        for phase in range(2):
            at = (2 * n + phase) * feats
            out[phase] = moved[at : at + feats]


def sort_slab(slab, layers, n_tensor, turn, place):
    rows, columns = slab.shape
    kept = layers // 2
    cdev = columns // n_tensor
    feats = ROWBLOCK // layers
    return pl.pallas_call(
        functools.partial(sort_kernel, layers),
        grid_spec=pltpu.PrefetchScalarGridSpec(
            num_scalar_prefetch=1,
            grid=(rows // ROWBLOCK,),
            in_specs=[pl.BlockSpec((ROWBLOCK, cdev), lambda i, s: (i, s[1] ^ turn))],
            out_specs=[pl.BlockSpec((2, feats, cdev), lambda i, s: (0, i, 0))] * kept,
        ),
        out_shape=[jax.ShapeDtypeStruct((2, rows // layers, cdev), jnp.bfloat16)] * kept,
        compiler_params=pltpu.CompilerParams(vmem_limit_bytes=VMEM),
        cost_estimate=pl.CostEstimate(
            flops=2 * rows * cdev * ROWBLOCK, bytes_accessed=4 * rows * cdev, transcendentals=0
        ),
    )(place, slab)


def project_kernel(tick, tiles, tilew, n_y, scalars, mine, other, gains, *rest):
    weights, (out, normed, held, sems) = rest[:-4], rest[-4:]
    rows, half = mine.shape
    width = 2 * half
    shard = half // n_y
    chunks, size, cdev = held.shape
    per = size // tilew
    core, phase = scalars[0], scalars[1 + tick]

    def fetch(n):
        target = held.at[n // per, pl.ds(n % per * tilew, tilew)]
        return pltpu.make_async_copy(weights[n].at[phase], target, sems.at[n])

    for n in range(tiles):
        fetch(n).start()

    here = mine[...].astype(jnp.float32)
    there = other[...].astype(jnp.float32)
    total = jnp.sum(here * here, axis=1, keepdims=True)
    total = total + jnp.sum(there * there, axis=1, keepdims=True)
    inverse = lax.rsqrt(total / width + 1e-06)
    gain = jnp.where(phase == 0, gains[0:1], gains[1:2])
    low = jnp.where(core == 0, here, there) * inverse
    high = jnp.where(core == 0, there, here) * inverse
    for y in range(n_y):
        at = 2 * y * shard
        piece = slice(y * shard, (y + 1) * shard)
        normed[:, at : at + shard] = low[:, piece] * gain[:, at : at + shard]
        at = at + shard
        normed[:, at : at + shard] = high[:, piece] * gain[:, at : at + shard]
    normed[:, width:] = jnp.zeros((rows, WINDOW), jnp.float32)

    along = CHUNK // tilew
    base = scalars.shape[0] - 2 * tiles
    lane = lax.broadcasted_iota(jnp.int32, (rows, CHUNK), 1)

    def spread(j):
        value = jnp.zeros((rows, CHUNK), jnp.float32)
        for a in range(along):
            start = scalars[base + j * along + a] * FB
            count = scalars[base + tiles + j * along + a] * FB
            aligned = start // 128 * 128
            window = normed[:, pl.ds(pl.multiple_of(aligned, 128), WINDOW)]
            put = a * tilew
            shift = (put - (start - aligned) + WINDOW) % WINDOW
            rolled = pltpu.roll(window, shift, 1)[:, :CHUNK]
            value = jnp.where((lane >= put) & (lane < put + count), rolled, value)
        return value.astype(jnp.bfloat16)

    acc = jnp.zeros((rows, cdev), jnp.float32)
    for j in range(chunks):
        parts = [spread(j * (size // CHUNK) + i) for i in range(size // CHUNK)]
        for n in range(j * per, (j + 1) * per):
            fetch(n).wait()
        acc = acc + jnp.dot(
            jnp.concatenate(parts, axis=1), held[j], preferred_element_type=jnp.float32
        )
    out[...] = acc.astype(jnp.bfloat16)


def project(tick, tiles, tilew, n_y, scalars, mine, other, gains, weights):
    rows, half = mine.shape
    cdev = weights[0].shape[2]
    depth = tiles * tilew
    size = 2 * CHUNK
    vmem = pl.BlockSpec(memory_space=pltpu.VMEM)
    return pl.pallas_call(
        functools.partial(project_kernel, tick, tiles, tilew, n_y),
        in_specs=[pl.BlockSpec(memory_space=pltpu.SMEM)]
        + [vmem] * 3
        + [pl.BlockSpec(memory_space=pltpu.HBM)] * len(weights),
        out_specs=vmem,
        scratch_shapes=[
            pltpu.VMEM((rows, 2 * half + WINDOW), jnp.float32),
            pltpu.VMEM((depth // size, size, cdev), jnp.bfloat16),
            pltpu.SemaphoreType.DMA((tiles,)),
        ],
        out_shape=jax.ShapeDtypeStruct((rows, cdev), jnp.bfloat16),
        compiler_params=pltpu.CompilerParams(vmem_limit_bytes=VMEM),
        cost_estimate=pl.CostEstimate(
            flops=2 * rows * depth * cdev, bytes_accessed=2 * depth * cdev, transcendentals=0
        ),
    )(scalars, mine, other, gains, *weights)


def attend_kernel(steps, brow, kvlocal, groups, n_y, item_at, scalars, own, sent, spans, ckeys, cvals, wo, theirs, ours, attn, kheld, vheld, held, sems):
    rows = steps * brow
    length = ckeys.shape[1]
    scale = 1.0 / HDIM**0.5
    qdim = kvlocal * groups * HDIM
    kvdim = kvlocal * HDIM
    shard = held.shape[2]
    core = scalars[0]
    item = scalars[item_at]
    first = pl.multiple_of(item * brow, brow)
    gets = [
        pltpu.make_async_copy(ckeys.at[pl.ds(first, brow)], kheld, sems.at[2 * n_y]),
        pltpu.make_async_copy(cvals.at[pl.ds(first, brow)], vheld, sems.at[2 * n_y + 1]),
    ]
    for k in range(2 * n_y):
        side = 1 - core if k < n_y else core
        at = pl.multiple_of((k % n_y * 2 + side) * shard, shard)
        gets.append(
            pltpu.make_async_copy(wo.at[0, :, pl.ds(at, shard)], held.at[k], sems.at[k])
        )
    for get in gets:
        get.start()
    gets[0].wait()
    gets[1].wait()
    span = spans[item]

    qkv = (own[...].astype(jnp.float32) + sent[...].astype(jnp.float32)).astype(jnp.bfloat16)
    qkv = qkv.astype(jnp.float32)
    keys = kheld[...].reshape(brow * length, kvdim)
    values = vheld[...].reshape(brow * length, kvdim)
    tall = groups * rows
    at = lax.broadcasted_iota(jnp.int32, (tall, brow * length), 0)
    col = lax.broadcasted_iota(jnp.int32, (tall, brow * length), 1)
    cmask = (at % brow == col // length) & (col % length < span)
    at = lax.broadcasted_iota(jnp.int32, (tall, rows), 0)
    col = lax.broadcasted_iota(jnp.int32, (tall, rows), 1)
    nmask = (at % brow == col % brow) & (col // brow <= at % rows // brow)
    contract = (((1,), (1,)), ((), ()))
    for head in range(kvlocal):
        lanes = slice(head * HDIM, (head + 1) * HDIM)
        first = head * groups * HDIM
        query = jnp.concatenate(
            [qkv[:, first + g * HDIM : first + (g + 1) * HDIM] for g in range(groups)], axis=0
        ).astype(jnp.bfloat16)
        at = qdim + head * HDIM
        knew = qkv[:, at : at + HDIM].astype(jnp.bfloat16)
        at = at + kvdim
        vnew = qkv[:, at : at + HDIM].astype(jnp.bfloat16)
        scache = scale * lax.dot_general(
            query, keys[:, lanes], contract, preferred_element_type=jnp.float32
        )
        snew = scale * lax.dot_general(
            query, knew, contract, preferred_element_type=jnp.float32
        )
        scache = jnp.where(cmask, scache, -1e30)
        snew = jnp.where(nmask, snew, -1e30)
        top = jnp.maximum(
            jnp.max(scache, axis=1, keepdims=True), jnp.max(snew, axis=1, keepdims=True)
        )
        ecache = jnp.where(cmask, jnp.exp(scache - top), 0.0)
        enew = jnp.where(nmask, jnp.exp(snew - top), 0.0)
        total = jnp.sum(ecache, axis=1, keepdims=True) + jnp.sum(enew, axis=1, keepdims=True)
        inverse = 1.0 / total
        wcache = (ecache * inverse).astype(jnp.bfloat16)
        wnew = (enew * inverse).astype(jnp.bfloat16)
        mixed = jnp.dot(wcache, values[:, lanes], preferred_element_type=jnp.float32)
        mixed = mixed + jnp.dot(wnew, vnew, preferred_element_type=jnp.float32)
        for g in range(groups):
            attn[:, first + g * HDIM : first + (g + 1) * HDIM] = mixed[
                g * rows : (g + 1) * rows
            ].astype(jnp.bfloat16)

    for k in range(2 * n_y):
        gets[2 + k].wait()
        product = jnp.dot(attn[...], held[k], preferred_element_type=jnp.float32)
        target = theirs if k < n_y else ours
        at = k % n_y * shard
        target[:, at : at + shard] = product.astype(jnp.bfloat16)


def attend(item_at, steps, brow, n_y, scalars, own, sent, spans, keys, values, wo):
    rows, cdev = own.shape
    _, qdim, width = wo.shape
    length, kvdim = keys.shape[1:]
    kvlocal = kvdim // HDIM
    groups = qdim // kvdim
    shard = width // (2 * n_y)
    vmem = pl.BlockSpec(memory_space=pltpu.VMEM)
    return pl.pallas_call(
        functools.partial(attend_kernel, steps, brow, kvlocal, groups, n_y, item_at),
        in_specs=[pl.BlockSpec(memory_space=pltpu.SMEM)]
        + [vmem] * 3
        + [pl.BlockSpec(memory_space=pltpu.HBM)] * 3,
        out_specs=[vmem] * 2,
        scratch_shapes=[
            pltpu.VMEM((rows, qdim), jnp.bfloat16),
            pltpu.VMEM((brow, length, kvdim), jnp.bfloat16),
            pltpu.VMEM((brow, length, kvdim), jnp.bfloat16),
            pltpu.VMEM((2 * n_y, qdim, shard), jnp.bfloat16),
            pltpu.SemaphoreType.DMA((2 * n_y + 2,)),
        ],
        out_shape=[jax.ShapeDtypeStruct((rows, shard * n_y), jnp.bfloat16)] * 2,
        compiler_params=pltpu.CompilerParams(vmem_limit_bytes=VMEM),
        cost_estimate=pl.CostEstimate(
            flops=2 * rows * qdim * width, bytes_accessed=2 * qdim * width, transcendentals=0
        ),
    )(scalars, own, sent, spans, keys, values, wo)


def per_device(
    trainer_tiles,
    tile_lengths,
    wo_rollout,
    cache_keys,
    cache_values,
    cache_lengths,
    norm_gain,
    step_inputs,
):
    n_zone = lax.axis_size("zone")
    n_spot = lax.axis_size("spot")
    n_tensor = lax.axis_size("tensor")
    layers = n_zone * n_spot
    tiles = n_spot * n_tensor
    n_y = n_tensor // 2
    slab, columns = trainer_tiles.shape
    cdev = columns // n_tensor
    tilew = slab // layers
    width = wo_rollout.shape[2]
    shard = width // n_tensor
    half = n_y * shard
    steps = step_inputs.shape[0]
    seqs, length = cache_keys.shape[1:3]
    n_item = STREAMS * ITEMS
    brow = seqs // n_item
    rows = steps * brow
    ticks = layers + ITEMS - 1
    zone = lax.axis_index("zone")
    spot = lax.axis_index("spot")
    tpos = lax.axis_index("tensor")
    core = tpos % 2
    layer = zone * n_spot + spot

    all_s, all_t = n_spot - 1, n_tensor - 2
    turns = sorted(range(n_tensor), key=lambda kt: (kt % 2, kt))
    offsets = [(ks, kt) for kt in turns for ks in range(n_spot)]
    place = jnp.stack([spot ^ core * all_s, tpos ^ core * all_t]).astype(jnp.int32)

    def exchange(offset, piece):
        pairs = []
        for s in range(n_spot):
            for t in range(n_tensor):
                bits = 1 if offset == (all_s, all_t) else t % 2
                ks, kt = (0, 0) if offset == (all_s, all_t) else offset
                target = (s ^ ks ^ bits * all_s) * n_tensor + (t ^ kt ^ bits * all_t)
                pairs.append((s * n_tensor + t, target))
        return lax.ppermute(piece, ("spot", "tensor"), pairs)

    pieces = {}
    for kt in turns:
        for ks, piece in enumerate(sort_slab(trainer_tiles, layers, n_tensor, kt, place)):
            pieces[ks, kt] = piece
        place, _ = lax.optimization_barrier((place, piece))
    first, last = pieces[0, 0], pieces[all_s, all_t]
    pieces[0, 0] = jnp.where(core == 0, first, last)
    pieces[all_s, all_t] = jnp.where(core == 0, last, first)
    weights = [
        exchange(offset, pieces[offset]) if offset != (0, 0) else pieces[offset]
        for offset in offsets
    ]

    ends = jnp.cumsum(tile_lengths)
    offset = np.array(offsets, np.int32)
    sender = (offset[:, 1] % 2) ^ core
    fixed = (offset == [0, 0]).all(axis=1) | (offset == [all_s, all_t]).all(axis=1)
    sender = jnp.where(fixed, 0, sender)
    sources = (offset[:, 0] ^ spot ^ sender * all_s) * n_tensor
    sources = sources + (offset[:, 1] ^ tpos ^ sender * all_t) + zone * tiles
    starts = (ends - tile_lengths)[sources]
    counts = tile_lengths[sources]
    tick_ids = jnp.arange(ticks, dtype=jnp.int32)
    phases = (tick_ids >= spot + n_spot).astype(jnp.int32)
    turns = jnp.clip(tick_ids - layer, 0, ITEMS - 1)
    turns = jnp.concatenate([turns + stream * ITEMS for stream in range(STREAMS)])
    scalars = jnp.concatenate([core[None], phases, turns, starts, counts]).astype(jnp.int32)
    flip = [(z, 1 - z) for z in range(2)]
    swapped = lax.ppermute(norm_gain, "zone", flip)
    gains = jnp.concatenate(
        [jnp.where(zone == 0, norm_gain, swapped), jnp.where(zone == 0, swapped, norm_gain)]
    )
    spans = jnp.repeat(cache_lengths, length).reshape(n_item, 1, brow * length)
    axes = ("zone", "spot", "tensor")

    def spots(tick):
        return sorted({(tick - i) % n_spot for i in range(ITEMS)})

    def hop(tick, turn):
        pairs = []
        for s in spots(tick):
            for z in range(n_zone):
                ahead = z if s + 1 < n_spot else 1 - z
                pairs.append((z * n_spot + s, (ahead ^ turn) * n_spot + (s + 1) % n_spot))
        return sorted(pairs)

    def mirror(tick):
        return sorted(
            (z * n_spot + s, (1 - z) * n_spot + s) for s in spots(tick) for z in range(n_zone)
        )

    across = [(t, t ^ 1) for t in range(n_tensor)]
    shown = step_inputs.reshape(steps, n_item, brow, n_y, 2, shard)
    records = []
    for stream in range(STREAMS):
        arrived, record = None, [jnp.zeros((rows, half), jnp.float32)] * ITEMS
        for tick in range(ticks):
            if tick < ITEMS:
                item = stream * ITEMS + tick
                fresh = shown[:, item].reshape(rows, n_y, 2, shard)
                mine = lax.dynamic_index_in_dim(fresh, core, 2, False).reshape(rows, half)
                mine = jnp.where(spot == 0, mine, arrived if tick else 0)
            else:
                mine = arrived
            if tick:
                other = lax.ppermute(mine, "tensor", across)
            else:
                other = lax.dynamic_index_in_dim(fresh, 1 - core, 2, False).reshape(rows, half)
            own = project(tick, tiles, tilew, n_y, scalars, mine, other, gains, weights)
            sent = lax.ppermute(own, ("zone", "spot"), mirror(tick))
            item_at = 1 + ticks + stream * ticks + tick
            theirs, ours = attend(
                item_at, steps, brow, n_y, scalars, own, sent, spans, cache_keys[0], cache_values[0], wo_rollout
            )
            part = ours.astype(jnp.float32) + lax.ppermute(theirs, "tensor", across).astype(
                jnp.float32
            )
            bit = 2
            while bit < n_tensor:
                part = part.astype(jnp.bfloat16)
                moved = lax.ppermute(part, "tensor", [(t, t ^ bit) for t in range(n_tensor)])
                part = part.astype(jnp.float32) + moved.astype(jnp.float32)
                bit = bit * 2
            wide = mine.astype(jnp.float32) + part
            for item in range(ITEMS):
                record[item] = jnp.where(layer == tick - item, wide, record[item])
            after = wide.astype(jnp.bfloat16)
            if tick + 1 < ticks:
                at_home = phases[tick + 1] == zone
                near = lax.ppermute(after, ("zone", "spot"), hop(tick, 0))
                far = lax.ppermute(after, ("zone", "spot"), hop(tick, 1))
                arrived = jnp.where(at_home, near, far)
        for value in record:
            value = lax.dynamic_slice_in_dim(value, tpos // 2 * shard, shard, 1)
            records.append(value.reshape(steps, brow, shard))
    return jnp.concatenate(records, axis=1)[None]


def solution(mesh):
    n_section, n_tensor = mesh.devices.shape
    fine = Mesh(mesh.devices.reshape(2, n_section // 2, n_tensor), ("zone", "spot", "tensor"))
    section = ("zone", "spot")
    placed = (
        P(("zone", "spot", "tensor"), None),
        P(),
        P(section, "tensor", None),
        P(section, None, None, "tensor"),
        P(section, None, None, "tensor"),
        P(),
        P(section, None),
        P(),
    )
    return jax.shard_map(
        per_device,
        mesh=fine,
        in_specs=placed,
        out_specs=P(section, None, None, "tensor"),
        check_vma=False,
    )
```

```python
import functools

import jax
import jax.numpy as jnp
import numpy as np
from jax import lax
from jax.experimental import pallas as pl
from jax.experimental.pallas import tpu as pltpu
from jax.sharding import Mesh, PartitionSpec as P

HDIM = 128
FB = 8
STREAMS = 1
ITEMS = 2
ROWBLOCK = 256
CHUNK = 384
WINDOW = 512
VMEM = 48 * 1024 * 1024
WHOLE_VMEM = 62 * 1024 * 1024


def sort_kernel(layers, place, slab, *outs):
    feats = ROWBLOCK // layers
    kept = len(outs)
    row = lax.broadcasted_iota(jnp.int32, (ROWBLOCK, ROWBLOCK), 0)
    col = lax.broadcasted_iota(jnp.int32, (ROWBLOCK, ROWBLOCK), 1)
    layer = row // feats % 2 * kept + ((row // (2 * feats)) ^ place[0])
    order = jnp.where(col == row % feats * layers + layer, 1.0, 0.0).astype(jnp.bfloat16)
    moved = jnp.dot(order, slab[...], preferred_element_type=jnp.float32).astype(jnp.bfloat16)
    for n, out in enumerate(outs):
        for phase in range(2):
            at = (2 * n + phase) * feats
            out[phase] = moved[at : at + feats]


def sort_slab(slab, layers, n_tensor, turn, place):
    rows, columns = slab.shape
    kept = layers // 2
    cdev = columns // n_tensor
    feats = ROWBLOCK // layers
    return pl.pallas_call(
        functools.partial(sort_kernel, layers),
        grid_spec=pltpu.PrefetchScalarGridSpec(
            num_scalar_prefetch=1,
            grid=(rows // ROWBLOCK,),
            in_specs=[pl.BlockSpec((ROWBLOCK, cdev), lambda i, s: (i, s[1] ^ turn))],
            out_specs=[pl.BlockSpec((2, feats, cdev), lambda i, s: (0, i, 0))] * kept,
        ),
        out_shape=[jax.ShapeDtypeStruct((2, rows // layers, cdev), jnp.bfloat16)] * kept,
        compiler_params=pltpu.CompilerParams(vmem_limit_bytes=WHOLE_VMEM),
        cost_estimate=pl.CostEstimate(
            flops=2 * rows * cdev * ROWBLOCK, bytes_accessed=4 * rows * cdev, transcendentals=0
        ),
    )(place, slab)


def project_kernel(tick, tiles, tilew, n_y, scalars, mine, other, gains, *rest):
    weights, (out, normed, held, sems) = rest[:-4], rest[-4:]
    rows, half = mine.shape
    width = 2 * half
    shard = half // n_y
    chunks, size, cdev = held.shape
    per = size // tilew
    core, phase = scalars[0], scalars[1 + tick]

    def fetch(n):
        target = held.at[n // per, pl.ds(n % per * tilew, tilew)]
        return pltpu.make_async_copy(weights[n].at[phase], target, sems.at[n])

    for n in range(tiles):
        fetch(n).start()

    here = mine[...].astype(jnp.float32)
    there = other[...].astype(jnp.float32)
    total = jnp.sum(here * here, axis=1, keepdims=True)
    total = total + jnp.sum(there * there, axis=1, keepdims=True)
    inverse = lax.rsqrt(total / width + 1e-06)
    gain = jnp.where(phase == 0, gains[0:1], gains[1:2])
    low = jnp.where(core == 0, here, there) * inverse
    high = jnp.where(core == 0, there, here) * inverse
    for y in range(n_y):
        at = 2 * y * shard
        piece = slice(y * shard, (y + 1) * shard)
        normed[:, at : at + shard] = low[:, piece] * gain[:, at : at + shard]
        at = at + shard
        normed[:, at : at + shard] = high[:, piece] * gain[:, at : at + shard]
    normed[:, width:] = jnp.zeros((rows, WINDOW), jnp.float32)

    along = CHUNK // tilew
    base = scalars.shape[0] - 2 * tiles
    lane = lax.broadcasted_iota(jnp.int32, (rows, CHUNK), 1)

    def spread(j):
        value = jnp.zeros((rows, CHUNK), jnp.float32)
        for a in range(along):
            start = scalars[base + j * along + a] * FB
            count = scalars[base + tiles + j * along + a] * FB
            aligned = start // 128 * 128
            window = normed[:, pl.ds(pl.multiple_of(aligned, 128), WINDOW)]
            put = a * tilew
            shift = (put - (start - aligned) + WINDOW) % WINDOW
            rolled = pltpu.roll(window, shift, 1)[:, :CHUNK]
            value = jnp.where((lane >= put) & (lane < put + count), rolled, value)
        return value.astype(jnp.bfloat16)

    acc = jnp.zeros((rows, cdev), jnp.float32)
    for j in range(chunks):
        parts = [spread(j * (size // CHUNK) + i) for i in range(size // CHUNK)]
        for n in range(j * per, (j + 1) * per):
            fetch(n).wait()
        acc = acc + jnp.dot(
            jnp.concatenate(parts, axis=1), held[j], preferred_element_type=jnp.float32
        )
    out[...] = acc.astype(jnp.bfloat16)


def project(tick, tiles, tilew, n_y, scalars, mine, other, gains, weights):
    rows, half = mine.shape
    cdev = weights[0].shape[2]
    depth = tiles * tilew
    size = 2 * CHUNK
    vmem = pl.BlockSpec(memory_space=pltpu.VMEM)
    return pl.pallas_call(
        functools.partial(project_kernel, tick, tiles, tilew, n_y),
        in_specs=[pl.BlockSpec(memory_space=pltpu.SMEM)]
        + [vmem] * 3
        + [pl.BlockSpec(memory_space=pltpu.HBM)] * len(weights),
        out_specs=vmem,
        scratch_shapes=[
            pltpu.VMEM((rows, 2 * half + WINDOW), jnp.float32),
            pltpu.VMEM((depth // size, size, cdev), jnp.bfloat16),
            pltpu.SemaphoreType.DMA((tiles,)),
        ],
        out_shape=jax.ShapeDtypeStruct((rows, cdev), jnp.bfloat16),
        compiler_params=pltpu.CompilerParams(vmem_limit_bytes=VMEM if tick else WHOLE_VMEM),
        cost_estimate=pl.CostEstimate(
            flops=2 * rows * depth * cdev, bytes_accessed=2 * depth * cdev, transcendentals=0
        ),
    )(scalars, mine, other, gains, *weights)


def attend_kernel(steps, brow, kvlocal, groups, n_y, item_at, scalars, own, sent, spans, ckeys, cvals, wo, theirs, ours, attn, kheld, vheld, held, sems):
    rows = steps * brow
    length = ckeys.shape[1]
    scale = 1.0 / HDIM**0.5
    qdim = kvlocal * groups * HDIM
    kvdim = kvlocal * HDIM
    shard = held.shape[2]
    core = scalars[0]
    item = scalars[item_at]
    first = pl.multiple_of(item * brow, brow)
    gets = [
        pltpu.make_async_copy(ckeys.at[pl.ds(first, brow)], kheld, sems.at[2 * n_y]),
        pltpu.make_async_copy(cvals.at[pl.ds(first, brow)], vheld, sems.at[2 * n_y + 1]),
    ]
    for k in range(2 * n_y):
        side = 1 - core if k < n_y else core
        at = pl.multiple_of((k % n_y * 2 + side) * shard, shard)
        gets.append(
            pltpu.make_async_copy(wo.at[0, :, pl.ds(at, shard)], held.at[k], sems.at[k])
        )
    for get in gets:
        get.start()
    gets[0].wait()
    gets[1].wait()
    span = spans[item]

    qkv = (own[...].astype(jnp.float32) + sent[...].astype(jnp.float32)).astype(jnp.bfloat16)
    qkv = qkv.astype(jnp.float32)
    keys = kheld[...].reshape(brow * length, kvdim)
    values = vheld[...].reshape(brow * length, kvdim)
    tall = groups * rows
    at = lax.broadcasted_iota(jnp.int32, (tall, brow * length), 0)
    col = lax.broadcasted_iota(jnp.int32, (tall, brow * length), 1)
    cmask = (at % brow == col // length) & (col % length < span)
    at = lax.broadcasted_iota(jnp.int32, (tall, rows), 0)
    col = lax.broadcasted_iota(jnp.int32, (tall, rows), 1)
    nmask = (at % brow == col % brow) & (col // brow <= at % rows // brow)
    contract = (((1,), (1,)), ((), ()))
    for head in range(kvlocal):
        lanes = slice(head * HDIM, (head + 1) * HDIM)
        first = head * groups * HDIM
        query = jnp.concatenate(
            [qkv[:, first + g * HDIM : first + (g + 1) * HDIM] for g in range(groups)], axis=0
        ).astype(jnp.bfloat16)
        at = qdim + head * HDIM
        knew = qkv[:, at : at + HDIM].astype(jnp.bfloat16)
        at = at + kvdim
        vnew = qkv[:, at : at + HDIM].astype(jnp.bfloat16)
        scache = scale * lax.dot_general(
            query, keys[:, lanes], contract, preferred_element_type=jnp.float32
        )
        snew = scale * lax.dot_general(
            query, knew, contract, preferred_element_type=jnp.float32
        )
        scache = jnp.where(cmask, scache, -1e30)
        snew = jnp.where(nmask, snew, -1e30)
        top = jnp.maximum(
            jnp.max(scache, axis=1, keepdims=True), jnp.max(snew, axis=1, keepdims=True)
        )
        ecache = jnp.where(cmask, jnp.exp(scache - top), 0.0)
        enew = jnp.where(nmask, jnp.exp(snew - top), 0.0)
        total = jnp.sum(ecache, axis=1, keepdims=True) + jnp.sum(enew, axis=1, keepdims=True)
        inverse = 1.0 / total
        wcache = (ecache * inverse).astype(jnp.bfloat16)
        wnew = (enew * inverse).astype(jnp.bfloat16)
        mixed = jnp.dot(wcache, values[:, lanes], preferred_element_type=jnp.float32)
        mixed = mixed + jnp.dot(wnew, vnew, preferred_element_type=jnp.float32)
        for g in range(groups):
            attn[:, first + g * HDIM : first + (g + 1) * HDIM] = mixed[
                g * rows : (g + 1) * rows
            ].astype(jnp.bfloat16)

    for k in range(2 * n_y):
        gets[2 + k].wait()
        product = jnp.dot(attn[...], held[k], preferred_element_type=jnp.float32)
        target = theirs if k < n_y else ours
        at = k % n_y * shard
        target[:, at : at + shard] = product.astype(jnp.bfloat16)


def attend(item_at, steps, brow, n_y, scalars, own, sent, spans, keys, values, wo):
    rows, cdev = own.shape
    _, qdim, width = wo.shape
    length, kvdim = keys.shape[1:]
    kvlocal = kvdim // HDIM
    groups = qdim // kvdim
    shard = width // (2 * n_y)
    vmem = pl.BlockSpec(memory_space=pltpu.VMEM)
    return pl.pallas_call(
        functools.partial(attend_kernel, steps, brow, kvlocal, groups, n_y, item_at),
        in_specs=[pl.BlockSpec(memory_space=pltpu.SMEM)]
        + [vmem] * 3
        + [pl.BlockSpec(memory_space=pltpu.HBM)] * 3,
        out_specs=[vmem] * 2,
        scratch_shapes=[
            pltpu.VMEM((rows, qdim), jnp.bfloat16),
            pltpu.VMEM((brow, length, kvdim), jnp.bfloat16),
            pltpu.VMEM((brow, length, kvdim), jnp.bfloat16),
            pltpu.VMEM((2 * n_y, qdim, shard), jnp.bfloat16),
            pltpu.SemaphoreType.DMA((2 * n_y + 2,)),
        ],
        out_shape=[jax.ShapeDtypeStruct((rows, shard * n_y), jnp.bfloat16)] * 2,
        compiler_params=pltpu.CompilerParams(vmem_limit_bytes=VMEM),
        cost_estimate=pl.CostEstimate(
            flops=2 * rows * qdim * width, bytes_accessed=2 * qdim * width, transcendentals=0
        ),
    )(scalars, own, sent, spans, keys, values, wo)


def per_device(
    trainer_tiles,
    tile_lengths,
    wo_rollout,
    cache_keys,
    cache_values,
    cache_lengths,
    norm_gain,
    step_inputs,
):
    n_zone = lax.axis_size("zone")
    n_spot = lax.axis_size("spot")
    n_tensor = lax.axis_size("tensor")
    layers = n_zone * n_spot
    tiles = n_spot * n_tensor
    n_y = n_tensor // 2
    slab, columns = trainer_tiles.shape
    cdev = columns // n_tensor
    tilew = slab // layers
    width = wo_rollout.shape[2]
    shard = width // n_tensor
    half = n_y * shard
    steps = step_inputs.shape[0]
    seqs, length = cache_keys.shape[1:3]
    n_item = STREAMS * ITEMS
    brow = seqs // n_item
    rows = steps * brow
    ticks = layers + ITEMS - 1
    zone = lax.axis_index("zone")
    spot = lax.axis_index("spot")
    tpos = lax.axis_index("tensor")
    core = tpos % 2
    layer = zone * n_spot + spot

    all_s, all_t = n_spot - 1, n_tensor - 2
    turns = sorted(range(n_tensor), key=lambda kt: (kt % 2, kt))
    offsets = [(ks, kt) for kt in turns for ks in range(n_spot)]
    place = jnp.stack([spot ^ core * all_s, tpos ^ core * all_t]).astype(jnp.int32)

    def exchange(offset, piece):
        pairs = []
        for s in range(n_spot):
            for t in range(n_tensor):
                bits = 1 if offset == (all_s, all_t) else t % 2
                ks, kt = (0, 0) if offset == (all_s, all_t) else offset
                target = (s ^ ks ^ bits * all_s) * n_tensor + (t ^ kt ^ bits * all_t)
                pairs.append((s * n_tensor + t, target))
        return lax.ppermute(piece, ("spot", "tensor"), pairs)

    pieces = {}
    for kt in turns:
        for ks, piece in enumerate(sort_slab(trainer_tiles, layers, n_tensor, kt, place)):
            pieces[ks, kt] = piece
        place, _ = lax.optimization_barrier((place, piece))
    first, last = pieces[0, 0], pieces[all_s, all_t]
    pieces[0, 0] = jnp.where(core == 0, first, last)
    pieces[all_s, all_t] = jnp.where(core == 0, last, first)
    weights = [
        exchange(offset, pieces[offset]) if offset != (0, 0) else pieces[offset]
        for offset in offsets
    ]

    ends = jnp.cumsum(tile_lengths)
    offset = np.array(offsets, np.int32)
    sender = (offset[:, 1] % 2) ^ core
    fixed = (offset == [0, 0]).all(axis=1) | (offset == [all_s, all_t]).all(axis=1)
    sender = jnp.where(fixed, 0, sender)
    sources = (offset[:, 0] ^ spot ^ sender * all_s) * n_tensor
    sources = sources + (offset[:, 1] ^ tpos ^ sender * all_t) + zone * tiles
    starts = (ends - tile_lengths)[sources]
    counts = tile_lengths[sources]
    tick_ids = jnp.arange(ticks, dtype=jnp.int32)
    phases = (tick_ids >= spot + n_spot).astype(jnp.int32)
    turns = jnp.clip(tick_ids - layer, 0, ITEMS - 1)
    turns = jnp.concatenate([turns + stream * ITEMS for stream in range(STREAMS)])
    scalars = jnp.concatenate([core[None], phases, turns, starts, counts]).astype(jnp.int32)
    flip = [(z, 1 - z) for z in range(2)]
    swapped = lax.ppermute(norm_gain, "zone", flip)
    gains = jnp.concatenate(
        [jnp.where(zone == 0, norm_gain, swapped), jnp.where(zone == 0, swapped, norm_gain)]
    )
    spans = jnp.repeat(cache_lengths, length).reshape(n_item, 1, brow * length)
    axes = ("zone", "spot", "tensor")

    def spots(tick):
        return sorted({(tick - i) % n_spot for i in range(ITEMS)})

    def hop(tick, turn):
        pairs = []
        for s in spots(tick):
            for z in range(n_zone):
                ahead = z if s + 1 < n_spot else 1 - z
                pairs.append((z * n_spot + s, (ahead ^ turn) * n_spot + (s + 1) % n_spot))
        return sorted(pairs)

    def mirror(tick):
        return sorted(
            (z * n_spot + s, (1 - z) * n_spot + s) for s in spots(tick) for z in range(n_zone)
        )

    across = [(t, t ^ 1) for t in range(n_tensor)]
    shown = step_inputs.reshape(steps, n_item, brow, n_y, 2, shard)
    records = []
    for stream in range(STREAMS):
        arrived, record = None, [jnp.zeros((rows, half), jnp.float32)] * ITEMS
        for tick in range(ticks):
            if tick < ITEMS:
                item = stream * ITEMS + tick
                fresh = shown[:, item].reshape(rows, n_y, 2, shard)
                mine = lax.dynamic_index_in_dim(fresh, core, 2, False).reshape(rows, half)
                mine = jnp.where(spot == 0, mine, arrived if tick else 0)
            else:
                mine = arrived
            if tick:
                other = lax.ppermute(mine, "tensor", across)
            else:
                other = lax.dynamic_index_in_dim(fresh, 1 - core, 2, False).reshape(rows, half)
            own = project(tick, tiles, tilew, n_y, scalars, mine, other, gains, weights)
            sent = lax.ppermute(own, ("zone", "spot"), mirror(tick))
            item_at = 1 + ticks + stream * ticks + tick
            theirs, ours = attend(
                item_at, steps, brow, n_y, scalars, own, sent, spans, cache_keys[0], cache_values[0], wo_rollout
            )
            part = ours.astype(jnp.float32) + lax.ppermute(theirs, "tensor", across).astype(
                jnp.float32
            )
            bit = 2
            while bit < n_tensor:
                part = part.astype(jnp.bfloat16)
                moved = lax.ppermute(part, "tensor", [(t, t ^ bit) for t in range(n_tensor)])
                part = part.astype(jnp.float32) + moved.astype(jnp.float32)
                bit = bit * 2
            wide = mine.astype(jnp.float32) + part
            for item in range(ITEMS):
                record[item] = jnp.where(layer == tick - item, wide, record[item])
            after = wide.astype(jnp.bfloat16)
            if tick + 1 < ticks:
                at_home = phases[tick + 1] == zone
                near = lax.ppermute(after, ("zone", "spot"), hop(tick, 0))
                far = lax.ppermute(after, ("zone", "spot"), hop(tick, 1))
                arrived = jnp.where(at_home, near, far)
        for value in record:
            value = lax.dynamic_slice_in_dim(value, tpos // 2 * shard, shard, 1)
            records.append(value.reshape(steps, brow, shard))
    return jnp.concatenate(records, axis=1)[None]


def solution(mesh):
    n_section, n_tensor = mesh.devices.shape
    fine = Mesh(mesh.devices.reshape(2, n_section // 2, n_tensor), ("zone", "spot", "tensor"))
    section = ("zone", "spot")
    placed = (
        P(("zone", "spot", "tensor"), None),
        P(),
        P(section, "tensor", None),
        P(section, None, None, "tensor"),
        P(section, None, None, "tensor"),
        P(),
        P(section, None),
        P(),
    )
    return jax.shard_map(
        per_device,
        mesh=fine,
        in_specs=placed,
        out_specs=P(section, None, None, "tensor"),
        check_vma=False,
    )
```

```python
import functools

import jax
import jax.numpy as jnp
import numpy as np
from jax import lax
from jax.experimental import pallas as pl
from jax.experimental.pallas import tpu as pltpu
from jax.sharding import Mesh, PartitionSpec as P

HDIM = 128
FB = 8
STREAMS = 1
ITEMS = 2
ROWBLOCK = 256
CHUNK = 384
WINDOW = 512
VMEM = 48 * 1024 * 1024
WHOLE_VMEM = 62 * 1024 * 1024


def sort_kernel(layers, place, slab, *outs):
    feats = ROWBLOCK // layers
    kept = len(outs)
    row = lax.broadcasted_iota(jnp.int32, (ROWBLOCK, ROWBLOCK), 0)
    col = lax.broadcasted_iota(jnp.int32, (ROWBLOCK, ROWBLOCK), 1)
    layer = row // feats % 2 * kept + ((row // (2 * feats)) ^ place[0])
    order = jnp.where(col == row % feats * layers + layer, 1.0, 0.0).astype(jnp.bfloat16)
    moved = jnp.dot(order, slab[...], preferred_element_type=jnp.float32).astype(jnp.bfloat16)
    for n, out in enumerate(outs):
        for phase in range(2):
            at = (2 * n + phase) * feats
            out[phase] = moved[at : at + feats]


def sort_slab(slab, layers, n_tensor, turn, place):
    rows, columns = slab.shape
    kept = layers // 2
    cdev = columns // n_tensor
    feats = ROWBLOCK // layers
    return pl.pallas_call(
        functools.partial(sort_kernel, layers),
        grid_spec=pltpu.PrefetchScalarGridSpec(
            num_scalar_prefetch=1,
            grid=(rows // ROWBLOCK,),
            in_specs=[pl.BlockSpec((ROWBLOCK, cdev), lambda i, s: (i, s[1] ^ turn))],
            out_specs=[pl.BlockSpec((2, feats, cdev), lambda i, s: (0, i, 0))] * kept,
        ),
        out_shape=[jax.ShapeDtypeStruct((2, rows // layers, cdev), jnp.bfloat16)] * kept,
        compiler_params=pltpu.CompilerParams(vmem_limit_bytes=WHOLE_VMEM),
        cost_estimate=pl.CostEstimate(
            flops=2 * rows * cdev * ROWBLOCK, bytes_accessed=4 * rows * cdev, transcendentals=0
        ),
    )(place, slab)


def project_kernel(tick, tiles, tilew, n_y, scalars, mine, other, gains, *rest):
    weights, (out, normed, held, sems) = rest[:-4], rest[-4:]
    rows, half = mine.shape
    width = 2 * half
    shard = half // n_y
    chunks, size, cdev = held.shape
    per = size // tilew
    core, phase = scalars[0], scalars[1 + tick]

    def fetch(n):
        target = held.at[n // per, pl.ds(n % per * tilew, tilew)]
        return pltpu.make_async_copy(weights[n].at[phase], target, sems.at[n])

    for n in range(tiles):
        fetch(n).start()

    here = mine[...].astype(jnp.float32)
    there = other[...].astype(jnp.float32)
    total = jnp.sum(here * here, axis=1, keepdims=True)
    total = total + jnp.sum(there * there, axis=1, keepdims=True)
    inverse = lax.rsqrt(total / width + 1e-06)
    gain = jnp.where(phase == 0, gains[0:1], gains[1:2])
    low = jnp.where(core == 0, here, there) * inverse
    high = jnp.where(core == 0, there, here) * inverse
    for y in range(n_y):
        at = 2 * y * shard
        piece = slice(y * shard, (y + 1) * shard)
        normed[:, at : at + shard] = low[:, piece] * gain[:, at : at + shard]
        at = at + shard
        normed[:, at : at + shard] = high[:, piece] * gain[:, at : at + shard]
    normed[:, width:] = jnp.zeros((rows, WINDOW), jnp.float32)

    along = CHUNK // tilew
    base = scalars.shape[0] - 2 * tiles
    lane = lax.broadcasted_iota(jnp.int32, (rows, CHUNK), 1)

    def spread(j):
        value = jnp.zeros((rows, CHUNK), jnp.float32)
        for a in range(along):
            start = scalars[base + j * along + a] * FB
            count = scalars[base + tiles + j * along + a] * FB
            aligned = start // 128 * 128
            window = normed[:, pl.ds(pl.multiple_of(aligned, 128), WINDOW)]
            put = a * tilew
            shift = (put - (start - aligned) + WINDOW) % WINDOW
            rolled = pltpu.roll(window, shift, 1)[:, :CHUNK]
            value = jnp.where((lane >= put) & (lane < put + count), rolled, value)
        return value.astype(jnp.bfloat16)

    acc = jnp.zeros((rows, cdev), jnp.float32)
    for j in range(chunks):
        parts = [spread(j * (size // CHUNK) + i) for i in range(size // CHUNK)]
        for n in range(j * per, (j + 1) * per):
            fetch(n).wait()
        acc = acc + jnp.dot(
            jnp.concatenate(parts, axis=1), held[j], preferred_element_type=jnp.float32
        )
    out[...] = acc.astype(jnp.bfloat16)


def project(tick, tiles, tilew, n_y, scalars, mine, other, gains, weights):
    rows, half = mine.shape
    cdev = weights[0].shape[2]
    depth = tiles * tilew
    size = 2 * CHUNK
    vmem = pl.BlockSpec(memory_space=pltpu.VMEM)
    return pl.pallas_call(
        functools.partial(project_kernel, tick, tiles, tilew, n_y),
        in_specs=[pl.BlockSpec(memory_space=pltpu.SMEM)]
        + [vmem] * 3
        + [pl.BlockSpec(memory_space=pltpu.HBM)] * len(weights),
        out_specs=vmem,
        scratch_shapes=[
            pltpu.VMEM((rows, 2 * half + WINDOW), jnp.float32),
            pltpu.VMEM((depth // size, size, cdev), jnp.bfloat16),
            pltpu.SemaphoreType.DMA((tiles,)),
        ],
        out_shape=jax.ShapeDtypeStruct((rows, cdev), jnp.bfloat16),
        compiler_params=pltpu.CompilerParams(vmem_limit_bytes=VMEM if tick else WHOLE_VMEM),
        cost_estimate=pl.CostEstimate(
            flops=2 * rows * depth * cdev, bytes_accessed=2 * depth * cdev, transcendentals=0
        ),
    )(scalars, mine, other, gains, *weights)


def attend_kernel(steps, brow, kvlocal, groups, n_y, item_at, scalars, own, sent, spans, ckeys, cvals, wo, theirs, ours, attn, kheld, vheld, held, sems):
    rows = steps * brow
    length = ckeys.shape[1]
    scale = 1.0 / HDIM**0.5
    qdim = kvlocal * groups * HDIM
    kvdim = kvlocal * HDIM
    shard = held.shape[2]
    core = scalars[0]
    item = scalars[item_at]
    first = pl.multiple_of(item * brow, brow)
    gets = [
        pltpu.make_async_copy(ckeys.at[pl.ds(first, brow)], kheld, sems.at[2 * n_y]),
        pltpu.make_async_copy(cvals.at[pl.ds(first, brow)], vheld, sems.at[2 * n_y + 1]),
    ]
    for k in range(2 * n_y):
        side = 1 - core if k < n_y else core
        at = pl.multiple_of((k % n_y * 2 + side) * shard, shard)
        gets.append(
            pltpu.make_async_copy(wo.at[0, :, pl.ds(at, shard)], held.at[k], sems.at[k])
        )
    for get in gets:
        get.start()
    gets[0].wait()
    gets[1].wait()
    span = spans[item]

    qkv = (own[...].astype(jnp.float32) + sent[...].astype(jnp.float32)).astype(jnp.bfloat16)
    qkv = qkv.astype(jnp.float32)
    keys = kheld[...].reshape(brow * length, kvdim)
    values = vheld[...].reshape(brow * length, kvdim)
    tall = groups * rows
    at = lax.broadcasted_iota(jnp.int32, (tall, brow * length), 0)
    col = lax.broadcasted_iota(jnp.int32, (tall, brow * length), 1)
    cmask = (at % brow == col // length) & (col % length < span)
    at = lax.broadcasted_iota(jnp.int32, (tall, rows), 0)
    col = lax.broadcasted_iota(jnp.int32, (tall, rows), 1)
    nmask = (at % brow == col % brow) & (col // brow <= at % rows // brow)
    contract = (((1,), (1,)), ((), ()))
    for head in range(kvlocal):
        lanes = slice(head * HDIM, (head + 1) * HDIM)
        first = head * groups * HDIM
        query = jnp.concatenate(
            [qkv[:, first + g * HDIM : first + (g + 1) * HDIM] for g in range(groups)], axis=0
        ).astype(jnp.bfloat16)
        at = qdim + head * HDIM
        knew = qkv[:, at : at + HDIM].astype(jnp.bfloat16)
        at = at + kvdim
        vnew = qkv[:, at : at + HDIM].astype(jnp.bfloat16)
        scache = scale * lax.dot_general(
            query, keys[:, lanes], contract, preferred_element_type=jnp.float32
        )
        snew = scale * lax.dot_general(
            query, knew, contract, preferred_element_type=jnp.float32
        )
        scache = jnp.where(cmask, scache, -1e30)
        snew = jnp.where(nmask, snew, -1e30)
        top = jnp.maximum(
            jnp.max(scache, axis=1, keepdims=True), jnp.max(snew, axis=1, keepdims=True)
        )
        ecache = jnp.where(cmask, jnp.exp(scache - top), 0.0)
        enew = jnp.where(nmask, jnp.exp(snew - top), 0.0)
        total = jnp.sum(ecache, axis=1, keepdims=True) + jnp.sum(enew, axis=1, keepdims=True)
        inverse = 1.0 / total
        wcache = (ecache * inverse).astype(jnp.bfloat16)
        wnew = (enew * inverse).astype(jnp.bfloat16)
        mixed = jnp.dot(wcache, values[:, lanes], preferred_element_type=jnp.float32)
        mixed = mixed + jnp.dot(wnew, vnew, preferred_element_type=jnp.float32)
        for g in range(groups):
            attn[:, first + g * HDIM : first + (g + 1) * HDIM] = mixed[
                g * rows : (g + 1) * rows
            ].astype(jnp.bfloat16)

    for k in range(2 * n_y):
        gets[2 + k].wait()
        product = jnp.dot(attn[...], held[k], preferred_element_type=jnp.float32)
        target = theirs if k < n_y else ours
        at = k % n_y * shard
        target[:, at : at + shard] = product.astype(jnp.bfloat16)


def attend(item_at, steps, brow, n_y, scalars, own, sent, spans, keys, values, wo):
    rows, cdev = own.shape
    _, qdim, width = wo.shape
    length, kvdim = keys.shape[1:]
    kvlocal = kvdim // HDIM
    groups = qdim // kvdim
    shard = width // (2 * n_y)
    vmem = pl.BlockSpec(memory_space=pltpu.VMEM)
    return pl.pallas_call(
        functools.partial(attend_kernel, steps, brow, kvlocal, groups, n_y, item_at),
        in_specs=[pl.BlockSpec(memory_space=pltpu.SMEM)]
        + [vmem] * 3
        + [pl.BlockSpec(memory_space=pltpu.HBM)] * 3,
        out_specs=[vmem] * 2,
        scratch_shapes=[
            pltpu.VMEM((rows, qdim), jnp.bfloat16),
            pltpu.VMEM((brow, length, kvdim), jnp.bfloat16),
            pltpu.VMEM((brow, length, kvdim), jnp.bfloat16),
            pltpu.VMEM((2 * n_y, qdim, shard), jnp.bfloat16),
            pltpu.SemaphoreType.DMA((2 * n_y + 2,)),
        ],
        out_shape=[jax.ShapeDtypeStruct((rows, shard * n_y), jnp.bfloat16)] * 2,
        compiler_params=pltpu.CompilerParams(vmem_limit_bytes=VMEM),
        cost_estimate=pl.CostEstimate(
            flops=2 * rows * qdim * width, bytes_accessed=2 * qdim * width, transcendentals=0
        ),
    )(scalars, own, sent, spans, keys, values, wo)


def join_kernel(part, moved, mine, out):
    total = part[...].astype(jnp.float32) + moved[...].astype(jnp.float32)
    out[...] = (mine[...].astype(jnp.float32) + total).astype(jnp.bfloat16)


def choose_kernel(flag, near, far, out):
    out[...] = jnp.where(flag[0] == 1, near[...], far[...])


def in_vmem(kernel, arrays, flag=None):
    vmem = pl.BlockSpec(memory_space=pltpu.VMEM)
    scalar = [] if flag is None else [flag.astype(jnp.int32)[None]]
    return pl.pallas_call(
        kernel,
        in_specs=[pl.BlockSpec(memory_space=pltpu.SMEM)] * len(scalar) + [vmem] * len(arrays),
        out_specs=vmem,
        out_shape=jax.ShapeDtypeStruct(arrays[0].shape, jnp.bfloat16),
        compiler_params=pltpu.CompilerParams(vmem_limit_bytes=VMEM),
    )(*scalar, *arrays)


def per_device(
    trainer_tiles,
    tile_lengths,
    wo_rollout,
    cache_keys,
    cache_values,
    cache_lengths,
    norm_gain,
    step_inputs,
):
    n_zone = lax.axis_size("zone")
    n_spot = lax.axis_size("spot")
    n_tensor = lax.axis_size("tensor")
    layers = n_zone * n_spot
    tiles = n_spot * n_tensor
    n_y = n_tensor // 2
    slab, columns = trainer_tiles.shape
    cdev = columns // n_tensor
    tilew = slab // layers
    width = wo_rollout.shape[2]
    shard = width // n_tensor
    half = n_y * shard
    steps = step_inputs.shape[0]
    seqs, length = cache_keys.shape[1:3]
    n_item = STREAMS * ITEMS
    brow = seqs // n_item
    rows = steps * brow
    ticks = layers + ITEMS - 1
    zone = lax.axis_index("zone")
    spot = lax.axis_index("spot")
    tpos = lax.axis_index("tensor")
    core = tpos % 2
    layer = zone * n_spot + spot

    all_s, all_t = n_spot - 1, n_tensor - 2
    turns = sorted(range(n_tensor), key=lambda kt: (kt % 2, kt))
    offsets = [(ks, kt) for kt in turns for ks in range(n_spot)]
    place = jnp.stack([spot ^ core * all_s, tpos ^ core * all_t]).astype(jnp.int32)

    def exchange(offset, piece):
        pairs = []
        for s in range(n_spot):
            for t in range(n_tensor):
                bits = 1 if offset == (all_s, all_t) else t % 2
                ks, kt = (0, 0) if offset == (all_s, all_t) else offset
                target = (s ^ ks ^ bits * all_s) * n_tensor + (t ^ kt ^ bits * all_t)
                pairs.append((s * n_tensor + t, target))
        return lax.ppermute(piece, ("spot", "tensor"), pairs)

    pieces = {}
    for kt in turns:
        for ks, piece in enumerate(sort_slab(trainer_tiles, layers, n_tensor, kt, place)):
            pieces[ks, kt] = piece
        place, _ = lax.optimization_barrier((place, piece))
    first, last = pieces[0, 0], pieces[all_s, all_t]
    pieces[0, 0] = jnp.where(core == 0, first, last)
    pieces[all_s, all_t] = jnp.where(core == 0, last, first)
    weights = [
        exchange(offset, pieces[offset]) if offset != (0, 0) else pieces[offset]
        for offset in offsets
    ]

    ends = jnp.cumsum(tile_lengths)
    offset = np.array(offsets, np.int32)
    sender = (offset[:, 1] % 2) ^ core
    fixed = (offset == [0, 0]).all(axis=1) | (offset == [all_s, all_t]).all(axis=1)
    sender = jnp.where(fixed, 0, sender)
    sources = (offset[:, 0] ^ spot ^ sender * all_s) * n_tensor
    sources = sources + (offset[:, 1] ^ tpos ^ sender * all_t) + zone * tiles
    starts = (ends - tile_lengths)[sources]
    counts = tile_lengths[sources]
    tick_ids = jnp.arange(ticks, dtype=jnp.int32)
    phases = (tick_ids >= spot + n_spot).astype(jnp.int32)
    turns = jnp.clip(tick_ids - layer, 0, ITEMS - 1)
    turns = jnp.concatenate([turns + stream * ITEMS for stream in range(STREAMS)])
    scalars = jnp.concatenate([core[None], phases, turns, starts, counts]).astype(jnp.int32)
    flip = [(z, 1 - z) for z in range(2)]
    swapped = lax.ppermute(norm_gain, "zone", flip)
    gains = jnp.concatenate(
        [jnp.where(zone == 0, norm_gain, swapped), jnp.where(zone == 0, swapped, norm_gain)]
    )
    spans = jnp.repeat(cache_lengths, length).reshape(n_item, 1, brow * length)
    axes = ("zone", "spot", "tensor")

    def spots(tick):
        return sorted({(tick - i) % n_spot for i in range(ITEMS)})

    def hop(tick, turn):
        pairs = []
        for s in spots(tick):
            for z in range(n_zone):
                ahead = z if s + 1 < n_spot else 1 - z
                pairs.append((z * n_spot + s, (ahead ^ turn) * n_spot + (s + 1) % n_spot))
        return sorted(pairs)

    def mirror(tick):
        return sorted(
            (z * n_spot + s, (1 - z) * n_spot + s) for s in spots(tick) for z in range(n_zone)
        )

    across = [(t, t ^ 1) for t in range(n_tensor)]
    shown = step_inputs.reshape(steps, n_item, brow, n_y, 2, shard)
    records = []
    for stream in range(STREAMS):
        arrived, record = None, []
        for tick in range(ticks):
            if tick < ITEMS:
                item = stream * ITEMS + tick
                fresh = shown[:, item].reshape(rows, n_y, 2, shard)
                mine = lax.dynamic_index_in_dim(fresh, core, 2, False).reshape(rows, half)
                mine = jnp.where(spot == 0, mine, arrived if tick else 0)
            else:
                mine = arrived
            if tick:
                other = lax.ppermute(mine, "tensor", across)
            else:
                other = lax.dynamic_index_in_dim(fresh, 1 - core, 2, False).reshape(rows, half)
            own = project(tick, tiles, tilew, n_y, scalars, mine, other, gains, weights)
            sent = lax.ppermute(own, ("zone", "spot"), mirror(tick))
            item_at = 1 + ticks + stream * ticks + tick
            theirs, ours = attend(
                item_at, steps, brow, n_y, scalars, own, sent, spans, cache_keys[0], cache_values[0], wo_rollout
            )
            moved = lax.ppermute(theirs, "tensor", across)
            part = (ours.astype(jnp.float32) + moved.astype(jnp.float32)).astype(jnp.bfloat16)
            bit = 2
            while bit < n_tensor:
                moved = lax.ppermute(part, "tensor", [(t, t ^ bit) for t in range(n_tensor)])
                bit = bit * 2
                if bit < n_tensor:
                    part = part.astype(jnp.float32) + moved.astype(jnp.float32)
                    part = part.astype(jnp.bfloat16)
            after = in_vmem(join_kernel, [part, moved, mine])
            record.append(after)
            if tick + 1 < ticks:
                at_home = phases[tick + 1] == zone
                far = lax.ppermute(after, ("zone", "spot"), hop(tick, 1))
                near = lax.ppermute(after, ("zone", "spot"), hop(tick, 0))
                arrived = in_vmem(choose_kernel, [near, far], at_home)
        for item in range(ITEMS):
            value = jnp.zeros((rows, half), jnp.bfloat16)
            for tick in range(item, ticks):
                value = jnp.where(layer == tick - item, record[tick], value)
            value = lax.dynamic_slice_in_dim(value, tpos // 2 * shard, shard, 1)
            records.append(value.astype(jnp.float32).reshape(steps, brow, shard))
    return jnp.concatenate(records, axis=1)[None]


def solution(mesh):
    n_section, n_tensor = mesh.devices.shape
    fine = Mesh(mesh.devices.reshape(2, n_section // 2, n_tensor), ("zone", "spot", "tensor"))
    section = ("zone", "spot")
    placed = (
        P(("zone", "spot", "tensor"), None),
        P(),
        P(section, "tensor", None),
        P(section, None, None, "tensor"),
        P(section, None, None, "tensor"),
        P(),
        P(section, None),
        P(),
    )
    return jax.shard_map(
        per_device,
        mesh=fine,
        in_specs=placed,
        out_specs=P(section, None, None, "tensor"),
        check_vma=False,
    )
```

```python
import functools

import jax
import jax.numpy as jnp
import numpy as np
from jax import lax
from jax.experimental import pallas as pl
from jax.experimental.pallas import tpu as pltpu
from jax.sharding import Mesh, PartitionSpec as P

HDIM = 128
FB = 8
ITEMS = 4
ROWBLOCK = 256
CHUNK = 384
WINDOW = 512
VMEM = 48 * 1024 * 1024
WHOLE_VMEM = 62 * 1024 * 1024


def sort_kernel(layers, place, slab, *outs):
    feats = ROWBLOCK // layers
    kept = len(outs)
    row = lax.broadcasted_iota(jnp.int32, (ROWBLOCK, ROWBLOCK), 0)
    col = lax.broadcasted_iota(jnp.int32, (ROWBLOCK, ROWBLOCK), 1)
    layer = row // feats % 2 * kept + ((row // (2 * feats)) ^ place[0])
    order = jnp.where(col == row % feats * layers + layer, 1.0, 0.0).astype(jnp.bfloat16)
    moved = jnp.dot(order, slab[...], preferred_element_type=jnp.float32).astype(jnp.bfloat16)
    for n, out in enumerate(outs):
        for phase in range(2):
            at = (2 * n + phase) * feats
            out[phase] = moved[at : at + feats]


def sort_slab(slab, layers, n_tensor, turn, place):
    rows, columns = slab.shape
    kept = layers // 2
    cdev = columns // n_tensor
    feats = ROWBLOCK // layers
    return pl.pallas_call(
        functools.partial(sort_kernel, layers),
        grid_spec=pltpu.PrefetchScalarGridSpec(
            num_scalar_prefetch=1,
            grid=(rows // ROWBLOCK,),
            in_specs=[pl.BlockSpec((ROWBLOCK, cdev), lambda i, s: (i, s[1] ^ turn))],
            out_specs=[pl.BlockSpec((2, feats, cdev), lambda i, s: (0, i, 0))] * kept,
        ),
        out_shape=[jax.ShapeDtypeStruct((2, rows // layers, cdev), jnp.bfloat16)] * kept,
        compiler_params=pltpu.CompilerParams(vmem_limit_bytes=WHOLE_VMEM),
        cost_estimate=pl.CostEstimate(
            flops=2 * rows * cdev * ROWBLOCK, bytes_accessed=4 * rows * cdev, transcendentals=0
        ),
    )(place, slab)


def core_here():
    return lax.axis_index("tensor") % 2


def phase_at(tick):
    n_spot = lax.axis_size("spot")
    return (tick >= lax.axis_index("spot") + n_spot).astype(jnp.int32)


def item_at(tick):
    layer = lax.axis_index("zone") * lax.axis_size("spot") + lax.axis_index("spot")
    return jnp.clip(tick - layer, 0, ITEMS - 1)


def project_kernel(tick, tiles, tilew, n_y, table, mine, other, gains, *rest):
    weights, (out, normed, held, scalars, sems) = rest[:-5], rest[-5:]
    rows, half = mine.shape
    width = 2 * half
    shard = half // n_y
    chunks, size, cdev = held.shape
    per = size // tilew
    core, phase = core_here(), phase_at(tick)
    lookup = pltpu.make_async_copy(table, scalars, sems.at[tiles])

    def fetch(n):
        target = held.at[n // per, pl.ds(n % per * tilew, tilew)]
        return pltpu.make_async_copy(weights[n].at[phase], target, sems.at[n])

    for n in range(tiles):
        fetch(n).start()
        if n == 0:
            lookup.start()

    here = mine[...].astype(jnp.float32)
    there = other[...].astype(jnp.float32)
    total = jnp.sum(here * here, axis=1, keepdims=True)
    total = total + jnp.sum(there * there, axis=1, keepdims=True)
    inverse = lax.rsqrt(total / width + 1e-06)
    gain = jnp.where(phase == 0, gains[0:1], gains[1:2])
    low = jnp.where(core == 0, here, there) * inverse
    high = jnp.where(core == 0, there, here) * inverse
    for y in range(n_y):
        at = 2 * y * shard
        piece = slice(y * shard, (y + 1) * shard)
        normed[:, at : at + shard] = low[:, piece] * gain[:, at : at + shard]
        at = at + shard
        normed[:, at : at + shard] = high[:, piece] * gain[:, at : at + shard]
    normed[:, width:] = jnp.zeros((rows, WINDOW), jnp.float32)

    along = CHUNK // tilew
    lookup.wait()
    lane = lax.broadcasted_iota(jnp.int32, (rows, CHUNK), 1)

    def spread(j):
        value = jnp.zeros((rows, CHUNK), jnp.float32)
        for a in range(along):
            start = scalars[j * along + a] * FB
            count = scalars[tiles + j * along + a] * FB
            aligned = start // 128 * 128
            window = normed[:, pl.ds(pl.multiple_of(aligned, 128), WINDOW)]
            put = a * tilew
            shift = (put - (start - aligned) + WINDOW) % WINDOW
            rolled = pltpu.roll(window, shift, 1)[:, :CHUNK]
            value = jnp.where((lane >= put) & (lane < put + count), rolled, value)
        return value.astype(jnp.bfloat16)

    acc = jnp.zeros((rows, cdev), jnp.float32)
    for j in range(chunks):
        parts = [spread(j * (size // CHUNK) + i) for i in range(size // CHUNK)]
        for n in range(j * per, (j + 1) * per):
            fetch(n).wait()
        acc = acc + jnp.dot(
            jnp.concatenate(parts, axis=1), held[j], preferred_element_type=jnp.float32
        )
    out[...] = acc.astype(jnp.bfloat16)


def project(tick, tiles, tilew, n_y, table, mine, other, gains, weights):
    rows, half = mine.shape
    cdev = weights[0].shape[2]
    depth = tiles * tilew
    size = 2 * CHUNK
    vmem = pl.BlockSpec(memory_space=pltpu.VMEM)
    return pl.pallas_call(
        functools.partial(project_kernel, tick, tiles, tilew, n_y),
        in_specs=[pl.BlockSpec(memory_space=pltpu.HBM)]
        + [vmem] * 3
        + [pl.BlockSpec(memory_space=pltpu.HBM)] * len(weights),
        out_specs=vmem,
        scratch_shapes=[
            pltpu.VMEM((rows, 2 * half + WINDOW), jnp.float32),
            pltpu.VMEM((depth // size, size, cdev), jnp.bfloat16),
            pltpu.SMEM(table.shape, jnp.int32),
            pltpu.SemaphoreType.DMA((tiles + 1,)),
        ],
        out_shape=jax.ShapeDtypeStruct((rows, cdev), jnp.bfloat16),
        compiler_params=pltpu.CompilerParams(vmem_limit_bytes=VMEM if tick else WHOLE_VMEM),
        cost_estimate=pl.CostEstimate(
            flops=2 * rows * depth * cdev, bytes_accessed=2 * depth * cdev, transcendentals=0
        ),
    )(table, mine, other, gains, *weights)


def attend_kernel(steps, brow, kvlocal, groups, n_y, tick, own, sent, spans, ckeys, cvals, wo, theirs, ours, attn, kheld, vheld, held, sems):
    rows = steps * brow
    length = ckeys.shape[1]
    scale = 1.0 / HDIM**0.5
    qdim = kvlocal * groups * HDIM
    kvdim = kvlocal * HDIM
    shard = held.shape[2]
    core = core_here()
    item = item_at(tick)
    first = pl.multiple_of(item * brow, brow)
    gets = [
        pltpu.make_async_copy(ckeys.at[pl.ds(first, brow)], kheld, sems.at[2 * n_y]),
        pltpu.make_async_copy(cvals.at[pl.ds(first, brow)], vheld, sems.at[2 * n_y + 1]),
    ]
    for k in range(2 * n_y):
        side = 1 - core if k < n_y else core
        at = pl.multiple_of((k % n_y * 2 + side) * shard, shard)
        gets.append(
            pltpu.make_async_copy(wo.at[0, :, pl.ds(at, shard)], held.at[k], sems.at[k])
        )
    for get in gets:
        get.start()
    gets[0].wait()
    gets[1].wait()
    span = spans[item]

    qkv = (own[...].astype(jnp.float32) + sent[...].astype(jnp.float32)).astype(jnp.bfloat16)
    qkv = qkv.astype(jnp.float32)
    keys = kheld[...].reshape(brow * length, kvdim)
    values = vheld[...].reshape(brow * length, kvdim)
    tall = groups * rows
    at = lax.broadcasted_iota(jnp.int32, (tall, brow * length), 0)
    col = lax.broadcasted_iota(jnp.int32, (tall, brow * length), 1)
    cmask = (at % brow == col // length) & (col % length < span)
    at = lax.broadcasted_iota(jnp.int32, (tall, rows), 0)
    col = lax.broadcasted_iota(jnp.int32, (tall, rows), 1)
    nmask = (at % brow == col % brow) & (col // brow <= at % rows // brow)
    contract = (((1,), (1,)), ((), ()))
    for head in range(kvlocal):
        lanes = slice(head * HDIM, (head + 1) * HDIM)
        first = head * groups * HDIM
        query = jnp.concatenate(
            [qkv[:, first + g * HDIM : first + (g + 1) * HDIM] for g in range(groups)], axis=0
        ).astype(jnp.bfloat16)
        at = qdim + head * HDIM
        knew = qkv[:, at : at + HDIM].astype(jnp.bfloat16)
        at = at + kvdim
        vnew = qkv[:, at : at + HDIM].astype(jnp.bfloat16)
        scache = scale * lax.dot_general(
            query, keys[:, lanes], contract, preferred_element_type=jnp.float32
        )
        snew = scale * lax.dot_general(
            query, knew, contract, preferred_element_type=jnp.float32
        )
        scache = jnp.where(cmask, scache, -1e30)
        snew = jnp.where(nmask, snew, -1e30)
        top = jnp.maximum(
            jnp.max(scache, axis=1, keepdims=True), jnp.max(snew, axis=1, keepdims=True)
        )
        ecache = jnp.where(cmask, jnp.exp(scache - top), 0.0)
        enew = jnp.where(nmask, jnp.exp(snew - top), 0.0)
        total = jnp.sum(ecache, axis=1, keepdims=True) + jnp.sum(enew, axis=1, keepdims=True)
        inverse = 1.0 / total
        wcache = (ecache * inverse).astype(jnp.bfloat16)
        wnew = (enew * inverse).astype(jnp.bfloat16)
        mixed = jnp.dot(wcache, values[:, lanes], preferred_element_type=jnp.float32)
        mixed = mixed + jnp.dot(wnew, vnew, preferred_element_type=jnp.float32)
        for g in range(groups):
            attn[:, first + g * HDIM : first + (g + 1) * HDIM] = mixed[
                g * rows : (g + 1) * rows
            ].astype(jnp.bfloat16)

    for k in range(2 * n_y):
        gets[2 + k].wait()
        product = jnp.dot(attn[...], held[k], preferred_element_type=jnp.float32)
        target = theirs if k < n_y else ours
        at = k % n_y * shard
        target[:, at : at + shard] = product.astype(jnp.bfloat16)


def attend(tick, steps, brow, n_y, own, sent, spans, keys, values, wo):
    rows, cdev = own.shape
    _, qdim, width = wo.shape
    length, kvdim = keys.shape[1:]
    kvlocal = kvdim // HDIM
    groups = qdim // kvdim
    shard = width // (2 * n_y)
    vmem = pl.BlockSpec(memory_space=pltpu.VMEM)
    return pl.pallas_call(
        functools.partial(attend_kernel, steps, brow, kvlocal, groups, n_y, tick),
        in_specs=[vmem] * 3
        + [pl.BlockSpec(memory_space=pltpu.HBM)] * 3,
        out_specs=[vmem] * 2,
        scratch_shapes=[
            pltpu.VMEM((rows, qdim), jnp.bfloat16),
            pltpu.VMEM((brow, length, kvdim), jnp.bfloat16),
            pltpu.VMEM((brow, length, kvdim), jnp.bfloat16),
            pltpu.VMEM((2 * n_y, qdim, shard), jnp.bfloat16),
            pltpu.SemaphoreType.DMA((2 * n_y + 2,)),
        ],
        out_shape=[jax.ShapeDtypeStruct((rows, shard * n_y), jnp.bfloat16)] * 2,
        compiler_params=pltpu.CompilerParams(vmem_limit_bytes=VMEM),
        cost_estimate=pl.CostEstimate(
            flops=2 * rows * qdim * width, bytes_accessed=2 * qdim * width, transcendentals=0
        ),
    )(own, sent, spans, keys, values, wo)


def join_kernel(part, moved, mine, out):
    total = part[...].astype(jnp.float32) + moved[...].astype(jnp.float32)
    out[...] = (mine[...].astype(jnp.float32) + total).astype(jnp.bfloat16)


def choose_kernel(tick, near, far, out):
    at_home = phase_at(tick) == lax.axis_index("zone")
    out[...] = jnp.where(at_home, near[...], far[...])


def in_vmem(kernel, *arrays):
    vmem = pl.BlockSpec(memory_space=pltpu.VMEM)
    return pl.pallas_call(
        kernel,
        in_specs=[vmem] * len(arrays),
        out_specs=vmem,
        out_shape=jax.ShapeDtypeStruct(arrays[0].shape, jnp.bfloat16),
        compiler_params=pltpu.CompilerParams(vmem_limit_bytes=VMEM),
    )(*arrays)


def per_device(
    trainer_tiles,
    tile_lengths,
    wo_rollout,
    cache_keys,
    cache_values,
    cache_lengths,
    norm_gain,
    step_inputs,
):
    n_zone = lax.axis_size("zone")
    n_spot = lax.axis_size("spot")
    n_tensor = lax.axis_size("tensor")
    layers = n_zone * n_spot
    tiles = n_spot * n_tensor
    n_y = n_tensor // 2
    slab, columns = trainer_tiles.shape
    cdev = columns // n_tensor
    tilew = slab // layers
    width = wo_rollout.shape[2]
    shard = width // n_tensor
    half = n_y * shard
    steps = step_inputs.shape[0]
    seqs, length = cache_keys.shape[1:3]
    brow = seqs // ITEMS
    rows = steps * brow
    ticks = layers + ITEMS - 1
    zone = lax.axis_index("zone")
    spot = lax.axis_index("spot")
    tpos = lax.axis_index("tensor")
    core = tpos % 2
    layer = zone * n_spot + spot

    all_s, all_t = n_spot - 1, n_tensor - 2
    turns = sorted(range(n_tensor), key=lambda kt: (kt % 2, kt))
    offsets = [(ks, kt) for kt in turns for ks in range(n_spot)]
    place = jnp.stack([spot ^ core * all_s, tpos ^ core * all_t]).astype(jnp.int32)

    def exchange(offset, piece):
        pairs = []
        for s in range(n_spot):
            for t in range(n_tensor):
                bits = 1 if offset == (all_s, all_t) else t % 2
                ks, kt = (0, 0) if offset == (all_s, all_t) else offset
                target = (s ^ ks ^ bits * all_s) * n_tensor + (t ^ kt ^ bits * all_t)
                pairs.append((s * n_tensor + t, target))
        return lax.ppermute(piece, ("spot", "tensor"), pairs)

    pieces = {}
    for kt in turns:
        for ks, piece in enumerate(sort_slab(trainer_tiles, layers, n_tensor, kt, place)):
            pieces[ks, kt] = piece
        place, _ = lax.optimization_barrier((place, piece))
    first, last = pieces[0, 0], pieces[all_s, all_t]
    pieces[0, 0] = jnp.where(core == 0, first, last)
    pieces[all_s, all_t] = jnp.where(core == 0, last, first)
    weights = [
        exchange(offset, pieces[offset]) if offset != (0, 0) else pieces[offset]
        for offset in offsets
    ]

    ends = jnp.cumsum(tile_lengths)
    offset = np.array(offsets, np.int32)
    sender = (offset[:, 1] % 2) ^ core
    fixed = (offset == [0, 0]).all(axis=1) | (offset == [all_s, all_t]).all(axis=1)
    sender = jnp.where(fixed, 0, sender)
    sources = (offset[:, 0] ^ spot ^ sender * all_s) * n_tensor
    sources = sources + (offset[:, 1] ^ tpos ^ sender * all_t) + zone * tiles
    starts = (ends - tile_lengths)[sources]
    counts = tile_lengths[sources]
    table = jnp.concatenate([starts, counts]).astype(jnp.int32)
    flip = [(z, 1 - z) for z in range(2)]
    swapped = lax.ppermute(norm_gain, "zone", flip)
    gains = jnp.concatenate(
        [jnp.where(zone == 0, norm_gain, swapped), jnp.where(zone == 0, swapped, norm_gain)]
    )
    spans = jnp.repeat(cache_lengths, length).reshape(ITEMS, 1, brow * length)
    axes = ("zone", "spot", "tensor")

    def spots(tick):
        return sorted({(tick - i) % n_spot for i in range(ITEMS)})

    def hop(tick, turn):
        pairs = []
        for s in spots(tick):
            for z in range(n_zone):
                ahead = z if s + 1 < n_spot else 1 - z
                pairs.append((z * n_spot + s, (ahead ^ turn) * n_spot + (s + 1) % n_spot))
        return sorted(pairs)

    def mirror(tick):
        return sorted(
            (z * n_spot + s, (1 - z) * n_spot + s) for s in spots(tick) for z in range(n_zone)
        )

    across = [(t, t ^ 1) for t in range(n_tensor)]
    shown = step_inputs.reshape(steps, ITEMS, brow, n_y, 2, shard)
    records = []
    arrived, record = None, []
    for tick in range(ticks):
        if tick < ITEMS:
            fresh = shown[:, tick].reshape(rows, n_y, 2, shard)
            mine = lax.dynamic_index_in_dim(fresh, core, 2, False).reshape(rows, half)
            mine = jnp.where(spot == 0, mine, arrived if tick else 0)
        else:
            mine = arrived
        if tick:
            other = lax.ppermute(mine, "tensor", across)
        else:
            other = lax.dynamic_index_in_dim(fresh, 1 - core, 2, False).reshape(rows, half)
        own = project(tick, tiles, tilew, n_y, table, mine, other, gains, weights)
        sent = lax.ppermute(own, ("zone", "spot"), mirror(tick))
        theirs, ours = attend(
            tick, steps, brow, n_y, own, sent, spans, cache_keys[0], cache_values[0], wo_rollout
        )
        moved = lax.ppermute(theirs, "tensor", across)
        part = (ours.astype(jnp.float32) + moved.astype(jnp.float32)).astype(jnp.bfloat16)
        bit = 2
        while bit < n_tensor:
            moved = lax.ppermute(part, "tensor", [(t, t ^ bit) for t in range(n_tensor)])
            bit = bit * 2
            if bit < n_tensor:
                part = part.astype(jnp.float32) + moved.astype(jnp.float32)
                part = part.astype(jnp.bfloat16)
        after = in_vmem(join_kernel, part, moved, mine)
        record.append(after)
        if tick + 1 < ticks:
            far = lax.ppermute(after, ("zone", "spot"), hop(tick, 1))
            near = lax.ppermute(after, ("zone", "spot"), hop(tick, 0))
            arrived = in_vmem(functools.partial(choose_kernel, tick + 1), near, far)
    for item in range(ITEMS):
        value = jnp.zeros((rows, half), jnp.bfloat16)
        for tick in range(item, ticks):
            value = jnp.where(layer == tick - item, record[tick], value)
        value = lax.dynamic_slice_in_dim(value, tpos // 2 * shard, shard, 1)
        records.append(value.astype(jnp.float32).reshape(steps, brow, shard))
    return jnp.concatenate(records, axis=1)[None]


def solution(mesh):
    n_section, n_tensor = mesh.devices.shape
    fine = Mesh(mesh.devices.reshape(2, n_section // 2, n_tensor), ("zone", "spot", "tensor"))
    section = ("zone", "spot")
    placed = (
        P(("zone", "spot", "tensor"), None),
        P(),
        P(section, "tensor", None),
        P(section, None, None, "tensor"),
        P(section, None, None, "tensor"),
        P(),
        P(section, None),
        P(),
    )
    return jax.shard_map(
        per_device,
        mesh=fine,
        in_specs=placed,
        out_specs=P(section, None, None, "tensor"),
        check_vma=False,
    )
```

```python
import functools

import jax
import jax.numpy as jnp
import numpy as np
from jax import lax
from jax.experimental import pallas as pl
from jax.experimental.pallas import tpu as pltpu
from jax.sharding import Mesh, PartitionSpec as P

HDIM = 128
FB = 8
ITEMS = 4
ROWBLOCK = 256
CHUNK = 384
WINDOW = 512
VMEM = 48 * 1024 * 1024
WHOLE_VMEM = 62 * 1024 * 1024


def sort_kernel(layers, place, slab, *outs):
    feats = ROWBLOCK // layers
    kept = len(outs)
    row = lax.broadcasted_iota(jnp.int32, (ROWBLOCK, ROWBLOCK), 0)
    col = lax.broadcasted_iota(jnp.int32, (ROWBLOCK, ROWBLOCK), 1)
    layer = row // feats % 2 * kept + ((row // (2 * feats)) ^ place[0])
    order = jnp.where(col == row % feats * layers + layer, 1.0, 0.0).astype(jnp.bfloat16)
    moved = jnp.dot(order, slab[...], preferred_element_type=jnp.float32).astype(jnp.bfloat16)
    for n, out in enumerate(outs):
        for phase in range(2):
            at = (2 * n + phase) * feats
            out[phase] = moved[at : at + feats]


def sort_slab(slab, layers, n_tensor, turn, place):
    rows, columns = slab.shape
    kept = layers // 2
    cdev = columns // n_tensor
    feats = ROWBLOCK // layers
    return pl.pallas_call(
        functools.partial(sort_kernel, layers),
        grid_spec=pltpu.PrefetchScalarGridSpec(
            num_scalar_prefetch=1,
            grid=(rows // ROWBLOCK,),
            in_specs=[pl.BlockSpec((ROWBLOCK, cdev), lambda i, s: (i, s[1] ^ turn))],
            out_specs=[pl.BlockSpec((2, feats, cdev), lambda i, s: (0, i, 0))] * kept,
        ),
        out_shape=[jax.ShapeDtypeStruct((2, rows // layers, cdev), jnp.bfloat16)] * kept,
        compiler_params=pltpu.CompilerParams(vmem_limit_bytes=WHOLE_VMEM),
        cost_estimate=pl.CostEstimate(
            flops=2 * rows * cdev * ROWBLOCK, bytes_accessed=4 * rows * cdev, transcendentals=0
        ),
    )(place, slab)


def core_here():
    return lax.axis_index("tensor") % 2


def phase_at(tick):
    n_spot = lax.axis_size("spot")
    return (tick >= lax.axis_index("spot") + n_spot).astype(jnp.int32)


def item_at(tick):
    layer = lax.axis_index("zone") * lax.axis_size("spot") + lax.axis_index("spot")
    return jnp.clip(tick - layer, 0, ITEMS - 1)


def project_kernel(tick, tiles, tilew, n_y, table, mine, other, gains, *rest):
    weights, (out, normed, held, scalars, sems) = rest[:-5], rest[-5:]
    rows, half = mine.shape
    width = 2 * half
    shard = half // n_y
    chunks, size, cdev = held.shape
    per = size // tilew
    core, phase = core_here(), phase_at(tick)
    lookup = pltpu.make_async_copy(table, scalars, sems.at[tiles])

    def fetch(n):
        target = held.at[n // per, pl.ds(n % per * tilew, tilew)]
        return pltpu.make_async_copy(weights[n].at[phase], target, sems.at[n])

    for n in range(tiles):
        fetch(n).start()
        if n == 0:
            lookup.start()

    here = mine[...].astype(jnp.float32)
    there = other[...].astype(jnp.float32)
    total = jnp.sum(here * here, axis=1, keepdims=True)
    total = total + jnp.sum(there * there, axis=1, keepdims=True)
    inverse = lax.rsqrt(total / width + 1e-06)
    gain = jnp.where(phase == 0, gains[0:1], gains[1:2])
    low = jnp.where(core == 0, here, there) * inverse
    high = jnp.where(core == 0, there, here) * inverse
    for y in range(n_y):
        at = 2 * y * shard
        piece = slice(y * shard, (y + 1) * shard)
        normed[:, at : at + shard] = low[:, piece] * gain[:, at : at + shard]
        at = at + shard
        normed[:, at : at + shard] = high[:, piece] * gain[:, at : at + shard]
    normed[:, width:] = jnp.zeros((rows, WINDOW), jnp.float32)

    along = CHUNK // tilew
    lookup.wait()
    lane = lax.broadcasted_iota(jnp.int32, (rows, CHUNK), 1)

    def spread(j):
        value = jnp.zeros((rows, CHUNK), jnp.float32)
        for a in range(along):
            start = scalars[j * along + a] * FB
            count = scalars[tiles + j * along + a] * FB
            aligned = start // 128 * 128
            window = normed[:, pl.ds(pl.multiple_of(aligned, 128), WINDOW)]
            put = a * tilew
            shift = (put - (start - aligned) + WINDOW) % WINDOW
            rolled = pltpu.roll(window, shift, 1)[:, :CHUNK]
            value = jnp.where((lane >= put) & (lane < put + count), rolled, value)
        return value.astype(jnp.bfloat16)

    acc = jnp.zeros((rows, cdev), jnp.float32)
    for j in range(chunks):
        parts = [spread(j * (size // CHUNK) + i) for i in range(size // CHUNK)]
        for n in range(j * per, (j + 1) * per):
            fetch(n).wait()
        acc = acc + jnp.dot(
            jnp.concatenate(parts, axis=1), held[j], preferred_element_type=jnp.float32
        )
    out[...] = acc.astype(jnp.bfloat16)


def project(tick, tiles, tilew, n_y, table, mine, other, gains, weights):
    rows, half = mine.shape
    cdev = weights[0].shape[2]
    depth = tiles * tilew
    size = 2 * CHUNK
    vmem = pl.BlockSpec(memory_space=pltpu.VMEM)
    return pl.pallas_call(
        functools.partial(project_kernel, tick, tiles, tilew, n_y),
        in_specs=[pl.BlockSpec(memory_space=pltpu.HBM)]
        + [vmem] * 3
        + [pl.BlockSpec(memory_space=pltpu.HBM)] * len(weights),
        out_specs=vmem,
        scratch_shapes=[
            pltpu.VMEM((rows, 2 * half + WINDOW), jnp.float32),
            pltpu.VMEM((depth // size, size, cdev), jnp.bfloat16),
            pltpu.SMEM(table.shape, jnp.int32),
            pltpu.SemaphoreType.DMA((tiles + 1,)),
        ],
        out_shape=jax.ShapeDtypeStruct((rows, cdev), jnp.bfloat16),
        compiler_params=pltpu.CompilerParams(vmem_limit_bytes=VMEM if tick else WHOLE_VMEM),
        cost_estimate=pl.CostEstimate(
            flops=2 * rows * depth * cdev, bytes_accessed=2 * depth * cdev, transcendentals=0
        ),
    )(table, mine, other, gains, *weights)


def attend_kernel(steps, brow, kvlocal, groups, n_y, tick, own, sent, spans, ckeys, cvals, wo, theirs, ours, attn, kheld, vheld, held, sems):
    rows = steps * brow
    length = ckeys.shape[1]
    scale = 1.0 / HDIM**0.5
    qdim = kvlocal * groups * HDIM
    kvdim = kvlocal * HDIM
    shard = held.shape[2]
    core = core_here()
    item = item_at(tick)
    first = pl.multiple_of(item * brow, brow)
    gets = [
        pltpu.make_async_copy(ckeys.at[pl.ds(first, brow)], kheld, sems.at[2 * n_y]),
        pltpu.make_async_copy(cvals.at[pl.ds(first, brow)], vheld, sems.at[2 * n_y + 1]),
    ]
    for k in range(2 * n_y):
        side = 1 - core if k < n_y else core
        at = pl.multiple_of((k % n_y * 2 + side) * shard, shard)
        gets.append(
            pltpu.make_async_copy(wo.at[0, :, pl.ds(at, shard)], held.at[k], sems.at[k])
        )
    for get in gets:
        get.start()
    gets[0].wait()
    gets[1].wait()
    span = spans[item]

    qkv = (own[...].astype(jnp.float32) + sent[...].astype(jnp.float32)).astype(jnp.bfloat16)
    qkv = qkv.astype(jnp.float32)
    keys = kheld[...].reshape(brow * length, kvdim)
    values = vheld[...].reshape(brow * length, kvdim)
    tall = groups * rows
    at = lax.broadcasted_iota(jnp.int32, (tall, brow * length), 0)
    col = lax.broadcasted_iota(jnp.int32, (tall, brow * length), 1)
    cmask = (at % brow == col // length) & (col % length < span)
    at = lax.broadcasted_iota(jnp.int32, (tall, rows), 0)
    col = lax.broadcasted_iota(jnp.int32, (tall, rows), 1)
    nmask = (at % brow == col % brow) & (col // brow <= at % rows // brow)
    contract = (((1,), (1,)), ((), ()))
    for head in range(kvlocal):
        lanes = slice(head * HDIM, (head + 1) * HDIM)
        first = head * groups * HDIM
        query = jnp.concatenate(
            [qkv[:, first + g * HDIM : first + (g + 1) * HDIM] for g in range(groups)], axis=0
        ).astype(jnp.bfloat16)
        at = qdim + head * HDIM
        knew = qkv[:, at : at + HDIM].astype(jnp.bfloat16)
        at = at + kvdim
        vnew = qkv[:, at : at + HDIM].astype(jnp.bfloat16)
        scache = scale * lax.dot_general(
            query, keys[:, lanes], contract, preferred_element_type=jnp.float32
        )
        snew = scale * lax.dot_general(
            query, knew, contract, preferred_element_type=jnp.float32
        )
        scache = jnp.where(cmask, scache, -1e30)
        snew = jnp.where(nmask, snew, -1e30)
        top = jnp.maximum(
            jnp.max(scache, axis=1, keepdims=True), jnp.max(snew, axis=1, keepdims=True)
        )
        ecache = jnp.where(cmask, jnp.exp(scache - top), 0.0)
        enew = jnp.where(nmask, jnp.exp(snew - top), 0.0)
        total = jnp.sum(ecache, axis=1, keepdims=True) + jnp.sum(enew, axis=1, keepdims=True)
        inverse = 1.0 / total
        wcache = (ecache * inverse).astype(jnp.bfloat16)
        wnew = (enew * inverse).astype(jnp.bfloat16)
        mixed = jnp.dot(wcache, values[:, lanes], preferred_element_type=jnp.float32)
        mixed = mixed + jnp.dot(wnew, vnew, preferred_element_type=jnp.float32)
        for g in range(groups):
            attn[:, first + g * HDIM : first + (g + 1) * HDIM] = mixed[
                g * rows : (g + 1) * rows
            ].astype(jnp.bfloat16)

    for k in range(2 * n_y):
        gets[2 + k].wait()
        product = jnp.dot(attn[...], held[k], preferred_element_type=jnp.float32)
        target = theirs if k < n_y else ours
        at = k % n_y * shard
        target[:, at : at + shard] = product.astype(jnp.bfloat16)


def attend(tick, steps, brow, n_y, own, sent, spans, keys, values, wo):
    rows, cdev = own.shape
    _, qdim, width = wo.shape
    length, kvdim = keys.shape[1:]
    kvlocal = kvdim // HDIM
    groups = qdim // kvdim
    shard = width // (2 * n_y)
    vmem = pl.BlockSpec(memory_space=pltpu.VMEM)
    return pl.pallas_call(
        functools.partial(attend_kernel, steps, brow, kvlocal, groups, n_y, tick),
        in_specs=[vmem] * 3
        + [pl.BlockSpec(memory_space=pltpu.HBM)] * 3,
        out_specs=[vmem] * 2,
        scratch_shapes=[
            pltpu.VMEM((rows, qdim), jnp.bfloat16),
            pltpu.VMEM((brow, length, kvdim), jnp.bfloat16),
            pltpu.VMEM((brow, length, kvdim), jnp.bfloat16),
            pltpu.VMEM((2 * n_y, qdim, shard), jnp.bfloat16),
            pltpu.SemaphoreType.DMA((2 * n_y + 2,)),
        ],
        out_shape=[jax.ShapeDtypeStruct((rows, shard * n_y), jnp.bfloat16)] * 2,
        compiler_params=pltpu.CompilerParams(vmem_limit_bytes=VMEM),
        cost_estimate=pl.CostEstimate(
            flops=2 * rows * qdim * width, bytes_accessed=2 * qdim * width, transcendentals=0
        ),
    )(own, sent, spans, keys, values, wo)


def join_kernel(part, moved, mine, out):
    total = part[...].astype(jnp.float32) + moved[...].astype(jnp.float32)
    out[...] = (mine[...].astype(jnp.float32) + total).astype(jnp.bfloat16)


def copy_kernel(value, out):
    out[...] = value[...]


def choose_kernel(tick, far, near, out):
    at_home = phase_at(tick) == lax.axis_index("zone")
    out[...] = jnp.where(at_home, near[...], far[...])


def in_vmem(kernel, *arrays):
    vmem = pl.BlockSpec(memory_space=pltpu.VMEM)
    return pl.pallas_call(
        kernel,
        in_specs=[vmem] * len(arrays),
        out_specs=vmem,
        out_shape=jax.ShapeDtypeStruct(arrays[0].shape, jnp.bfloat16),
        compiler_params=pltpu.CompilerParams(vmem_limit_bytes=VMEM),
    )(*arrays)


def per_device(
    trainer_tiles,
    tile_lengths,
    wo_rollout,
    cache_keys,
    cache_values,
    cache_lengths,
    norm_gain,
    step_inputs,
):
    n_zone = lax.axis_size("zone")
    n_spot = lax.axis_size("spot")
    n_tensor = lax.axis_size("tensor")
    layers = n_zone * n_spot
    tiles = n_spot * n_tensor
    n_y = n_tensor // 2
    slab, columns = trainer_tiles.shape
    cdev = columns // n_tensor
    tilew = slab // layers
    width = wo_rollout.shape[2]
    shard = width // n_tensor
    half = n_y * shard
    steps = step_inputs.shape[0]
    seqs, length = cache_keys.shape[1:3]
    brow = seqs // ITEMS
    rows = steps * brow
    ticks = layers + ITEMS - 1
    zone = lax.axis_index("zone")
    spot = lax.axis_index("spot")
    tpos = lax.axis_index("tensor")
    core = tpos % 2
    layer = zone * n_spot + spot

    all_s, all_t = n_spot - 1, n_tensor - 2
    turns = sorted(range(n_tensor), key=lambda kt: (kt % 2, kt))
    offsets = [(ks, kt) for kt in turns for ks in range(n_spot)]
    place = jnp.stack([spot ^ core * all_s, tpos ^ core * all_t]).astype(jnp.int32)

    def exchange(offset, piece):
        pairs = []
        for s in range(n_spot):
            for t in range(n_tensor):
                bits = 1 if offset == (all_s, all_t) else t % 2
                ks, kt = (0, 0) if offset == (all_s, all_t) else offset
                target = (s ^ ks ^ bits * all_s) * n_tensor + (t ^ kt ^ bits * all_t)
                pairs.append((s * n_tensor + t, target))
        return lax.ppermute(piece, ("spot", "tensor"), pairs)

    pieces = {}
    for kt in turns:
        for ks, piece in enumerate(sort_slab(trainer_tiles, layers, n_tensor, kt, place)):
            pieces[ks, kt] = piece
        place, _ = lax.optimization_barrier((place, piece))
    first, last = pieces[0, 0], pieces[all_s, all_t]
    pieces[0, 0] = jnp.where(core == 0, first, last)
    pieces[all_s, all_t] = jnp.where(core == 0, last, first)
    weights = [
        exchange(offset, pieces[offset]) if offset != (0, 0) else pieces[offset]
        for offset in offsets
    ]

    ends = jnp.cumsum(tile_lengths)
    offset = np.array(offsets, np.int32)
    sender = (offset[:, 1] % 2) ^ core
    fixed = (offset == [0, 0]).all(axis=1) | (offset == [all_s, all_t]).all(axis=1)
    sender = jnp.where(fixed, 0, sender)
    sources = (offset[:, 0] ^ spot ^ sender * all_s) * n_tensor
    sources = sources + (offset[:, 1] ^ tpos ^ sender * all_t) + zone * tiles
    starts = (ends - tile_lengths)[sources]
    counts = tile_lengths[sources]
    table = jnp.concatenate([starts, counts]).astype(jnp.int32)
    flip = [(z, 1 - z) for z in range(2)]
    swapped = lax.ppermute(norm_gain, "zone", flip)
    gains = jnp.concatenate(
        [jnp.where(zone == 0, norm_gain, swapped), jnp.where(zone == 0, swapped, norm_gain)]
    )
    spans = jnp.repeat(cache_lengths, length).reshape(ITEMS, 1, brow * length)
    axes = ("zone", "spot", "tensor")

    def actives(tick):
        held = {(tick - i) % n_spot for i in range(ITEMS)}
        return [(s, int(tick >= s + n_spot)) for s in sorted(held)]

    def hop(tick, turn):
        pairs = []
        for s, z in actives(tick):
            ahead = z if s + 1 < n_spot else 1 - z
            pairs.append((z * n_spot + s, (ahead ^ turn) * n_spot + (s + 1) % n_spot))
        return sorted(pairs)

    def mirror(tick):
        return sorted(((1 - z) * n_spot + s, z * n_spot + s) for s, z in actives(tick))

    across = [(t, t ^ 1) for t in range(n_tensor)]
    shown = step_inputs.reshape(steps, ITEMS, brow, n_y, 2, shard)
    records = []
    arrived, record = None, []
    for tick in range(ticks):
        if tick < ITEMS:
            fresh = shown[:, tick].reshape(rows, n_y, 2, shard)
            mine = lax.dynamic_index_in_dim(fresh, core, 2, False).reshape(rows, half)
            mine = jnp.where(spot == 0, mine, arrived if tick else 0)
        else:
            mine = arrived
        if tick:
            other = lax.ppermute(mine, "tensor", across)
        else:
            other = lax.dynamic_index_in_dim(fresh, 1 - core, 2, False).reshape(rows, half)
        own = project(tick, tiles, tilew, n_y, table, mine, other, gains, weights)
        sent = lax.ppermute(own, ("zone", "spot"), mirror(tick))
        theirs, ours = attend(
            tick, steps, brow, n_y, own, sent, spans, cache_keys[0], cache_values[0], wo_rollout
        )
        moved = lax.ppermute(theirs, "tensor", across)
        part = (ours.astype(jnp.float32) + moved.astype(jnp.float32)).astype(jnp.bfloat16)
        bit = 2
        while bit < n_tensor:
            moved = lax.ppermute(part, "tensor", [(t, t ^ bit) for t in range(n_tensor)])
            bit = bit * 2
            if bit < n_tensor:
                part = part.astype(jnp.float32) + moved.astype(jnp.float32)
                part = part.astype(jnp.bfloat16)
        after = in_vmem(join_kernel, part, moved, mine)
        record.append(after)
        if tick + 1 < ticks:
            far = lax.ppermute(after, ("zone", "spot"), hop(tick, 1))
            behind = in_vmem(copy_kernel, after)
            near = lax.ppermute(behind, ("zone", "spot"), hop(tick, 0))
            arrived = in_vmem(functools.partial(choose_kernel, tick + 1), far, near)
    for item in range(ITEMS):
        value = jnp.zeros((rows, half), jnp.bfloat16)
        for tick in range(item, ticks):
            value = jnp.where(layer == tick - item, record[tick], value)
        value = lax.dynamic_slice_in_dim(value, tpos // 2 * shard, shard, 1)
        records.append(value.astype(jnp.float32).reshape(steps, brow, shard))
    return jnp.concatenate(records, axis=1)[None]


def solution(mesh):
    n_section, n_tensor = mesh.devices.shape
    fine = Mesh(mesh.devices.reshape(2, n_section // 2, n_tensor), ("zone", "spot", "tensor"))
    section = ("zone", "spot")
    placed = (
        P(("zone", "spot", "tensor"), None),
        P(),
        P(section, "tensor", None),
        P(section, None, None, "tensor"),
        P(section, None, None, "tensor"),
        P(),
        P(section, None),
        P(),
    )
    return jax.shard_map(
        per_device,
        mesh=fine,
        in_specs=placed,
        out_specs=P(section, None, None, "tensor"),
        check_vma=False,
    )
```

```python
import functools

import jax
import jax.numpy as jnp
import numpy as np
from jax import lax
from jax.experimental import pallas as pl
from jax.experimental.pallas import tpu as pltpu
from jax.sharding import Mesh, PartitionSpec as P

HDIM = 128
FB = 8
ITEMS = 4
ROWBLOCK = 256
CHUNK = 384
WINDOW = 512
VMEM = 48 * 1024 * 1024
WHOLE_VMEM = 62 * 1024 * 1024


def sort_kernel(layers, place, slab, *outs):
    feats = ROWBLOCK // layers
    kept = len(outs)
    row = lax.broadcasted_iota(jnp.int32, (ROWBLOCK, ROWBLOCK), 0)
    col = lax.broadcasted_iota(jnp.int32, (ROWBLOCK, ROWBLOCK), 1)
    layer = row // feats % 2 * kept + ((row // (2 * feats)) ^ place[0])
    order = jnp.where(col == row % feats * layers + layer, 1.0, 0.0).astype(jnp.bfloat16)
    moved = jnp.dot(order, slab[...], preferred_element_type=jnp.float32).astype(jnp.bfloat16)
    for n, out in enumerate(outs):
        for phase in range(2):
            at = (2 * n + phase) * feats
            out[phase] = moved[at : at + feats]


def sort_slab(slab, layers, n_tensor, turn, place):
    rows, columns = slab.shape
    kept = layers // 2
    cdev = columns // n_tensor
    feats = ROWBLOCK // layers
    return pl.pallas_call(
        functools.partial(sort_kernel, layers),
        grid_spec=pltpu.PrefetchScalarGridSpec(
            num_scalar_prefetch=1,
            grid=(rows // ROWBLOCK,),
            in_specs=[pl.BlockSpec((ROWBLOCK, cdev), lambda i, s: (i, s[1] ^ turn))],
            out_specs=[pl.BlockSpec((2, feats, cdev), lambda i, s: (0, i, 0))] * kept,
        ),
        out_shape=[jax.ShapeDtypeStruct((2, rows // layers, cdev), jnp.bfloat16)] * kept,
        compiler_params=pltpu.CompilerParams(vmem_limit_bytes=WHOLE_VMEM),
        cost_estimate=pl.CostEstimate(
            flops=2 * rows * cdev * ROWBLOCK, bytes_accessed=4 * rows * cdev, transcendentals=0
        ),
    )(place, slab)


def core_here():
    return lax.axis_index("tensor") % 2


def phase_at(tick):
    n_spot = lax.axis_size("spot")
    return (tick >= lax.axis_index("spot") + n_spot).astype(jnp.int32)


def item_at(tick):
    layer = lax.axis_index("zone") * lax.axis_size("spot") + lax.axis_index("spot")
    return jnp.clip(tick - layer, 0, ITEMS - 1)


def project_kernel(tick, tiles, tilew, n_y, table, mine, other, gains, *rest):
    weights, (out, normed, held, scalars, sems) = rest[:-5], rest[-5:]
    rows, half = mine.shape
    width = 2 * half
    shard = half // n_y
    chunks, size, cdev = held.shape
    per = size // tilew
    core, phase = core_here(), phase_at(tick)
    lookup = pltpu.make_async_copy(table, scalars, sems.at[tiles])

    def fetch(n):
        target = held.at[n // per, pl.ds(n % per * tilew, tilew)]
        return pltpu.make_async_copy(weights[n].at[phase], target, sems.at[n])

    for n in range(tiles):
        fetch(n).start()
        if n == 0:
            lookup.start()

    here = mine[...].astype(jnp.float32)
    there = other[...].astype(jnp.float32)
    total = jnp.sum(here * here, axis=1, keepdims=True)
    total = total + jnp.sum(there * there, axis=1, keepdims=True)
    inverse = lax.rsqrt(total / width + 1e-06)
    gain = jnp.where(phase == 0, gains[0:1], gains[1:2])
    low = jnp.where(core == 0, here, there) * inverse
    high = jnp.where(core == 0, there, here) * inverse
    for y in range(n_y):
        at = 2 * y * shard
        piece = slice(y * shard, (y + 1) * shard)
        normed[:, at : at + shard] = low[:, piece] * gain[:, at : at + shard]
        at = at + shard
        normed[:, at : at + shard] = high[:, piece] * gain[:, at : at + shard]
    normed[:, width:] = jnp.zeros((rows, WINDOW), jnp.float32)

    along = CHUNK // tilew
    lookup.wait()
    lane = lax.broadcasted_iota(jnp.int32, (rows, CHUNK), 1)

    def spread(j):
        value = jnp.zeros((rows, CHUNK), jnp.float32)
        for a in range(along):
            start = scalars[j * along + a] * FB
            count = scalars[tiles + j * along + a] * FB
            aligned = start // 128 * 128
            window = normed[:, pl.ds(pl.multiple_of(aligned, 128), WINDOW)]
            put = a * tilew
            shift = (put - (start - aligned) + WINDOW) % WINDOW
            rolled = pltpu.roll(window, shift, 1)[:, :CHUNK]
            value = jnp.where((lane >= put) & (lane < put + count), rolled, value)
        return value.astype(jnp.bfloat16)

    acc = jnp.zeros((rows, cdev), jnp.float32)
    for j in range(chunks):
        parts = [spread(j * (size // CHUNK) + i) for i in range(size // CHUNK)]
        for n in range(j * per, (j + 1) * per):
            fetch(n).wait()
        acc = acc + jnp.dot(
            jnp.concatenate(parts, axis=1), held[j], preferred_element_type=jnp.float32
        )
    out[...] = acc.astype(jnp.bfloat16)


def project(tick, tiles, tilew, n_y, table, mine, other, gains, weights):
    rows, half = mine.shape
    cdev = weights[0].shape[2]
    depth = tiles * tilew
    size = 2 * CHUNK
    vmem = pl.BlockSpec(memory_space=pltpu.VMEM)
    return pl.pallas_call(
        functools.partial(project_kernel, tick, tiles, tilew, n_y),
        in_specs=[pl.BlockSpec(memory_space=pltpu.HBM)]
        + [vmem] * 3
        + [pl.BlockSpec(memory_space=pltpu.HBM)] * len(weights),
        out_specs=vmem,
        scratch_shapes=[
            pltpu.VMEM((rows, 2 * half + WINDOW), jnp.float32),
            pltpu.VMEM((depth // size, size, cdev), jnp.bfloat16),
            pltpu.SMEM(table.shape, jnp.int32),
            pltpu.SemaphoreType.DMA((tiles + 1,)),
        ],
        out_shape=jax.ShapeDtypeStruct((rows, cdev), jnp.bfloat16),
        compiler_params=pltpu.CompilerParams(vmem_limit_bytes=VMEM if tick else WHOLE_VMEM),
        cost_estimate=pl.CostEstimate(
            flops=2 * rows * depth * cdev, bytes_accessed=2 * depth * cdev, transcendentals=0
        ),
    )(table, mine, other, gains, *weights)


def attend_kernel(steps, brow, kvlocal, groups, n_y, tick, own, sent, spans, ckeys, cvals, wo, theirs, ours, attn, kheld, vheld, held, sems):
    rows = steps * brow
    length = ckeys.shape[1]
    scale = 1.0 / HDIM**0.5
    qdim = kvlocal * groups * HDIM
    kvdim = kvlocal * HDIM
    shard = held.shape[2]
    core = core_here()
    item = item_at(tick)
    first = pl.multiple_of(item * brow, brow)
    gets = [
        pltpu.make_async_copy(ckeys.at[pl.ds(first, brow)], kheld, sems.at[2 * n_y]),
        pltpu.make_async_copy(cvals.at[pl.ds(first, brow)], vheld, sems.at[2 * n_y + 1]),
    ]
    for k in range(2 * n_y):
        side = 1 - core if k < n_y else core
        at = pl.multiple_of((k % n_y * 2 + side) * shard, shard)
        gets.append(
            pltpu.make_async_copy(wo.at[0, :, pl.ds(at, shard)], held.at[k], sems.at[k])
        )
    for get in gets:
        get.start()
    gets[0].wait()
    gets[1].wait()
    span = spans[item]

    qkv = (own[...].astype(jnp.float32) + sent[...].astype(jnp.float32)).astype(jnp.bfloat16)
    qkv = qkv.astype(jnp.float32)
    keys = kheld[...].reshape(brow * length, kvdim)
    values = vheld[...].reshape(brow * length, kvdim)
    tall = groups * rows
    at = lax.broadcasted_iota(jnp.int32, (tall, brow * length), 0)
    col = lax.broadcasted_iota(jnp.int32, (tall, brow * length), 1)
    cmask = (at % brow == col // length) & (col % length < span)
    at = lax.broadcasted_iota(jnp.int32, (tall, rows), 0)
    col = lax.broadcasted_iota(jnp.int32, (tall, rows), 1)
    nmask = (at % brow == col % brow) & (col // brow <= at % rows // brow)
    contract = (((1,), (1,)), ((), ()))
    for head in range(kvlocal):
        lanes = slice(head * HDIM, (head + 1) * HDIM)
        first = head * groups * HDIM
        query = jnp.concatenate(
            [qkv[:, first + g * HDIM : first + (g + 1) * HDIM] for g in range(groups)], axis=0
        ).astype(jnp.bfloat16)
        at = qdim + head * HDIM
        knew = qkv[:, at : at + HDIM].astype(jnp.bfloat16)
        at = at + kvdim
        vnew = qkv[:, at : at + HDIM].astype(jnp.bfloat16)
        scache = scale * lax.dot_general(
            query, keys[:, lanes], contract, preferred_element_type=jnp.float32
        )
        snew = scale * lax.dot_general(
            query, knew, contract, preferred_element_type=jnp.float32
        )
        scache = jnp.where(cmask, scache, -1e30)
        snew = jnp.where(nmask, snew, -1e30)
        top = jnp.maximum(
            jnp.max(scache, axis=1, keepdims=True), jnp.max(snew, axis=1, keepdims=True)
        )
        ecache = jnp.where(cmask, jnp.exp(scache - top), 0.0)
        enew = jnp.where(nmask, jnp.exp(snew - top), 0.0)
        total = jnp.sum(ecache, axis=1, keepdims=True) + jnp.sum(enew, axis=1, keepdims=True)
        inverse = 1.0 / total
        wcache = (ecache * inverse).astype(jnp.bfloat16)
        wnew = (enew * inverse).astype(jnp.bfloat16)
        mixed = jnp.dot(wcache, values[:, lanes], preferred_element_type=jnp.float32)
        mixed = mixed + jnp.dot(wnew, vnew, preferred_element_type=jnp.float32)
        for g in range(groups):
            attn[:, first + g * HDIM : first + (g + 1) * HDIM] = mixed[
                g * rows : (g + 1) * rows
            ].astype(jnp.bfloat16)

    for k in range(2 * n_y):
        gets[2 + k].wait()
        product = jnp.dot(attn[...], held[k], preferred_element_type=jnp.float32)
        target = theirs if k < n_y else ours
        at = k % n_y * shard
        target[:, at : at + shard] = product.astype(jnp.bfloat16)


def attend(tick, steps, brow, n_y, own, sent, spans, keys, values, wo):
    rows, cdev = own.shape
    _, qdim, width = wo.shape
    length, kvdim = keys.shape[1:]
    kvlocal = kvdim // HDIM
    groups = qdim // kvdim
    shard = width // (2 * n_y)
    vmem = pl.BlockSpec(memory_space=pltpu.VMEM)
    return pl.pallas_call(
        functools.partial(attend_kernel, steps, brow, kvlocal, groups, n_y, tick),
        in_specs=[vmem] * 3
        + [pl.BlockSpec(memory_space=pltpu.HBM)] * 3,
        out_specs=[vmem] * 2,
        scratch_shapes=[
            pltpu.VMEM((rows, qdim), jnp.bfloat16),
            pltpu.VMEM((brow, length, kvdim), jnp.bfloat16),
            pltpu.VMEM((brow, length, kvdim), jnp.bfloat16),
            pltpu.VMEM((2 * n_y, qdim, shard), jnp.bfloat16),
            pltpu.SemaphoreType.DMA((2 * n_y + 2,)),
        ],
        out_shape=[jax.ShapeDtypeStruct((rows, shard * n_y), jnp.bfloat16)] * 2,
        compiler_params=pltpu.CompilerParams(vmem_limit_bytes=VMEM),
        cost_estimate=pl.CostEstimate(
            flops=2 * rows * qdim * width, bytes_accessed=2 * qdim * width, transcendentals=0
        ),
    )(own, sent, spans, keys, values, wo)


def join_kernel(part, moved, mine, out):
    total = part[...].astype(jnp.float32) + moved[...].astype(jnp.float32)
    out[...] = (mine[...].astype(jnp.float32) + total).astype(jnp.bfloat16)


def copy_kernel(value, out):
    out[...] = value[...]


def choose_kernel(tick, far, near, out):
    at_home = phase_at(tick) == lax.axis_index("zone")
    out[...] = jnp.where(at_home, near[...], far[...])


def in_vmem(kernel, *arrays):
    vmem = pl.BlockSpec(memory_space=pltpu.VMEM)
    return pl.pallas_call(
        kernel,
        in_specs=[vmem] * len(arrays),
        out_specs=vmem,
        out_shape=jax.ShapeDtypeStruct(arrays[0].shape, jnp.bfloat16),
        compiler_params=pltpu.CompilerParams(vmem_limit_bytes=VMEM),
    )(*arrays)


def per_device(
    trainer_tiles,
    tile_lengths,
    wo_rollout,
    cache_keys,
    cache_values,
    cache_lengths,
    norm_gain,
    step_inputs,
):
    n_zone = lax.axis_size("zone")
    n_spot = lax.axis_size("spot")
    n_tensor = lax.axis_size("tensor")
    layers = n_zone * n_spot
    tiles = n_spot * n_tensor
    n_y = n_tensor // 2
    slab, columns = trainer_tiles.shape
    cdev = columns // n_tensor
    tilew = slab // layers
    width = wo_rollout.shape[2]
    shard = width // n_tensor
    half = n_y * shard
    steps = step_inputs.shape[0]
    seqs, length = cache_keys.shape[1:3]
    brow = seqs // ITEMS
    rows = steps * brow
    ticks = layers + ITEMS - 1
    zone = lax.axis_index("zone")
    spot = lax.axis_index("spot")
    tpos = lax.axis_index("tensor")
    core = tpos % 2
    layer = zone * n_spot + spot

    all_s, all_t = n_spot - 1, n_tensor - 2
    turns = sorted(range(n_tensor), key=lambda kt: (kt % 2, kt))
    offsets = [(ks, kt) for kt in turns for ks in range(n_spot)]
    place = jnp.stack([spot ^ core * all_s, tpos ^ core * all_t]).astype(jnp.int32)

    def exchange(offset, piece):
        pairs = []
        for s in range(n_spot):
            for t in range(n_tensor):
                bits = 1 if offset == (all_s, all_t) else t % 2
                ks, kt = (0, 0) if offset == (all_s, all_t) else offset
                target = (s ^ ks ^ bits * all_s) * n_tensor + (t ^ kt ^ bits * all_t)
                pairs.append((s * n_tensor + t, target))
        return lax.ppermute(piece, ("spot", "tensor"), pairs)

    pieces = {}
    for kt in turns:
        for ks, piece in enumerate(sort_slab(trainer_tiles, layers, n_tensor, kt, place)):
            pieces[ks, kt] = piece
        place, _ = lax.optimization_barrier((place, piece))
    first, last = pieces[0, 0], pieces[all_s, all_t]
    pieces[0, 0] = jnp.where(core == 0, first, last)
    pieces[all_s, all_t] = jnp.where(core == 0, last, first)
    weights = [
        exchange(offset, pieces[offset]) if offset != (0, 0) else pieces[offset]
        for offset in offsets
    ]

    ends = jnp.cumsum(tile_lengths)
    offset = np.array(offsets, np.int32)
    sender = (offset[:, 1] % 2) ^ core
    fixed = (offset == [0, 0]).all(axis=1) | (offset == [all_s, all_t]).all(axis=1)
    sender = jnp.where(fixed, 0, sender)
    sources = (offset[:, 0] ^ spot ^ sender * all_s) * n_tensor
    sources = sources + (offset[:, 1] ^ tpos ^ sender * all_t) + zone * tiles
    starts = (ends - tile_lengths)[sources]
    counts = tile_lengths[sources]
    table = jnp.concatenate([starts, counts]).astype(jnp.int32)
    flip = [(z, 1 - z) for z in range(2)]
    norm_gain, _ = lax.optimization_barrier((norm_gain, place))
    swapped = lax.ppermute(norm_gain, "zone", flip)
    gains = jnp.concatenate(
        [jnp.where(zone == 0, norm_gain, swapped), jnp.where(zone == 0, swapped, norm_gain)]
    )
    spans = jnp.repeat(cache_lengths, length).reshape(ITEMS, 1, brow * length)
    axes = ("zone", "spot", "tensor")

    def spots(tick):
        return sorted({(tick - i) % n_spot for i in range(ITEMS)})

    def hop(tick, turn):
        pairs = []
        for s in spots(tick):
            for z in range(n_zone):
                ahead = z if s + 1 < n_spot else 1 - z
                pairs.append((z * n_spot + s, (ahead ^ turn) * n_spot + (s + 1) % n_spot))
        return sorted(pairs)

    def mirror(tick):
        return sorted(
            (z * n_spot + s, (1 - z) * n_spot + s) for s in spots(tick) for z in range(n_zone)
        )

    across = [(t, t ^ 1) for t in range(n_tensor)]
    shown = step_inputs.reshape(steps, ITEMS, brow, n_y, 2, shard)
    records = []
    arrived, record = None, []
    for tick in range(ticks):
        if tick < ITEMS:
            fresh = shown[:, tick].reshape(rows, n_y, 2, shard)
            mine = lax.dynamic_index_in_dim(fresh, core, 2, False).reshape(rows, half)
            mine = jnp.where(spot == 0, mine, arrived if tick else 0)
        else:
            mine = arrived
        if tick:
            other = lax.ppermute(mine, "tensor", across)
        else:
            other = lax.dynamic_index_in_dim(fresh, 1 - core, 2, False).reshape(rows, half)
        own = project(tick, tiles, tilew, n_y, table, mine, other, gains, weights)
        sent = lax.ppermute(own, ("zone", "spot"), mirror(tick))
        theirs, ours = attend(
            tick, steps, brow, n_y, own, sent, spans, cache_keys[0], cache_values[0], wo_rollout
        )
        moved = lax.ppermute(theirs, "tensor", across)
        part = (ours.astype(jnp.float32) + moved.astype(jnp.float32)).astype(jnp.bfloat16)
        bit = 2
        while bit < n_tensor:
            moved = lax.ppermute(part, "tensor", [(t, t ^ bit) for t in range(n_tensor)])
            bit = bit * 2
            if bit < n_tensor:
                part = part.astype(jnp.float32) + moved.astype(jnp.float32)
                part = part.astype(jnp.bfloat16)
        after = in_vmem(join_kernel, part, moved, mine)
        record.append(after)
        if tick + 1 < ticks:
            far = lax.ppermute(after, ("zone", "spot"), hop(tick, 1))
            behind = in_vmem(copy_kernel, after)
            near = lax.ppermute(behind, ("zone", "spot"), hop(tick, 0))
            arrived = in_vmem(functools.partial(choose_kernel, tick + 1), far, near)
    for item in range(ITEMS):
        value = jnp.zeros((rows, half), jnp.bfloat16)
        for tick in range(item, ticks):
            value = jnp.where(layer == tick - item, record[tick], value)
        value = lax.dynamic_slice_in_dim(value, tpos // 2 * shard, shard, 1)
        records.append(value.astype(jnp.float32).reshape(steps, brow, shard))
    return jnp.concatenate(records, axis=1)[None]


def solution(mesh):
    n_section, n_tensor = mesh.devices.shape
    fine = Mesh(mesh.devices.reshape(2, n_section // 2, n_tensor), ("zone", "spot", "tensor"))
    section = ("zone", "spot")
    placed = (
        P(("zone", "spot", "tensor"), None),
        P(),
        P(section, "tensor", None),
        P(section, None, None, "tensor"),
        P(section, None, None, "tensor"),
        P(),
        P(section, None),
        P(),
    )
    return jax.shard_map(
        per_device,
        mesh=fine,
        in_specs=placed,
        out_specs=P(section, None, None, "tensor"),
        check_vma=False,
    )
```

```python
import functools

import jax
import jax.numpy as jnp
import numpy as np
from jax import lax
from jax.experimental import pallas as pl
from jax.experimental.pallas import tpu as pltpu
from jax.sharding import Mesh, PartitionSpec as P

HDIM = 128
FB = 8
ITEMS = 4
ROWBLOCK = 256
CHUNK = 384
WINDOW = 512
VMEM = 48 * 1024 * 1024
WHOLE_VMEM = 62 * 1024 * 1024


def sort_kernel(layers, place, slab, *outs):
    feats = ROWBLOCK // layers
    kept = len(outs)
    row = lax.broadcasted_iota(jnp.int32, (ROWBLOCK, ROWBLOCK), 0)
    col = lax.broadcasted_iota(jnp.int32, (ROWBLOCK, ROWBLOCK), 1)
    layer = row // feats % 2 * kept + ((row // (2 * feats)) ^ place[0])
    order = jnp.where(col == row % feats * layers + layer, 1.0, 0.0).astype(jnp.bfloat16)
    for block in range(slab.shape[0] // ROWBLOCK):
        piece = slab[block * ROWBLOCK : (block + 1) * ROWBLOCK]
        moved = jnp.dot(order, piece, preferred_element_type=jnp.float32).astype(jnp.bfloat16)
        for n, out in enumerate(outs):
            for phase in range(2):
                at = (2 * n + phase) * feats
                out[phase, block * feats : (block + 1) * feats] = moved[at : at + feats]


def sort_slab(slab, layers, n_tensor, turn, place):
    rows, columns = slab.shape
    kept = layers // 2
    cdev = columns // n_tensor
    blocks = rows // ROWBLOCK
    taken = next(n for n in (3, 2, 1) if blocks % n == 0) * ROWBLOCK
    feats = taken // layers
    return pl.pallas_call(
        functools.partial(sort_kernel, layers),
        grid_spec=pltpu.PrefetchScalarGridSpec(
            num_scalar_prefetch=1,
            grid=(rows // taken,),
            in_specs=[pl.BlockSpec((taken, cdev), lambda i, s: (i, s[1] ^ turn))],
            out_specs=[pl.BlockSpec((2, feats, cdev), lambda i, s: (0, i, 0))] * kept,
        ),
        out_shape=[jax.ShapeDtypeStruct((2, rows // layers, cdev), jnp.bfloat16)] * kept,
        compiler_params=pltpu.CompilerParams(vmem_limit_bytes=WHOLE_VMEM),
        cost_estimate=pl.CostEstimate(
            flops=2 * rows * cdev * ROWBLOCK, bytes_accessed=4 * rows * cdev, transcendentals=0
        ),
    )(place, slab)


def core_here():
    return lax.axis_index("tensor") % 2


def phase_at(tick):
    n_spot = lax.axis_size("spot")
    return (tick >= lax.axis_index("spot") + n_spot).astype(jnp.int32)


def item_at(tick):
    layer = lax.axis_index("zone") * lax.axis_size("spot") + lax.axis_index("spot")
    return jnp.clip(tick - layer, 0, ITEMS - 1)


def project_kernel(tick, tiles, tilew, n_y, table, mine, other, gains, *rest):
    weights, (out, normed, held, scalars, sems) = rest[:-5], rest[-5:]
    rows, half = mine.shape
    width = 2 * half
    shard = half // n_y
    chunks, size, cdev = held.shape
    per = size // tilew
    core, phase = core_here(), phase_at(tick)
    lookup = pltpu.make_async_copy(table, scalars, sems.at[tiles])

    def fetch(n):
        target = held.at[n // per, pl.ds(n % per * tilew, tilew)]
        return pltpu.make_async_copy(weights[n].at[phase], target, sems.at[n])

    for n in range(tiles):
        fetch(n).start()
        if n == 0:
            lookup.start()

    here = mine[...].astype(jnp.float32)
    there = other[...].astype(jnp.float32)
    total = jnp.sum(here * here, axis=1, keepdims=True)
    total = total + jnp.sum(there * there, axis=1, keepdims=True)
    inverse = lax.rsqrt(total / width + 1e-06)
    gain = jnp.where(phase == 0, gains[0:1], gains[1:2])
    low = jnp.where(core == 0, here, there) * inverse
    high = jnp.where(core == 0, there, here) * inverse
    for y in range(n_y):
        at = 2 * y * shard
        piece = slice(y * shard, (y + 1) * shard)
        normed[:, at : at + shard] = low[:, piece] * gain[:, at : at + shard]
        at = at + shard
        normed[:, at : at + shard] = high[:, piece] * gain[:, at : at + shard]
    normed[:, width:] = jnp.zeros((rows, WINDOW), jnp.float32)

    along = CHUNK // tilew
    lookup.wait()
    lane = lax.broadcasted_iota(jnp.int32, (rows, CHUNK), 1)

    def spread(j):
        value = jnp.zeros((rows, CHUNK), jnp.float32)
        for a in range(along):
            start = scalars[j * along + a] * FB
            count = scalars[tiles + j * along + a] * FB
            aligned = start // 128 * 128
            window = normed[:, pl.ds(pl.multiple_of(aligned, 128), WINDOW)]
            put = a * tilew
            shift = (put - (start - aligned) + WINDOW) % WINDOW
            rolled = pltpu.roll(window, shift, 1)[:, :CHUNK]
            value = jnp.where((lane >= put) & (lane < put + count), rolled, value)
        return value.astype(jnp.bfloat16)

    acc = jnp.zeros((rows, cdev), jnp.float32)
    for j in range(chunks):
        parts = [spread(j * (size // CHUNK) + i) for i in range(size // CHUNK)]
        for n in range(j * per, (j + 1) * per):
            fetch(n).wait()
        acc = acc + jnp.dot(
            jnp.concatenate(parts, axis=1), held[j], preferred_element_type=jnp.float32
        )
    out[...] = acc.astype(jnp.bfloat16)


def project(tick, tiles, tilew, n_y, table, mine, other, gains, weights):
    rows, half = mine.shape
    cdev = weights[0].shape[2]
    depth = tiles * tilew
    size = 2 * CHUNK
    vmem = pl.BlockSpec(memory_space=pltpu.VMEM)
    return pl.pallas_call(
        functools.partial(project_kernel, tick, tiles, tilew, n_y),
        in_specs=[pl.BlockSpec(memory_space=pltpu.HBM)]
        + [vmem] * 3
        + [pl.BlockSpec(memory_space=pltpu.HBM)] * len(weights),
        out_specs=vmem,
        scratch_shapes=[
            pltpu.VMEM((rows, 2 * half + WINDOW), jnp.float32),
            pltpu.VMEM((depth // size, size, cdev), jnp.bfloat16),
            pltpu.SMEM(table.shape, jnp.int32),
            pltpu.SemaphoreType.DMA((tiles + 1,)),
        ],
        out_shape=jax.ShapeDtypeStruct((rows, cdev), jnp.bfloat16),
        compiler_params=pltpu.CompilerParams(vmem_limit_bytes=VMEM if tick else WHOLE_VMEM),
        cost_estimate=pl.CostEstimate(
            flops=2 * rows * depth * cdev, bytes_accessed=2 * depth * cdev, transcendentals=0
        ),
    )(table, mine, other, gains, *weights)


def attend_kernel(steps, brow, kvlocal, groups, n_y, tick, own, sent, spans, ckeys, cvals, wo, theirs, ours, attn, kheld, vheld, held, sems):
    rows = steps * brow
    length = ckeys.shape[1]
    scale = 1.0 / HDIM**0.5
    qdim = kvlocal * groups * HDIM
    kvdim = kvlocal * HDIM
    shard = held.shape[2]
    core = core_here()
    item = item_at(tick)
    first = pl.multiple_of(item * brow, brow)
    gets = [
        pltpu.make_async_copy(ckeys.at[pl.ds(first, brow)], kheld, sems.at[2 * n_y]),
        pltpu.make_async_copy(cvals.at[pl.ds(first, brow)], vheld, sems.at[2 * n_y + 1]),
    ]
    for k in range(2 * n_y):
        side = 1 - core if k < n_y else core
        at = pl.multiple_of((k % n_y * 2 + side) * shard, shard)
        gets.append(
            pltpu.make_async_copy(wo.at[0, :, pl.ds(at, shard)], held.at[k], sems.at[k])
        )
    for get in gets:
        get.start()
    gets[0].wait()
    gets[1].wait()
    span = spans[item]

    qkv = (own[...].astype(jnp.float32) + sent[...].astype(jnp.float32)).astype(jnp.bfloat16)
    qkv = qkv.astype(jnp.float32)
    keys = kheld[...].reshape(brow * length, kvdim)
    values = vheld[...].reshape(brow * length, kvdim)
    tall = groups * rows
    at = lax.broadcasted_iota(jnp.int32, (tall, brow * length), 0)
    col = lax.broadcasted_iota(jnp.int32, (tall, brow * length), 1)
    cmask = (at % brow == col // length) & (col % length < span)
    at = lax.broadcasted_iota(jnp.int32, (tall, rows), 0)
    col = lax.broadcasted_iota(jnp.int32, (tall, rows), 1)
    nmask = (at % brow == col % brow) & (col // brow <= at % rows // brow)
    contract = (((1,), (1,)), ((), ()))
    for head in range(kvlocal):
        lanes = slice(head * HDIM, (head + 1) * HDIM)
        first = head * groups * HDIM
        query = jnp.concatenate(
            [qkv[:, first + g * HDIM : first + (g + 1) * HDIM] for g in range(groups)], axis=0
        ).astype(jnp.bfloat16)
        at = qdim + head * HDIM
        knew = qkv[:, at : at + HDIM].astype(jnp.bfloat16)
        at = at + kvdim
        vnew = qkv[:, at : at + HDIM].astype(jnp.bfloat16)
        scache = scale * lax.dot_general(
            query, keys[:, lanes], contract, preferred_element_type=jnp.float32
        )
        snew = scale * lax.dot_general(
            query, knew, contract, preferred_element_type=jnp.float32
        )
        scache = jnp.where(cmask, scache, -1e30)
        snew = jnp.where(nmask, snew, -1e30)
        top = jnp.maximum(
            jnp.max(scache, axis=1, keepdims=True), jnp.max(snew, axis=1, keepdims=True)
        )
        ecache = jnp.where(cmask, jnp.exp(scache - top), 0.0)
        enew = jnp.where(nmask, jnp.exp(snew - top), 0.0)
        total = jnp.sum(ecache, axis=1, keepdims=True) + jnp.sum(enew, axis=1, keepdims=True)
        inverse = 1.0 / total
        wcache = (ecache * inverse).astype(jnp.bfloat16)
        wnew = (enew * inverse).astype(jnp.bfloat16)
        mixed = jnp.dot(wcache, values[:, lanes], preferred_element_type=jnp.float32)
        mixed = mixed + jnp.dot(wnew, vnew, preferred_element_type=jnp.float32)
        for g in range(groups):
            attn[:, first + g * HDIM : first + (g + 1) * HDIM] = mixed[
                g * rows : (g + 1) * rows
            ].astype(jnp.bfloat16)

    for k in range(2 * n_y):
        gets[2 + k].wait()
        product = jnp.dot(attn[...], held[k], preferred_element_type=jnp.float32)
        target = theirs if k < n_y else ours
        at = k % n_y * shard
        target[:, at : at + shard] = product.astype(jnp.bfloat16)


def attend(tick, steps, brow, n_y, own, sent, spans, keys, values, wo):
    rows, cdev = own.shape
    _, qdim, width = wo.shape
    length, kvdim = keys.shape[1:]
    kvlocal = kvdim // HDIM
    groups = qdim // kvdim
    shard = width // (2 * n_y)
    vmem = pl.BlockSpec(memory_space=pltpu.VMEM)
    return pl.pallas_call(
        functools.partial(attend_kernel, steps, brow, kvlocal, groups, n_y, tick),
        in_specs=[vmem] * 3
        + [pl.BlockSpec(memory_space=pltpu.HBM)] * 3,
        out_specs=[vmem] * 2,
        scratch_shapes=[
            pltpu.VMEM((rows, qdim), jnp.bfloat16),
            pltpu.VMEM((brow, length, kvdim), jnp.bfloat16),
            pltpu.VMEM((brow, length, kvdim), jnp.bfloat16),
            pltpu.VMEM((2 * n_y, qdim, shard), jnp.bfloat16),
            pltpu.SemaphoreType.DMA((2 * n_y + 2,)),
        ],
        out_shape=[jax.ShapeDtypeStruct((rows, shard * n_y), jnp.bfloat16)] * 2,
        compiler_params=pltpu.CompilerParams(vmem_limit_bytes=VMEM),
        cost_estimate=pl.CostEstimate(
            flops=2 * rows * qdim * width, bytes_accessed=2 * qdim * width, transcendentals=0
        ),
    )(own, sent, spans, keys, values, wo)


def join_kernel(part, moved, mine, out):
    total = part[...].astype(jnp.float32) + moved[...].astype(jnp.float32)
    out[...] = (mine[...].astype(jnp.float32) + total).astype(jnp.bfloat16)


def copy_kernel(value, out):
    out[...] = value[...]


def choose_kernel(tick, far, near, out):
    at_home = phase_at(tick) == lax.axis_index("zone")
    out[...] = jnp.where(at_home, near[...], far[...])


def late_kernel(value, piece, out):
    out[...] = value[...]


def after_piece(value, piece):
    vmem = pl.BlockSpec(memory_space=pltpu.VMEM)
    return pl.pallas_call(
        late_kernel,
        in_specs=[vmem, pl.BlockSpec(memory_space=pltpu.HBM)],
        out_specs=vmem,
        out_shape=jax.ShapeDtypeStruct(value.shape, value.dtype),
        compiler_params=pltpu.CompilerParams(vmem_limit_bytes=VMEM),
    )(value, piece)


def in_vmem(kernel, *arrays):
    vmem = pl.BlockSpec(memory_space=pltpu.VMEM)
    return pl.pallas_call(
        kernel,
        in_specs=[vmem] * len(arrays),
        out_specs=vmem,
        out_shape=jax.ShapeDtypeStruct(arrays[0].shape, jnp.bfloat16),
        compiler_params=pltpu.CompilerParams(vmem_limit_bytes=VMEM),
    )(*arrays)


def per_device(
    trainer_tiles,
    tile_lengths,
    wo_rollout,
    cache_keys,
    cache_values,
    cache_lengths,
    norm_gain,
    step_inputs,
):
    n_zone = lax.axis_size("zone")
    n_spot = lax.axis_size("spot")
    n_tensor = lax.axis_size("tensor")
    layers = n_zone * n_spot
    tiles = n_spot * n_tensor
    n_y = n_tensor // 2
    slab, columns = trainer_tiles.shape
    cdev = columns // n_tensor
    tilew = slab // layers
    width = wo_rollout.shape[2]
    shard = width // n_tensor
    half = n_y * shard
    steps = step_inputs.shape[0]
    seqs, length = cache_keys.shape[1:3]
    brow = seqs // ITEMS
    rows = steps * brow
    ticks = layers + ITEMS - 1
    zone = lax.axis_index("zone")
    spot = lax.axis_index("spot")
    tpos = lax.axis_index("tensor")
    core = tpos % 2
    layer = zone * n_spot + spot

    all_s, all_t = n_spot - 1, n_tensor - 2
    turns = sorted(range(n_tensor), key=lambda kt: (kt % 2, kt))
    offsets = [(ks, kt) for kt in turns for ks in range(n_spot)]
    place = jnp.stack([spot ^ core * all_s, tpos ^ core * all_t]).astype(jnp.int32)

    def exchange(offset, piece):
        pairs = []
        for s in range(n_spot):
            for t in range(n_tensor):
                bits = 1 if offset == (all_s, all_t) else t % 2
                ks, kt = (0, 0) if offset == (all_s, all_t) else offset
                target = (s ^ ks ^ bits * all_s) * n_tensor + (t ^ kt ^ bits * all_t)
                pairs.append((s * n_tensor + t, target))
        return lax.ppermute(piece, ("spot", "tensor"), pairs)

    pieces = {}
    for kt in turns:
        for ks, piece in enumerate(sort_slab(trainer_tiles, layers, n_tensor, kt, place)):
            pieces[ks, kt] = piece
        place, _ = lax.optimization_barrier((place, piece))
    first, last = pieces[0, 0], pieces[all_s, all_t]
    pieces[0, 0] = jnp.where(core == 0, first, last)
    pieces[all_s, all_t] = jnp.where(core == 0, last, first)
    weights = [
        exchange(offset, pieces[offset]) if offset != (0, 0) else pieces[offset]
        for offset in offsets
    ]

    ends = jnp.cumsum(tile_lengths)
    offset = np.array(offsets, np.int32)
    sender = (offset[:, 1] % 2) ^ core
    fixed = (offset == [0, 0]).all(axis=1) | (offset == [all_s, all_t]).all(axis=1)
    sender = jnp.where(fixed, 0, sender)
    sources = (offset[:, 0] ^ spot ^ sender * all_s) * n_tensor
    sources = sources + (offset[:, 1] ^ tpos ^ sender * all_t) + zone * tiles
    starts = (ends - tile_lengths)[sources]
    counts = tile_lengths[sources]
    table = jnp.concatenate([starts, counts]).astype(jnp.int32)
    flip = [(z, 1 - z) for z in range(2)]
    swapped = lax.ppermute(after_piece(norm_gain, piece), "zone", flip)
    gains = jnp.concatenate(
        [jnp.where(zone == 0, norm_gain, swapped), jnp.where(zone == 0, swapped, norm_gain)]
    )
    spans = jnp.repeat(cache_lengths, length).reshape(ITEMS, 1, brow * length)
    axes = ("zone", "spot", "tensor")

    def spots(tick):
        return sorted({(tick - i) % n_spot for i in range(ITEMS)})

    def hop(tick, turn):
        pairs = []
        for s in spots(tick):
            for z in range(n_zone):
                ahead = z if s + 1 < n_spot else 1 - z
                pairs.append((z * n_spot + s, (ahead ^ turn) * n_spot + (s + 1) % n_spot))
        return sorted(pairs)

    def mirror(tick):
        return sorted(
            (z * n_spot + s, (1 - z) * n_spot + s) for s in spots(tick) for z in range(n_zone)
        )

    across = [(t, t ^ 1) for t in range(n_tensor)]
    shown = step_inputs.reshape(steps, ITEMS, brow, n_y, 2, shard)
    records = []
    arrived, record = None, []
    for tick in range(ticks):
        if tick < ITEMS:
            fresh = shown[:, tick].reshape(rows, n_y, 2, shard)
            mine = lax.dynamic_index_in_dim(fresh, core, 2, False).reshape(rows, half)
            mine = jnp.where(spot == 0, mine, arrived if tick else 0)
        else:
            mine = arrived
        if tick:
            other = lax.ppermute(mine, "tensor", across)
        else:
            other = lax.dynamic_index_in_dim(fresh, 1 - core, 2, False).reshape(rows, half)
        own = project(tick, tiles, tilew, n_y, table, mine, other, gains, weights)
        sent = lax.ppermute(own, ("zone", "spot"), mirror(tick))
        theirs, ours = attend(
            tick, steps, brow, n_y, own, sent, spans, cache_keys[0], cache_values[0], wo_rollout
        )
        moved = lax.ppermute(theirs, "tensor", across)
        part = (ours.astype(jnp.float32) + moved.astype(jnp.float32)).astype(jnp.bfloat16)
        bit = 2
        while bit < n_tensor:
            moved = lax.ppermute(part, "tensor", [(t, t ^ bit) for t in range(n_tensor)])
            bit = bit * 2
            if bit < n_tensor:
                part = part.astype(jnp.float32) + moved.astype(jnp.float32)
                part = part.astype(jnp.bfloat16)
        after = in_vmem(join_kernel, part, moved, mine)
        record.append(after)
        if tick + 1 < ticks:
            far = lax.ppermute(after, ("zone", "spot"), hop(tick, 1))
            behind = in_vmem(copy_kernel, after)
            near = lax.ppermute(behind, ("zone", "spot"), hop(tick, 0))
            arrived = in_vmem(functools.partial(choose_kernel, tick + 1), far, near)
    for item in range(ITEMS):
        value = jnp.zeros((rows, half), jnp.bfloat16)
        for tick in range(item, ticks):
            value = jnp.where(layer == tick - item, record[tick], value)
        value = lax.dynamic_slice_in_dim(value, tpos // 2 * shard, shard, 1)
        records.append(value.astype(jnp.float32).reshape(steps, brow, shard))
    return jnp.concatenate(records, axis=1)[None]


def solution(mesh):
    n_section, n_tensor = mesh.devices.shape
    fine = Mesh(mesh.devices.reshape(2, n_section // 2, n_tensor), ("zone", "spot", "tensor"))
    section = ("zone", "spot")
    placed = (
        P(("zone", "spot", "tensor"), None),
        P(),
        P(section, "tensor", None),
        P(section, None, None, "tensor"),
        P(section, None, None, "tensor"),
        P(),
        P(section, None),
        P(),
    )
    return jax.shard_map(
        per_device,
        mesh=fine,
        in_specs=placed,
        out_specs=P(section, None, None, "tensor"),
        check_vma=False,
    )
```
